256 devices in a mesh: gz: 8 (over y, core), gx: 8 (over x, z_lo), gy: 4 (over z_hi).
Axes of the slice: x: 4, y: 4, z: 8 (z_hi: 4, z_lo: 2; z = z_hi * 2 + z_lo), core: 2. Of those that a mesh axis runs over, the one named last changes fastest.
Arguments:
- initial_field: float32 [16, 1024, 512], P('gz', 'gx', 'gy'), may hold values from -6 to 6
- source_term: float32 [16, 1024, 512], P('gz', 'gx', 'gy'), may hold values from -48 to 48
- block_inverse: float32 [1024, 512, 128], P('gx', 'gy'), may hold values from -0.1 to 0.1
Outputs:
- smoothed: float32 [16, 1024, 512], P('gz', 'gx', 'gy')
The draws below stay inside these ranges and needn't reach their ends.
All inputs are finite; a program needn't handle non-finite values.
Results may differ from the reference program's by a relative error of at most 0.00013.
Values sent between devices are 32-bit elements; how exact they have to be, the bound alone decides.
A program may use at most 64 MiB of HBM per device.

```python
import math
import jax
import jax.numpy as jnp
from jax import lax

LINE = 128
NZ = 16
NX = 1024
NY = 512


def smooth_wave(key, grid_shape, first_axis, first_count, second_axis, second_count):
    phases = jax.random.uniform(key, (2,), jnp.float32, -math.pi, math.pi)
    first_pos = lax.broadcasted_iota(jnp.float32, grid_shape, first_axis) * (2.0 * math.pi / first_count)
    second_pos = lax.broadcasted_iota(jnp.float32, grid_shape, second_axis) * (2.0 * math.pi / second_count)
    return jnp.cos(first_pos + phases[0]) * jnp.cos(second_pos + phases[1])


def draw_initial_field(key, part):
    wave_key, noise_key = jax.random.split(jax.random.fold_in(key, 21))
    grid_shape = (NZ, NX, NY)
    wave_part = smooth_wave(wave_key, grid_shape, 1, NX, 0, NZ)
    smooth_part = -2.0 * (1.0 + 0.4 * wave_part)
    noise_part = jnp.clip(jax.random.normal(noise_key, grid_shape, jnp.float32), -3.0, 3.0)
    return (smooth_part + noise_part).astype(jnp.float32)


def draw_source_term(key, part):
    wave_key, noise_key = jax.random.split(jax.random.fold_in(key, 31))
    grid_shape = (NZ, NX, NY)
    wave_part = smooth_wave(wave_key, grid_shape, 1, NX, 2, NY)
    smooth_part = 10.0 * (1.0 + 0.5 * wave_part)
    noise_part = jnp.clip(8.0 * jax.random.normal(noise_key, grid_shape, jnp.float32), -30.0, 30.0)
    return (smooth_part + noise_part).astype(jnp.float32)


def draw_block_inverse(key, part):
    first_key, second_key = jax.random.split(jax.random.fold_in(key, 11))
    row_index = lax.broadcasted_iota(jnp.int32, (NX, NY, LINE), 1) % LINE
    col_index = lax.broadcasted_iota(jnp.int32, (NX, NY, LINE), 2)
    strength = jnp.exp(jax.random.uniform(first_key, (NX, NY, 1), jnp.float32, math.log(1.2), math.log(1.9)))
    spread = jnp.clip(jax.random.normal(second_key, (NX, NY, LINE), jnp.float32), -5.0, 5.0)
    diagonal_part = jnp.where(row_index == col_index, strength, 0.0)
    off_part = spread * (0.4 / math.sqrt(LINE))
    return ((diagonal_part + off_part) / 26.0).astype(jnp.float32)


def setup_inputs(seed: int = 0) -> dict:
    arg_keys = jax.random.split(jax.random.key(seed), 4)
    return {
        "initial_field": draw_initial_field(jax.random.fold_in(arg_keys[3], 71), 0),
        "source_term": draw_source_term(jax.random.fold_in(arg_keys[3], 71), 0),
        "block_inverse": draw_block_inverse(jax.random.fold_in(arg_keys[3], 71), 0),
    }


exact_mode = lax.Precision.HIGHEST


def box_sum(plane):
    padded = jnp.pad(plane, 1)
    row_sums = padded[:-2] + padded[1:-1] + padded[2:]
    return row_sums[:, :-2] + row_sums[:, 1:-1] + row_sums[:, 2:]


def apply_blocks(block_inverse, residual):
    count_x, count_y = residual.shape
    width = block_inverse.shape[2]
    lines = residual.reshape(count_x, count_y // width, width)
    blocks = block_inverse.reshape(count_x, count_y // width, width, width)
    return jnp.einsum("xqij,xqj->xqi", blocks, lines, precision=exact_mode).reshape(count_x, count_y)


def sweep_planes(field_now, source_term, block_inverse, backward):
    padded = jnp.pad(field_now, ((1, 1), (0, 0), (0, 0)))

    def update_plane(step, padded):
        if backward:
            zindex = (NZ - 1 - step).astype(jnp.int32)
        else:
            zindex = jnp.asarray(step).astype(jnp.int32)
        triple = lax.dynamic_slice_in_dim(padded, zindex, 3, 0)
        neighbours = box_sum(triple[0]) + box_sum(triple[1]) + box_sum(triple[2])
        source_plane = lax.dynamic_index_in_dim(source_term, zindex, 0, keepdims=False)
        residual = source_plane - (27.0 * triple[1] - neighbours)
        fresh = triple[1] + apply_blocks(block_inverse, residual)
        return lax.dynamic_update_slice_in_dim(padded, fresh[None], zindex + 1, 0)

    padded = lax.fori_loop(0, NZ, update_plane, padded)
    return padded[1:-1]


def reference(initial_field, source_term, block_inverse):
    forward = sweep_planes(initial_field, source_term, block_inverse, False)
    return sweep_planes(forward, source_term, block_inverse, True)
```

```python
import functools

import jax
import jax.numpy as jnp
from jax import lax
from jax.experimental import pallas as pl
from jax.experimental.pallas import tpu as pltpu
from jax.sharding import PartitionSpec as P

MESH = pl.DeviceIdType.MESH
F32 = jnp.float32
OWN = 16
HALO = 8
SPAN = 32
STEPS = 4
NZ = 16
SHIFTS = range(-3, 4)


def roll(value, shift, axis=1):
    size = value.shape[axis]
    shift = shift % size
    return value if shift == 0 else pltpu.roll(value, shift, axis)


def kernel(
    n, gx, gy, depth,
    v_in, s_in, b_in, out,
    v_rows, s_rows, b_rows, blocks, old, src, fresh, halo, base,
    e_tmp, e_send, e_recv, t_send, t_recv, e_old, coef, given, rows2, imp, resp, out_rows,
    field_send, field_recv, b_recv, b_send, e_ssem, e_rsem, t_ssem, t_rsem, u_ssem, u_rsem, o_ssem, o_rsem,
):
    g, a, q = lax.axis_index("gz"), lax.axis_index("gx"), lax.axis_index("gy")
    par = lax.rem(a, 2)
    local = OWN * n

    def flip(p):
        return p + par * (n - 1 - 2 * p)

    p = flip(g)
    a_left, a_right = lax.rem(a + gx - 1, gx), lax.rem(a + 1, gx)
    step_up = 1 - 2 * par
    first, last = p == 0, p == n - 1
    left = (jnp.where(first, g, g - step_up), jnp.where(first, a_left, a))
    right = (jnp.where(last, g, g + step_up), jnp.where(last, a_right, a))
    places = (left, (g, a), right)

    def remote(source, target, send, recv, device):
        return pltpu.make_async_remote_copy(
            src_ref=source, dst_ref=target, send_sem=send, recv_sem=recv, device_id=device, device_id_type=MESH
        )

    def b_local(source_line, row, count, sem):
        return pltpu.make_async_copy(
            b_in.at[pl.ds(pl.multiple_of(source_line * 128, 128), count * 128)],
            b_rows.at[pl.ds(row * 128, count * 128)], sem,
        )

    b_local(OWN * p, HALO, OWN, b_recv.at[0]).start()

    @pl.when(p > 0)
    def _():
        b_local(OWN * p - HALO, 0, HALO, b_recv.at[1]).start()

    @pl.when(p < n - 1)
    def _():
        b_local(OWN * p + OWN, HALO + OWN, HALO, b_recv.at[2]).start()

    barrier = pltpu.get_barrier_semaphore()

    def greet(i, carry):
        g2, a2 = lax.rem(i, n), lax.rem(a + gx - 1 + i // n, gx)

        @pl.when(jnp.logical_or(g2 != g, a2 != a))
        def _():
            pl.semaphore_signal(barrier, inc=1, device_id=(g2, a2, q), device_id_type=MESH)

        return carry

    lax.fori_loop(0, 3 * n, greet, 0)
    for place in places:
        for k in range(1, gy):
            pl.semaphore_signal(
                barrier, inc=1, device_id=(place[0], place[1], lax.rem(q + k, gy)), device_id_type=MESH
            )
    pl.semaphore_wait(barrier, 3 * n - 1 + 3 * (gy - 1))

    fields = ((v_in, v_rows), (s_in, s_rows))
    planes = pl.ds(depth * g, depth)

    def field_copies(start):
        for other in range(n):
            lo, hi = max(0, OWN * other - HALO), min(local, OWN * other + OWN + HALO)
            row = lo - (OWN * other - HALO)
            target = flip(other)
            for f, (source, place) in enumerate(fields):
                args = (source.at[:, pl.ds(lo, hi - lo), :], place.at[planes, pl.ds(row, hi - lo), :])

                @pl.when(target != g)
                def _():
                    copy = remote(*args, field_send.at[f, other], field_recv.at[f], (target, a, q))
                    if start:
                        copy.start()
                    else:
                        copy.wait_send()

                if start:
                    @pl.when(target == g)
                    def _():
                        pltpu.make_async_copy(*args, field_recv.at[f]).start()

        for f, (source, place) in enumerate(fields):
            ends = (
                (local - HALO, 0, (flip(n - 1), a_right, q), n),
                (0, HALO + OWN, (flip(0), a_left, q), n + 1),
            )
            for line, row, device, sem in ends:
                copy = remote(
                    source.at[:, pl.ds(line, HALO), :], place.at[planes, pl.ds(row, HALO), :],
                    field_send.at[f, sem], field_recv.at[f], device,
                )
                if start:
                    copy.start()
                else:
                    copy.wait_send()

    field_copies(True)

    def b_remote(start):
        for cond, line, row, device, recv, send in (
            (last, local - HALO, 0, right, 1, 0), (first, 0, HALO + OWN, left, 2, 1),
        ):
            @pl.when(cond)
            def _():
                copy = remote(
                    b_in.at[pl.ds(line * 128, HALO * 128)], b_rows.at[pl.ds(row * 128, HALO * 128)],
                    b_send.at[send], b_recv.at[recv], (device[0], device[1], q),
                )
                if start:
                    copy.start()
                else:
                    copy.wait_send()

    b_remote(True)

    lane = lax.broadcasted_iota(jnp.int32, (SPAN, 128), 1)
    row = lax.broadcasted_iota(jnp.int32, (SPAN, 128), 0)
    group, xlane = lane // SPAN, lane % SPAN
    line = local * a + OWN * p - HALO + xlane
    inside = jnp.logical_and(line >= 0, line < local * gx)
    low_half, even = group < 2, group % 2 == 0
    top_cell, bottom_cell = jnp.logical_and(row == 0, group == 0), jnp.logical_and(row == SPAN - 1, group == 3)
    inside1, group1, xlane1 = inside[:1], group[:1], xlane[:1]
    group8, xlane8 = group[:8], xlane[:8]
    mine8 = jnp.logical_and(group8 == q, jnp.logical_and(xlane8 >= HALO, xlane8 < HALO + OWN))
    mine1 = mine8[:1]

    def y_sum(cells):
        up = jnp.where(group1 == 0, 0.0, roll(cells[SPAN - 1 :], SPAN))
        down = jnp.where(group1 == 3, 0.0, roll(cells[:1], -SPAN))
        return cells + jnp.where(row == 0, up, roll(cells, 1, 0)) + jnp.where(row == SPAN - 1, down, roll(cells, -1, 0))

    def box(cells):
        return y_sum(cells + roll(cells, 1) + roll(cells, -1))

    def apply(residual):
        acc = blocks[0] * residual[:1]
        for j in range(1, SPAN):
            acc = acc + blocks[j] * residual[j : j + 1]
        a0, a1, a2, a3 = (acc[SPAN * i : SPAN * (i + 1)] for i in range(4))
        b0 = jnp.where(low_half, a0, a2) + roll(jnp.where(low_half, a2, a0), 64)
        b1 = jnp.where(low_half, a1, a3) + roll(jnp.where(low_half, a3, a1), 64)
        other = jnp.where(even, b1, b0)
        return jnp.where(even, b0 + roll(other, -SPAN), b1 + roll(other, SPAN))

    b_local(0, HALO, OWN, b_recv.at[0]).wait()
    b_local(0, 0, HALO, b_recv.at[1]).wait()
    b_local(0, HALO + OWN, HALO, b_recv.at[2]).wait()

    def turn(x, carry):
        rows = pl.ds(pl.multiple_of(x * 128, 128), 128)
        b_rows[rows, :] = b_rows[rows, :].T
        return carry

    lax.fori_loop(0, SPAN, turn, 0)

    def gather(j, carry):
        parts = [b_rows[pl.ds(SPAN * jg + j, SPAN, stride=128), :] for jg in range(4)]
        blocks[j] = jnp.concatenate(parts, axis=0).T
        return carry

    lax.fori_loop(0, SPAN, gather, 0)

    cells = []
    for slot, at in ((0, 0), (SPAN - 1, 3)):
        column = jnp.zeros((SPAN, 128), F32)
        for i in range(4):
            column = jnp.where(group == i, roll(blocks[slot, SPAN * i : SPAN * (i + 1), :], SPAN * (i - at)), column)
        cells.append(y_sum(jnp.where(inside, column, 0.0)))
    for j in range(SPAN):
        rows2[0, j : j + 1, :] = blocks[j, :1, :]
        rows2[1, j : j + 1, :] = blocks[j, 127:, :]
    for e in range(2):
        for d in range(3):
            imp[3 * e + d] = roll(cells[e], -(d - 1))

    def respond(i, carry):
        resp[i] = y_sum(jnp.where(inside, apply(imp[i]), 0.0))
        return carry

    lax.fori_loop(0, 6, respond, 0)

    def keep(index, value):
        total = value + roll(value, 32)
        total = total + roll(total, 64)
        t_send[index : index + 1, :] = jnp.where(mine1, total, 0.0)

    def dot(e, value):
        return jnp.sum(rows2[e] * value, axis=0, keepdims=True)

    t_send[32:40, :] = jnp.zeros((8, 128), F32)
    for e in range(2):
        keep(2 * e, jnp.where(group1 == 0, rows2[e, :1, :], 0.0))
        keep(2 * e + 1, jnp.where(group1 == 3, rows2[e, SPAN - 1 :, :], 0.0))
        for f in range(2):
            for d in range(-1, 2):
                keep(4 + (2 * e + f) * 3 + d + 1, dot(e, roll(cells[f], -d)))
            for d in range(-2, 3):
                total = None
                for near in range(-1, 2):
                    far = d - near
                    if abs(far) <= 1:
                        term = roll(resp[3 * f + far + 1], -near)
                        total = term if total is None else total + term
                keep(16 + (2 * e + f) * 5 + d + 2, dot(e, total))

    whole = v_rows
    for f, (place, rows_ref) in enumerate(((old, v_rows), (src, s_rows))):
        pltpu.make_async_copy(rows_ref, rows_ref, field_recv.at[f]).wait()
        for w in range(NZ // 4):
            turned = rows_ref[4 * w : 4 * w + 4].reshape(128, 128).T
            for k in range(4):
                tile = jnp.zeros((SPAN, 128), F32)
                for i in range(4):
                    tile = jnp.where(group == i, roll(turned[SPAN * i : SPAN * (i + 1)], SPAN * (i - k)), tile)
                place[4 * w + k] = jnp.where(inside, tile, 0.0)
    zero_tile = jnp.zeros((SPAN, 128), F32)
    old[NZ] = zero_tile
    old[2 * NZ + 1] = zero_tile
    e_old[NZ] = jnp.zeros((8, 128), F32)
    e_old[2 * NZ + 1] = jnp.zeros((8, 128), F32)

    def own_edges(value, e):
        shift = SPAN * q if e == 0 else SPAN * (q + 1)
        return jnp.where(mine8, pltpu.roll(value, lax.rem(shift, 128), 1), 0.0)

    for z in range(NZ):
        e_tmp[z : z + 1, :] = old[z, :1, :]
        e_tmp[NZ + z : NZ + z + 1, :] = old[z, SPAN - 1 :, :]
    for k in range(4):
        t_send[40 + 8 * k : 48 + 8 * k, :] = own_edges(e_tmp[8 * k : 8 * k + 8, :], k // 2)

    def edge_copies(source, target, send, recv, start):
        for x, place in enumerate(places):
            for k in range(gy):
                if x == 1 and k == 0:
                    if start:
                        pltpu.make_async_copy(source, target.at[1, q], recv).start()
                    continue
                copy = remote(
                    source, target.at[2 - x, q], send.at[3 * k + x], recv, (place[0], place[1], lax.rem(q + k, gy))
                )
                if start:
                    copy.start()
                else:
                    copy.wait_send()

    edge_copies(t_send, t_recv, t_ssem, t_rsem, True)

    def gathered(ref, rows):
        sides = []
        for x in range(3):
            total = ref[x, 0, rows, :]
            for k in range(1, gy):
                total = total + ref[x, k, rows, :]
            sides.append(total)
        return jnp.where(
            xlane8 < HALO, roll(sides[0], -OWN), jnp.where(xlane8 >= HALO + OWN, roll(sides[2], OWN), sides[1])
        )

    def halo_copy(window, side, start):
        device = places[2 * side]
        device = (device[0], device[1], q)
        at = STEPS * window

        @pl.when(window < 4)
        def _():
            copy = remote(
                fresh.at[pl.ds(at, STEPS)], halo.at[window, 1 - side],
                u_ssem.at[window, side], u_rsem.at[window, 1 - side], device,
            )
            if start:
                copy.start()
            else:
                copy.wait_send()

        @pl.when(window >= 4)
        def _():
            copy = remote(
                fresh.at[at + STEPS - 1], halo.at[window, 1 - side, STEPS - 1],
                u_ssem.at[window, side], u_rsem.at[window, 1 - side], device,
            )
            if start:
                copy.start()
            else:
                copy.wait_send()

    def halo_wait(window):
        @pl.when(window < 4)
        def _():
            for side in range(2):
                ref = halo.at[window, side]
                pltpu.make_async_copy(ref, ref, u_rsem.at[window, side]).wait()

        @pl.when(window >= 4)
        def _():
            for side in range(2):
                ref = halo.at[window, side, STEPS - 1]
                pltpu.make_async_copy(ref, ref, u_rsem.at[window, side]).wait()

    def out_copy(z, start):
        owner = z // depth
        source = out_rows.at[z]
        target = out.at[lax.rem(z, depth), pl.ds(pl.multiple_of(OWN * p, OWN), OWN), :]

        @pl.when(owner != g)
        def _():
            copy = remote(source, target, o_ssem.at[z], o_rsem, (owner, a, q))
            if start:
                copy.start()
            else:
                copy.wait_send()

        if start:
            @pl.when(owner == g)
            def _():
                pltpu.make_async_copy(source, target, o_rsem).start()

    def window_step(window, carry):
        backward = window // 4
        m0 = STEPS * (window - 4 * backward)
        at = (NZ + 1) * backward + m0
        t0 = STEPS * window
        opening = m0 == 0

        def source_plane(m):
            return src[m + backward * (NZ - 1 - 2 * m)]

        @pl.when(opening)
        def _():
            base[0] = zero_tile

        @pl.when(jnp.logical_not(opening))
        def _():
            base[0] = fresh[jnp.maximum(t0 - 1, 0)]

        def base_step(t, before):
            cell = old[at + t]
            residual = source_plane(m0 + t) - 27.0 * cell + box(cell + old[at + t + 1] + before)
            now = jnp.where(inside, cell + apply(residual), 0.0)
            base[t + 1] = now
            return now

        lax.fori_loop(0, STEPS - 1, base_step, base[0])

        @pl.when(window == 0)
        def _():
            e_tmp[...] = jnp.zeros(e_tmp.shape, F32)

        @pl.when(window > 0)
        def _():
            for t in range(STEPS):
                tile = fresh.at[jnp.maximum(t0 - STEPS + t, 0)]
                e_tmp[t : t + 1, :] = tile[:1, :]
                e_tmp[8 + t : 9 + t, :] = tile[SPAN - 1 :, :]

        for t in range(1, STEPS):
            e_tmp[3 + t : 4 + t, :] = base[t, :1, :]
            e_tmp[11 + t : 12 + t, :] = base[t, SPAN - 1 :, :]
        for e in range(2):
            e_send[window, 8 * e : 8 * e + 8, :] = own_edges(e_tmp[8 * e : 8 * e + 8, :], e)
        edge_copies(e_send.at[window], e_recv.at[window], e_ssem.at[window], e_rsem.at[window], True)

        @pl.when(window == 0)
        def _():
            pltpu.make_async_copy(t_recv, t_recv, t_rsem).wait()
            for k in range(9):
                part = jnp.where(inside[:8], gathered(t_recv, slice(8 * k, 8 * k + 8)), 0.0)
                if k < 5:
                    coef[8 * k : 8 * k + 8, :] = part
                else:
                    e = (k - 5) // 2
                    for r in range(8):
                        e_old[8 * ((k - 5) % 2) + r, e : e + 1, :] = part[r : r + 1]

        arrived = e_recv.at[window]
        pltpu.make_async_copy(arrived, arrived, e_rsem.at[window]).wait()
        edges = [jnp.where(inside[:8], gathered(arrived, slice(8 * e, 8 * e + 8)), 0.0) for e in range(2)]

        @pl.when(jnp.logical_and(window > 0, window <= 4))
        def _():
            for t in range(STEPS):
                for e in range(2):
                    e_old[2 * NZ - jnp.maximum(t0 - STEPS + t, 0), e : e + 1, :] = edges[e][t : t + 1]

        before = [jnp.where(opening, 0.0, edges[e][STEPS - 1 : STEPS]) for e in range(2)]
        gives = []
        for t in range(STEPS):
            total = [
                before[e] + (e_old[at + t, e : e + 1, :] + e_old[at + t + 1, e : e + 1, :]) for e in range(2)
            ]
            from_low = [roll(total[1], SPAN - c) for c in SHIFTS]
            from_high = [roll(total[0], -SPAN - c) for c in SHIFTS]
            give = {}
            for d in range(-2, 3):
                k = d + 3
                give[0, d] = jnp.where(group1 > 0, from_low[k - 1] + from_low[k] + from_low[k + 1], 0.0)
                give[1, d] = jnp.where(group1 < gy - 1, from_high[k - 1] + from_high[k] + from_high[k + 1], 0.0)
            gives.append(give)
            given[t, 0:1, :] = pltpu.roll(give[0, 0], lax.rem(128 - SPAN * q, 128), 1)
            given[t, 1:2, :] = pltpu.roll(give[1, 0], SPAN * (3 - q), 1)
            if t == STEPS - 1:
                break
            before = []
            for e in range(2):
                value = edges[e][STEPS + t : STEPS + t + 1]
                for s in range(t + 1):
                    lag = t - s
                    first_row = (0, 4, 16)[lag]
                    for f in range(2):
                        for d in range(-lag, lag + 1):
                            r = first_row + (2 * e + f) * (2 * lag + 1) + d + lag
                            value = value + coef[r : r + 1, :] * gives[s][f, d]
                before.append(jnp.where(inside1, value, 0.0))

        @pl.when(window > 0)
        def _():
            halo_wait(window - 1)

        def merged(t):
            mid = fresh[jnp.maximum(t0 - STEPS + t, 0)]
            w = jnp.maximum(window - 1, 0)
            tile = jnp.where(
                xlane < HALO, roll(halo[w, 0, t], -OWN),
                jnp.where(xlane >= HALO + OWN, roll(halo[w, 1, t], OWN), mid),
            )
            return jnp.where(inside, tile, 0.0)

        @pl.when(jnp.logical_and(window > 0, window <= 4))
        def _():
            for t in range(STEPS):
                old[2 * NZ - jnp.maximum(t0 - STEPS + t, 0)] = merged(t)

        @pl.when(jnp.logical_not(opening))
        def _():
            base[0] = merged(STEPS - 1)

        def true_step(t, before):
            cell = old[at + t]
            residual = source_plane(m0 + t) - 27.0 * cell + box(cell + old[at + t + 1] + before)
            residual = residual + jnp.where(top_cell, given[t, 0:1, :], 0.0)
            residual = residual + jnp.where(bottom_cell, given[t, 1:2, :], 0.0)
            now = jnp.where(inside, cell + apply(residual), 0.0)
            fresh[t0 + t] = now

            @pl.when(backward == 0)
            def _():
                old[2 * NZ - jnp.minimum(t0 + t, NZ - 1)] = now

            return now

        lax.fori_loop(0, STEPS, true_step, base[0])

        @pl.when(window < 7)
        def _():
            halo_copy(window, 0, True)
            halo_copy(window, 1, True)

        @pl.when(backward == 1)
        def _():
            tiles = [fresh[t0 + k] for k in range(4)]
            parts = []
            for i in range(4):
                part = tiles[0] if i == 0 else roll(tiles[0], -SPAN * i)
                for k in range(1, 4):
                    part = jnp.where(group == k, roll(tiles[k], SPAN * (k - i)), part)
                parts.append(part)
            lines = jnp.concatenate(parts, axis=0).T
            for k in range(4):
                z = jnp.maximum(2 * NZ - 1 - t0 - k, 0)
                out_rows[z] = lines[SPAN * k + HALO : SPAN * k + HALO + OWN]
                out_copy(z, True)

        return carry

    lax.fori_loop(0, 8, window_step, 0)

    field_copies(False)
    b_remote(False)
    edge_copies(t_send, t_recv, t_ssem, t_rsem, False)

    def drain(window, carry):
        edge_copies(e_send.at[window], e_recv.at[window], e_ssem.at[window], e_rsem.at[window], False)

        @pl.when(window < 7)
        def _():
            halo_copy(window, 0, False)
            halo_copy(window, 1, False)

        return carry

    lax.fori_loop(0, 8, drain, 0)

    def drain_out(z, carry):
        out_copy(z, False)
        return carry

    lax.fori_loop(0, NZ, drain_out, 0)
    pltpu.make_async_copy(out, out, o_rsem).wait()


def solution(mesh):
    n, gx, gy = mesh.shape["gz"], mesh.shape["gx"], mesh.shape["gy"]

    def body(initial_field, source_term, block_inverse):
        depth, local, width = initial_field.shape
        vmem = lambda *shape: pltpu.VMEM(shape, F32)
        dma = pltpu.SemaphoreType.DMA
        return pl.pallas_call(
            functools.partial(kernel, n, gx, gy, depth),
            out_shape=jax.ShapeDtypeStruct(initial_field.shape, F32),
            in_specs=[pl.BlockSpec(memory_space=pl.ANY)] * 3,
            out_specs=pl.BlockSpec(memory_space=pltpu.VMEM),
            scratch_shapes=[
                vmem(NZ, SPAN, 128), vmem(NZ, SPAN, 128), vmem(SPAN * 128, 128), vmem(SPAN, 128, 128),
                vmem(2 * NZ + 2, SPAN, 128), vmem(NZ, SPAN, 128), vmem(2 * NZ, SPAN, 128),
                vmem(8, 2, STEPS, SPAN, 128), vmem(STEPS, SPAN, 128),
                vmem(2 * NZ, 128), vmem(8, 16, 128), vmem(8, 3, gy, 16, 128), vmem(72, 128), vmem(3, gy, 72, 128),
                vmem(2 * NZ + 2, 8, 128), vmem(40, 128), vmem(STEPS, 8, 128), vmem(2, SPAN, 128),
                vmem(6, SPAN, 128), vmem(6, SPAN, 128), vmem(NZ, OWN, 128),
                dma((2, n + 2)), dma((2,)), dma((3,)), dma((2,)),
                dma((8, 3 * gy)), dma((8,)), dma((3 * gy,)), dma,
                dma((8, 2)), dma((8, 2)), dma((NZ,)), dma,
            ],
            compiler_params=pltpu.CompilerParams(
                collective_id=0, has_side_effects=True, vmem_limit_bytes=40 * 1024 * 1024
            ),
        )(initial_field, source_term, block_inverse.reshape(local * width, width))

    return jax.shard_map(
        body, mesh=mesh,
        in_specs=(P("gz", "gx", "gy"), P("gz", "gx", "gy"), P("gx", "gy", None)),
        out_specs=P("gz", "gx", "gy"), check_vma=False,
    )
```

```python
import functools

import jax
import jax.numpy as jnp
from jax import lax
from jax.experimental import pallas as pl
from jax.experimental.pallas import tpu as pltpu
from jax.sharding import PartitionSpec as P

MESH = pl.DeviceIdType.MESH
F32 = jnp.float32
OWN = 16
HALO = 8
SPAN = 32
STEPS = 4
NZ = 16


def roll(value, shift, axis=1):
    size = value.shape[axis]
    shift = shift % size
    return value if shift == 0 else pltpu.roll(value, shift, axis)


def kernel(
    n, gx, gy, depth,
    v_in, s_in, b_in, out,
    v_rows, s_rows, b_rows, blocks, old, src, fresh, halo, base,
    free, e_send, e_recv, t_send, t_recv, e_old, coef, rows2, imp, resp, out_rows,
    field_send, field_recv, b_recv, b_send, e_ssem, e_rsem, t_ssem, t_rsem, u_ssem, u_rsem, o_ssem, o_rsem,
):
    g, a, q = lax.axis_index("gz"), lax.axis_index("gx"), lax.axis_index("gy")
    par = lax.rem(a, 2)
    local = OWN * n

    def flip(p):
        return p + par * (n - 1 - 2 * p)

    p = flip(g)
    a_left, a_right = lax.rem(a + gx - 1, gx), lax.rem(a + 1, gx)
    step_up = 1 - 2 * par
    first, last = p == 0, p == n - 1
    left = (jnp.where(first, g, g - step_up), jnp.where(first, a_left, a))
    right = (jnp.where(last, g, g + step_up), jnp.where(last, a_right, a))
    places = (left, (g, a), right)

    def remote(source, target, send, recv, device):
        return pltpu.make_async_remote_copy(
            src_ref=source, dst_ref=target, send_sem=send, recv_sem=recv, device_id=device, device_id_type=MESH
        )

    def b_local(source_line, row, count, sem):
        return pltpu.make_async_copy(
            b_in.at[pl.ds(pl.multiple_of(source_line * 128, 128), count * 128)],
            b_rows.at[pl.ds(row * 128, count * 128)], sem,
        )

    b_local(OWN * p, HALO, OWN, b_recv.at[0]).start()

    @pl.when(p > 0)
    def _():
        b_local(OWN * p - HALO, 0, HALO, b_recv.at[1]).start()

    @pl.when(p < n - 1)
    def _():
        b_local(OWN * p + OWN, HALO + OWN, HALO, b_recv.at[2]).start()

    barrier = pltpu.get_barrier_semaphore()

    def greet(i, carry):
        g2, a2 = lax.rem(i, n), lax.rem(a + gx - 1 + i // n, gx)

        @pl.when(jnp.logical_or(g2 != g, a2 != a))
        def _():
            pl.semaphore_signal(barrier, inc=1, device_id=(g2, a2, q), device_id_type=MESH)

        return carry

    lax.fori_loop(0, 3 * n, greet, 0)
    for place in places:
        for k in range(1, gy):
            pl.semaphore_signal(
                barrier, inc=1, device_id=(place[0], place[1], lax.rem(q + k, gy)), device_id_type=MESH
            )
    pl.semaphore_wait(barrier, 3 * n - 1 + 3 * (gy - 1))

    fields = ((v_in, v_rows), (s_in, s_rows))
    planes = pl.ds(depth * g, depth)

    def field_copies(start):
        for other in range(n):
            lo, hi = max(0, OWN * other - HALO), min(local, OWN * other + OWN + HALO)
            row = lo - (OWN * other - HALO)
            target = flip(other)
            for f, (source, place) in enumerate(fields):
                args = (source.at[:, pl.ds(lo, hi - lo), :], place.at[planes, pl.ds(row, hi - lo), :])

                @pl.when(target != g)
                def _():
                    copy = remote(*args, field_send.at[f, other], field_recv.at[f], (target, a, q))
                    if start:
                        copy.start()
                    else:
                        copy.wait_send()

                if start:
                    @pl.when(target == g)
                    def _():
                        pltpu.make_async_copy(*args, field_recv.at[f]).start()

        for f, (source, place) in enumerate(fields):
            ends = (
                (local - HALO, 0, (flip(n - 1), a_right, q), n),
                (0, HALO + OWN, (flip(0), a_left, q), n + 1),
            )
            for line, row, device, sem in ends:
                copy = remote(
                    source.at[:, pl.ds(line, HALO), :], place.at[planes, pl.ds(row, HALO), :],
                    field_send.at[f, sem], field_recv.at[f], device,
                )
                if start:
                    copy.start()
                else:
                    copy.wait_send()

    share = HALO // n

    def b_remote(start):
        for side, line, row, device in (
            (0, local - HALO, 0, (flip(n - 1), a_right, q)), (1, 0, HALO + OWN, (flip(0), a_left, q)),
        ):
            rows = lambda at: pl.ds(pl.multiple_of((at + share * g) * 128, 128), share * 128)
            copy = remote(b_in.at[rows(line)], b_rows.at[rows(row)], b_send.at[side], b_recv.at[1 + side], device)
            if start:
                copy.start()
            else:
                copy.wait_send()

    b_remote(True)
    field_copies(True)

    lane = lax.broadcasted_iota(jnp.int32, (SPAN, 128), 1)
    row = lax.broadcasted_iota(jnp.int32, (SPAN, 128), 0)
    group, xlane = lane // SPAN, lane % SPAN
    line = local * a + OWN * p - HALO + xlane
    inside = jnp.logical_and(line >= 0, line < local * gx)
    low_half, even = group < 2, group % 2 == 0
    group1 = group[:1]
    group8, xlane8, inside8, sub8 = group[:8], xlane[:8], inside[:8], row[:8]
    ends8 = jnp.logical_and(jnp.logical_or(sub8 == 0, sub8 == 7), jnp.logical_and(xlane8 >= HALO, xlane8 < HALO + OWN))
    top8, bottom8 = jnp.logical_and(sub8 == 0, group8 == 0), jnp.logical_and(sub8 == 7, group8 == 3)

    def y_sum(cells):
        up = jnp.where(group1 == 0, 0.0, roll(cells[SPAN - 1 :], SPAN))
        down = jnp.where(group1 == 3, 0.0, roll(cells[:1], -SPAN))
        return cells + jnp.where(row == 0, up, roll(cells, 1, 0)) + jnp.where(row == SPAN - 1, down, roll(cells, -1, 0))

    def box(cells):
        return y_sum(cells + roll(cells, 1) + roll(cells, -1))

    def apply(residual):
        acc = blocks[0] * residual[:1]
        for j in range(1, SPAN):
            acc = acc + blocks[j] * residual[j : j + 1]
        a0, a1, a2, a3 = (acc[SPAN * i : SPAN * (i + 1)] for i in range(4))
        b0 = jnp.where(low_half, a0, a2) + roll(jnp.where(low_half, a2, a0), 64)
        b1 = jnp.where(low_half, a1, a3) + roll(jnp.where(low_half, a3, a1), 64)
        other = jnp.where(even, b1, b0)
        return jnp.where(even, b0 + roll(other, -SPAN), b1 + roll(other, SPAN))

    def turn(x, carry):
        rows = pl.ds(pl.multiple_of(x * 128, 128), 128)
        b_rows[rows, :] = b_rows[rows, :].T
        return carry

    b_local(0, HALO, OWN, b_recv.at[0]).wait()
    lax.fori_loop(HALO, HALO + OWN, turn, 0, unroll=4)
    b_local(0, 0, HALO, b_recv.at[1]).wait()
    lax.fori_loop(0, HALO, turn, 0, unroll=4)
    b_local(0, HALO + OWN, HALO, b_recv.at[2]).wait()
    lax.fori_loop(HALO + OWN, SPAN, turn, 0, unroll=4)

    def gather(j, carry):
        parts = [b_rows[pl.ds(SPAN * jg + j, SPAN, stride=128), :] for jg in range(4)]
        blocks[j] = jnp.concatenate(parts, axis=0).T
        return carry

    lax.fori_loop(0, SPAN, gather, 0, unroll=4)

    columns, cells = [], []
    for slot, at in ((0, 0), (SPAN - 1, 3)):
        column = jnp.zeros((SPAN, 128), F32)
        for i in range(4):
            column = jnp.where(group == i, roll(blocks[slot, SPAN * i : SPAN * (i + 1), :], SPAN * (i - at)), column)
        columns.append(jnp.where(inside, column, 0.0))
        cells.append(y_sum(columns[-1]))
    resp[6], resp[7] = columns
    for j in range(SPAN):
        rows2[0, j : j + 1, :] = blocks[j, :1, :]
        rows2[1, j : j + 1, :] = blocks[j, 127:, :]
    for e in range(2):
        for d in range(3):
            imp[3 * e + d] = roll(cells[e], -(d - 1))

    def respond(i, carry):
        resp[i] = y_sum(jnp.where(inside, apply(imp[i]), 0.0))
        return carry

    lax.fori_loop(0, 6, respond, 0)

    def spread(value):
        total = value + roll(value, 32)
        return total + roll(total, 64)

    def pair(values):
        return jnp.where(sub8 == 0, spread(values[0]), spread(values[1]))

    def dots(value):
        return pair([jnp.sum(rows2[e] * value, axis=0, keepdims=True) for e in range(2)])

    def packed(pairs):
        tile = None
        for m in range(0, len(pairs), 4):
            part = jnp.zeros((8, 128), F32)
            for k, value in enumerate(pairs[m : m + 4]):
                part = jnp.where(group8 == k, value, part)
            part = roll(jnp.where(ends8, part, 0.0), m // 2, 0)
            tile = part if tile is None else tile + part
        return tile

    def edge_pair(top, bottom, k):
        return jnp.where(sub8 == 0, roll(top, SPAN * k), roll(bottom, SPAN * (k - 3)))

    first_pairs = [
        pair([jnp.where(group1 == 0, rows2[e, :1, :], 0.0) for e in range(2)]),
        pair([jnp.where(group1 == 3, rows2[e, SPAN - 1 :, :], 0.0) for e in range(2)]),
    ]
    coef[0] = packed(first_pairs)
    later_pairs = [dots(roll(cells[f], -d)) for f in range(2) for d in range(-1, 2)]
    for f in range(2):
        for d in range(-2, 3):
            total = None
            for near in range(-1, 2):
                far = d - near
                if abs(far) <= 1:
                    term = roll(resp[3 * f + far + 1], -near)
                    total = term if total is None else total + term
            later_pairs.append(dots(total))
    t_send[0] = packed(later_pairs)

    for f, (place, rows_ref) in enumerate(((old, v_rows), (src, s_rows))):
        pltpu.make_async_copy(rows_ref, rows_ref, field_recv.at[f]).wait()
        for w in range(NZ // 4):
            turned = rows_ref[4 * w : 4 * w + 4].reshape(128, 128).T
            for k in range(4):
                tile = jnp.zeros((SPAN, 128), F32)
                for i in range(4):
                    tile = jnp.where(group == i, roll(turned[SPAN * i : SPAN * (i + 1)], SPAN * (i - k)), tile)
                place[4 * w + k] = jnp.where(inside, tile, 0.0)
    zero_tile, zero8 = jnp.zeros((SPAN, 128), F32), jnp.zeros((8, 128), F32)
    old[NZ] = zero_tile
    old[2 * NZ + 1] = zero_tile
    e_old[NZ] = jnp.zeros((8, 128), F32)
    e_old[2 * NZ + 1] = jnp.zeros((8, 128), F32)
    t_send[1] = packed([edge_pair(old[z, :8, :], old[z, SPAN - 8 :, :], z % 4) for z in range(NZ)])

    def edge_copies(source, target, send, recv, start):
        for x, place in enumerate(places):
            for k in range(gy):
                if x == 1 and k == 0:
                    if start:
                        pltpu.make_async_copy(source, target.at[1, q], recv).start()
                    continue
                copy = remote(
                    source, target.at[2 - x, q], send.at[3 * k + x], recv, (place[0], place[1], lax.rem(q + k, gy))
                )
                if start:
                    copy.start()
                else:
                    copy.wait_send()

    edge_copies(t_send, t_recv, t_ssem, t_rsem, True)

    def unpacked(ref, at=None):
        tiles = []
        for k in range(gy):
            sides = [ref[x, k] if at is None else ref[x, k, at] for x in range(3)]
            tiles.append(jnp.where(
                xlane8 < HALO, roll(sides[0], -OWN), jnp.where(xlane8 >= HALO + OWN, roll(sides[2], OWN), sides[1])
            ))
        whole = []
        for k in range(4):
            tile = jnp.zeros((8, 128), F32)
            for b in range(gy):
                tile = jnp.where(group8 == b, roll(tiles[b], SPAN * (b - k)), tile)
            whole.append(jnp.where(inside8, tile, 0.0))
        return lambda i: roll(whole[i % 4], -2 * (i // 4), 0)

    def halo_copy(window, side, start):
        device = places[2 * side]
        device = (device[0], device[1], q)
        at = STEPS * window

        @pl.when(window < 4)
        def _():
            copy = remote(
                fresh.at[pl.ds(at, STEPS)], halo.at[window, 1 - side],
                u_ssem.at[window, side], u_rsem.at[window, 1 - side], device,
            )
            if start:
                copy.start()
            else:
                copy.wait_send()

        @pl.when(window >= 4)
        def _():
            copy = remote(
                fresh.at[at + STEPS - 1], halo.at[window, 1 - side, STEPS - 1],
                u_ssem.at[window, side], u_rsem.at[window, 1 - side], device,
            )
            if start:
                copy.start()
            else:
                copy.wait_send()

    def halo_wait(window):
        @pl.when(window < 4)
        def _():
            for side in range(2):
                ref = halo.at[window, side]
                pltpu.make_async_copy(ref, ref, u_rsem.at[window, side]).wait()

        @pl.when(window >= 4)
        def _():
            for side in range(2):
                ref = halo.at[window, side, STEPS - 1]
                pltpu.make_async_copy(ref, ref, u_rsem.at[window, side]).wait()

    def out_copy(z, start):
        owner = z // depth
        source = out_rows.at[z]
        target = out.at[lax.rem(z, depth), pl.ds(pl.multiple_of(OWN * p, OWN), OWN), :]

        @pl.when(owner != g)
        def _():
            copy = remote(source, target, o_ssem.at[z], o_rsem, (owner, a, q))
            if start:
                copy.start()
            else:
                copy.wait_send()

        if start:
            @pl.when(owner == g)
            def _():
                pltpu.make_async_copy(source, target, o_rsem).start()

    def window_step(window, carry):
        backward = window // 4
        m0 = STEPS * (window - 4 * backward)
        at = (NZ + 1) * backward + m0
        t0 = STEPS * window
        opening = m0 == 0

        def source_plane(m):
            return src[m + backward * (NZ - 1 - 2 * m)]

        @pl.when(opening)
        def _():
            base[0] = zero_tile

        @pl.when(jnp.logical_not(opening))
        def _():
            base[0] = fresh[jnp.maximum(t0 - 1, 0)]

        def base_step(t, before):
            cell = old[at + t]
            residual = source_plane(m0 + t) - 27.0 * cell + box(cell + old[at + t + 1] + before)
            now = jnp.where(inside, cell + apply(residual), 0.0)
            base[t + 1] = now
            return now

        lax.fori_loop(0, STEPS - 1, base_step, base[0])

        guesses = [edge_pair(base[k + 1, :8, :], base[k + 1, SPAN - 8 :, :], k) for k in range(STEPS - 1)]
        done = []
        for k in range(STEPS):
            tile = fresh.at[jnp.maximum(t0 - STEPS + k, 0)]
            done.append(edge_pair(tile[:8, :], tile[SPAN - 8 :, :], k))
        e_send[window] = jnp.where(window == 0, coef[0], packed(done)) + packed([zero8] * 4 + guesses)
        edge_copies(e_send.at[window], e_recv.at[window], e_ssem.at[window], e_rsem.at[window], True)

        @pl.when(window > 0)
        def _():
            halo_wait(window - 1)

        def merged(t):
            mid = fresh[jnp.maximum(t0 - STEPS + t, 0)]
            w = jnp.maximum(window - 1, 0)
            tile = jnp.where(
                xlane < HALO, roll(halo[w, 0, t], -OWN),
                jnp.where(xlane >= HALO + OWN, roll(halo[w, 1, t], OWN), mid),
            )
            return jnp.where(inside, tile, 0.0)

        @pl.when(jnp.logical_and(window > 0, window <= 4))
        def _():
            for t in range(STEPS):
                old[2 * NZ - jnp.maximum(t0 - STEPS + t, 0)] = merged(t)

        @pl.when(jnp.logical_not(opening))
        def _():
            base[0] = merged(STEPS - 1)

        for t in range(STEPS):
            cell = old[at + t]
            around = cell + old[at + t + 1]
            free[t] = source_plane(m0 + t) - 27.0 * cell + box(around + base[0] if t == 0 else around)
        free[0] = old[at] + apply(free[0])

        @pl.when(window == 0)
        def _():
            pltpu.make_async_copy(t_recv, t_recv, t_rsem).wait()
            item = unpacked(t_recv, 0)
            for r in range(16):
                coef[2 + r] = item(r)
            item = unpacked(t_recv, 1)
            for r in range(NZ):
                e_old[r] = item(r)

        arrived = e_recv.at[window]
        pltpu.make_async_copy(arrived, arrived, e_rsem.at[window]).wait()
        item = unpacked(arrived)

        @pl.when(window == 0)
        def _():
            for r in range(2):
                coef[r] = item(r)

        @pl.when(jnp.logical_and(window > 0, window <= 4))
        def _():
            for t in range(STEPS):
                e_old[2 * NZ - jnp.maximum(t0 - STEPS + t, 0)] = item(t)

        before = jnp.where(opening, 0.0, item(STEPS - 1))
        gives = []
        now = None
        for t in range(STEPS):
            total = before + (e_old[at + t] + e_old[at + t + 1])
            reach = max(0, STEPS - 2 - t)
            low, high = jnp.broadcast_to(total[7:], (8, 128)), jnp.broadcast_to(total[:1], (8, 128))
            from_low = {c: roll(low, SPAN - c) for c in range(-reach - 1, reach + 2)}
            from_high = {c: roll(high, -SPAN - c) for c in range(-reach - 1, reach + 2)}
            give = {}
            for d in range(-reach, reach + 1):
                give[0, d] = jnp.where(group8 > 0, from_low[d - 1] + from_low[d] + from_low[d + 1], 0.0)
                give[1, d] = jnp.where(group8 < gy - 1, from_high[d - 1] + from_high[d] + from_high[d + 1], 0.0)
            gives.append(give)
            if t == 0:
                mine = [spread(jnp.where(group8 == q, give[f, 0], 0.0)) for f in range(2)]
                change = [resp[6 + f] * mine[f][:1] for f in range(2)]
                now = jnp.where(inside, free[0] + (change[0] + change[1]), 0.0)
            else:
                mine = (
                    jnp.where(top8, pltpu.roll(give[0, 0], lax.rem(128 - SPAN * q, 128), 1), 0.0),
                    jnp.where(bottom8, pltpu.roll(give[1, 0], SPAN * (3 - q), 1), 0.0),
                )
                residual = free[t] + box(now)
                residual = jnp.concatenate(
                    [residual[:8] + mine[0], residual[8 : SPAN - 8], residual[SPAN - 8 :] + mine[1]], axis=0
                )
                now = jnp.where(inside, old[at + t] + apply(residual), 0.0)
            fresh[t0 + t] = now
            if t < STEPS - 1:
                value = item(STEPS + t)
                for s in range(t + 1):
                    lag = t - s
                    for f in range(2):
                        for d in range(-lag, lag + 1):
                            r = (0, 2, 8)[lag] + f * (2 * lag + 1) + d + lag
                            value = value + coef[r] * gives[s][f, d]
                before = jnp.where(inside8, value, 0.0)

        @pl.when(backward == 0)
        def _():
            for t in range(STEPS):
                old[2 * NZ - jnp.minimum(t0 + t, NZ - 1)] = fresh[t0 + t]

        @pl.when(window < 7)
        def _():
            halo_copy(window, 0, True)
            halo_copy(window, 1, True)

        @pl.when(backward == 1)
        def _():
            tiles = [fresh[t0 + k] for k in range(4)]
            parts = []
            for i in range(4):
                part = tiles[0] if i == 0 else roll(tiles[0], -SPAN * i)
                for k in range(1, 4):
                    part = jnp.where(group == k, roll(tiles[k], SPAN * (k - i)), part)
                parts.append(part)
            lines = jnp.concatenate(parts, axis=0).T
            for k in range(4):
                z = jnp.maximum(2 * NZ - 1 - t0 - k, 0)
                out_rows[z] = lines[SPAN * k + HALO : SPAN * k + HALO + OWN]
                out_copy(z, True)

        return carry

    lax.fori_loop(0, 8, window_step, 0)

    field_copies(False)
    b_remote(False)
    edge_copies(t_send, t_recv, t_ssem, t_rsem, False)

    def drain(window, carry):
        edge_copies(e_send.at[window], e_recv.at[window], e_ssem.at[window], e_rsem.at[window], False)

        @pl.when(window < 7)
        def _():
            halo_copy(window, 0, False)
            halo_copy(window, 1, False)

        return carry

    lax.fori_loop(0, 8, drain, 0)

    def drain_out(z, carry):
        out_copy(z, False)
        return carry

    lax.fori_loop(0, NZ, drain_out, 0)
    pltpu.make_async_copy(out, out, o_rsem).wait()


def solution(mesh):
    n, gx, gy = mesh.shape["gz"], mesh.shape["gx"], mesh.shape["gy"]

    def body(initial_field, source_term, block_inverse):
        depth, local, width = initial_field.shape
        vmem = lambda *shape: pltpu.VMEM(shape, F32)
        dma = pltpu.SemaphoreType.DMA
        return pl.pallas_call(
            functools.partial(kernel, n, gx, gy, depth),
            out_shape=jax.ShapeDtypeStruct(initial_field.shape, F32),
            in_specs=[pl.BlockSpec(memory_space=pltpu.HBM)] * 3,
            out_specs=pl.BlockSpec(memory_space=pltpu.VMEM),
            scratch_shapes=[
                vmem(NZ, SPAN, 128), vmem(NZ, SPAN, 128), vmem(SPAN * 128, 128), vmem(SPAN, 128, 128),
                vmem(2 * NZ + 2, SPAN, 128), vmem(NZ, SPAN, 128), vmem(2 * NZ, SPAN, 128),
                vmem(8, 2, STEPS, SPAN, 128), vmem(STEPS, SPAN, 128),
                vmem(STEPS, SPAN, 128), vmem(8, 8, 128), vmem(8, 3, gy, 8, 128), vmem(2, 8, 128), vmem(3, gy, 2, 8, 128),
                vmem(2 * NZ + 2, 8, 128), vmem(18, 8, 128), vmem(2, SPAN, 128),
                vmem(6, SPAN, 128), vmem(8, SPAN, 128), vmem(NZ, OWN, 128),
                dma((2, n + 2)), dma((2,)), dma((3,)), dma((2,)),
                dma((8, 3 * gy)), dma((8,)), dma((3 * gy,)), dma,
                dma((8, 2)), dma((8, 2)), dma((NZ,)), dma,
            ],
            compiler_params=pltpu.CompilerParams(
                collective_id=0, has_side_effects=True, vmem_limit_bytes=60 * 1024 * 1024
            ),
        )(initial_field, source_term, block_inverse.reshape(local * width, width))

    return jax.shard_map(
        body, mesh=mesh,
        in_specs=(P("gz", "gx", "gy"), P("gz", "gx", "gy"), P("gx", "gy", None)),
        out_specs=P("gz", "gx", "gy"), check_vma=False,
    )
```

```python
import functools

import jax
import jax.numpy as jnp
from jax import lax
from jax.experimental import pallas as pl
from jax.experimental.pallas import tpu as pltpu
from jax.sharding import PartitionSpec as P

MESH = pl.DeviceIdType.MESH
F32 = jnp.float32
OWN = 16
HALO = 8
SPAN = 32
STEPS = 4
NZ = 16


def roll(value, shift, axis=1):
    size = value.shape[axis]
    shift = shift % size
    return value if shift == 0 else pltpu.roll(value, shift, axis)


def kernel(
    n, gx, gy, depth,
    v_in, s_in, b_in, out,
    v_rows, s_rows, b_rows, blocks, old, src, fresh, halo,
    free, res, pad, last_box, start, e_send, e_recv, t_send, t_recv, e_old, coef, rows2, imp, resp, out_rows,
    field_send, field_recv, b_recv, b_send, e_ssem, e_rsem, t_ssem, t_rsem, u_ssem, u_rsem, o_ssem, o_rsem,
):
    g, a, q = lax.axis_index("gz"), lax.axis_index("gx"), lax.axis_index("gy")
    par = lax.rem(a, 2)
    local = OWN * n

    def flip(p):
        return p + par * (n - 1 - 2 * p)

    p = flip(g)
    a_left, a_right = lax.rem(a + gx - 1, gx), lax.rem(a + 1, gx)
    step_up = 1 - 2 * par
    first, last = p == 0, p == n - 1
    left = (jnp.where(first, g, g - step_up), jnp.where(first, a_left, a))
    right = (jnp.where(last, g, g + step_up), jnp.where(last, a_right, a))
    places = (left, (g, a), right)

    def remote(source, target, send, recv, device):
        return pltpu.make_async_remote_copy(
            src_ref=source, dst_ref=target, send_sem=send, recv_sem=recv, device_id=device, device_id_type=MESH
        )

    def b_local(source_line, row, count, sem):
        return pltpu.make_async_copy(
            b_in.at[pl.ds(pl.multiple_of(source_line * 128, 128), count * 128)],
            b_rows.at[pl.ds(row * 128, count * 128)], sem,
        )

    b_local(OWN * p, HALO, OWN, b_recv.at[0]).start()

    @pl.when(p > 0)
    def _():
        b_local(OWN * p - HALO, 0, HALO, b_recv.at[1]).start()

    @pl.when(p < n - 1)
    def _():
        b_local(OWN * p + OWN, HALO + OWN, HALO, b_recv.at[2]).start()

    barrier = pltpu.get_barrier_semaphore()

    def greet(i, carry):
        g2, a2 = lax.rem(i, n), lax.rem(a + gx - 1 + i // n, gx)

        @pl.when(jnp.logical_or(g2 != g, a2 != a))
        def _():
            pl.semaphore_signal(barrier, inc=1, device_id=(g2, a2, q), device_id_type=MESH)

        return carry

    lax.fori_loop(0, 3 * n, greet, 0)
    for place in places:
        for k in range(1, gy):
            pl.semaphore_signal(
                barrier, inc=1, device_id=(place[0], place[1], lax.rem(q + k, gy)), device_id_type=MESH
            )
    pl.semaphore_wait(barrier, 3 * n - 1 + 3 * (gy - 1))

    fields = ((v_in, v_rows), (s_in, s_rows))
    planes = pl.ds(depth * g, depth)

    def field_copies(start):
        for other in range(n):
            lo, hi = max(0, OWN * other - HALO), min(local, OWN * other + OWN + HALO)
            row = lo - (OWN * other - HALO)
            target = flip(other)
            for f, (source, place) in enumerate(fields):
                args = (source.at[:, pl.ds(lo, hi - lo), :], place.at[planes, pl.ds(row, hi - lo), :])

                @pl.when(target != g)
                def _():
                    copy = remote(*args, field_send.at[f, other], field_recv.at[f], (target, a, q))
                    if start:
                        copy.start()
                    else:
                        copy.wait_send()

                if start:
                    @pl.when(target == g)
                    def _():
                        pltpu.make_async_copy(*args, field_recv.at[f]).start()

        for f, (source, place) in enumerate(fields):
            ends = (
                (local - HALO, 0, (flip(n - 1), a_right, q), n),
                (0, HALO + OWN, (flip(0), a_left, q), n + 1),
            )
            for line, row, device, sem in ends:
                copy = remote(
                    source.at[:, pl.ds(line, HALO), :], place.at[planes, pl.ds(row, HALO), :],
                    field_send.at[f, sem], field_recv.at[f], device,
                )
                if start:
                    copy.start()
                else:
                    copy.wait_send()

    share = HALO // n

    def b_remote(start):
        for side, line, row, device in (
            (0, local - HALO, 0, (flip(n - 1), a_right, q)), (1, 0, HALO + OWN, (flip(0), a_left, q)),
        ):
            rows = lambda at: pl.ds(pl.multiple_of((at + share * g) * 128, 128), share * 128)
            copy = remote(b_in.at[rows(line)], b_rows.at[rows(row)], b_send.at[side], b_recv.at[1 + side], device)
            if start:
                copy.start()
            else:
                copy.wait_send()

    b_remote(True)
    field_copies(True)

    lane = lax.broadcasted_iota(jnp.int32, (SPAN, 128), 1)
    row = lax.broadcasted_iota(jnp.int32, (SPAN, 128), 0)
    group, xlane = lane // SPAN, lane % SPAN
    line = local * a + OWN * p - HALO + xlane
    inside = jnp.logical_and(line >= 0, line < local * gx)
    low_half, even = group < 2, group % 2 == 0
    group1 = group[:1]
    group8, xlane8, inside8, sub8 = group[:8], xlane[:8], inside[:8], row[:8]
    ends8 = jnp.logical_and(jnp.logical_or(sub8 == 0, sub8 == 7), jnp.logical_and(xlane8 >= HALO, xlane8 < HALO + OWN))
    top8, bottom8 = jnp.logical_and(sub8 == 0, group8 == 0), jnp.logical_and(sub8 == 7, group8 == 3)

    zero8 = jnp.zeros((8, 128), F32)

    def y_sum(cells):
        up = jnp.where(group1 == 0, 0.0, roll(cells[SPAN - 1 :], SPAN))
        down = jnp.where(group1 == 3, 0.0, roll(cells[:1], -SPAN))
        return cells + jnp.where(row == 0, up, roll(cells, 1, 0)) + jnp.where(row == SPAN - 1, down, roll(cells, -1, 0))

    def box(cells):
        return y_sum(cells + roll(cells, 1) + roll(cells, -1))

    def product(residual, slot):
        res[slot] = residual
        acc = blocks[0] * res[slot, :1, :]
        for j in range(1, SPAN):
            acc = acc + blocks[j] * res[slot, j : j + 1, :]
        rows = [acc[SPAN * i : SPAN * (i + 1)] for i in range(4)]
        parts = []
        for k in range(4):
            part = rows[-k % 4]
            for i in range(1, 4):
                part = jnp.where(group == i, rows[(i - k) % 4], part)
            parts.append(part)
        return parts

    def summed(parts, shifts, at=slice(None)):
        total = None
        for k in range(4):
            for shift in shifts:
                term = roll(parts[k][at], shift - SPAN * k)
                total = term if total is None else total + term
        return total

    def plain(parts, at=slice(None)):
        return summed(parts, (0,), at)

    def apply(residual):
        return plain(product(residual, 7))

    def boxed(parts, slot):
        up = summed(parts, (SPAN - 1, SPAN, SPAN + 1), slice(SPAN - 8, SPAN))
        down = summed(parts, (-SPAN - 1, -SPAN, -SPAN + 1), slice(0, 8))
        pad[slot, :8, :] = jnp.where(group8 == 0, 0.0, up)
        pad[slot, 8 : SPAN + 8, :] = summed(parts, (-1, 0, 1))
        pad[slot, SPAN + 8 :, :] = jnp.where(group8 == 3, 0.0, down)
        return pad[slot, 7 : SPAN + 7, :] + pad[slot, 8 : SPAN + 8, :] + pad[slot, 9 : SPAN + 9, :]

    def turn(x, carry):
        rows = pl.ds(pl.multiple_of(x * 128, 128), 128)
        b_rows[rows, :] = b_rows[rows, :].T
        return carry

    b_local(0, HALO, OWN, b_recv.at[0]).wait()
    lax.fori_loop(HALO, HALO + OWN, turn, 0, unroll=4)
    b_local(0, 0, HALO, b_recv.at[1]).wait()
    lax.fori_loop(0, HALO, turn, 0, unroll=4)
    b_local(0, HALO + OWN, HALO, b_recv.at[2]).wait()
    lax.fori_loop(HALO + OWN, SPAN, turn, 0, unroll=4)

    def gather(j, carry):
        parts = [b_rows[pl.ds(SPAN * jg + j, SPAN, stride=128), :] for jg in range(4)]
        blocks[j] = jnp.where(inside[:1], jnp.concatenate(parts, axis=0).T, 0.0)
        return carry

    lax.fori_loop(0, SPAN, gather, 0, unroll=4)

    columns, cells = [], []
    for slot, at in ((0, 0), (SPAN - 1, 3)):
        column = jnp.zeros((SPAN, 128), F32)
        for i in range(4):
            column = jnp.where(group == i, roll(blocks[slot, SPAN * i : SPAN * (i + 1), :], SPAN * (i - at)), column)
        columns.append(jnp.where(inside, column, 0.0))
        cells.append(y_sum(columns[-1]))
    resp[6], resp[7] = columns
    for j in range(SPAN):
        rows2[0, j : j + 1, :] = blocks[j, :1, :]
        rows2[1, j : j + 1, :] = blocks[j, 127:, :]
    for e in range(2):
        for d in range(3):
            imp[3 * e + d] = roll(cells[e], -(d - 1))

    def respond(i, carry):
        resp[i] = y_sum(jnp.where(inside, apply(imp[i]), 0.0))
        return carry

    lax.fori_loop(0, 6, respond, 0)

    def spread(value):
        return (value + roll(value, 32)) + (roll(value, 64) + roll(value, 96))

    def pair(values):
        return jnp.where(sub8 == 0, spread(values[0]), spread(values[1]))

    def dots(value):
        return pair([jnp.sum(rows2[e] * value, axis=0, keepdims=True) for e in range(2)])

    def packed(pairs):
        tile = None
        for m in range(0, len(pairs), 4):
            part = jnp.zeros((8, 128), F32)
            for k, value in enumerate(pairs[m : m + 4]):
                part = jnp.where(group8 == k, value, part)
            part = roll(jnp.where(ends8, part, 0.0), m // 2, 0)
            tile = part if tile is None else tile + part
        return tile

    def edge_pair(top, bottom, k):
        return jnp.where(sub8 == 0, roll(top, SPAN * k), roll(bottom, SPAN * (k - 3)))

    first_pairs = [
        pair([jnp.where(group1 == 0, rows2[e, :1, :], 0.0) for e in range(2)]),
        pair([jnp.where(group1 == 3, rows2[e, SPAN - 1 :, :], 0.0) for e in range(2)]),
    ]
    coef[0] = packed([zero8] * 4 + first_pairs)
    later_pairs = [dots(roll(cells[f], -d)) for f in range(2) for d in range(-1, 2)]
    for f in range(2):
        for d in range(-2, 3):
            total = None
            for near in range(-1, 2):
                far = d - near
                if abs(far) <= 1:
                    term = roll(resp[3 * f + far + 1], -near)
                    total = term if total is None else total + term
            later_pairs.append(dots(total))
    t_send[0] = packed(later_pairs)

    for f, (place, rows_ref) in enumerate(((old, v_rows), (src, s_rows))):
        pltpu.make_async_copy(rows_ref, rows_ref, field_recv.at[f]).wait()
        for w in range(NZ // 4):
            turned = rows_ref[4 * w : 4 * w + 4].reshape(128, 128).T
            for k in range(4):
                tile = jnp.zeros((SPAN, 128), F32)
                for i in range(4):
                    tile = jnp.where(group == i, roll(turned[SPAN * i : SPAN * (i + 1)], SPAN * (i - k)), tile)
                place[4 * w + k] = jnp.where(inside, tile, 0.0)
    zero_tile = jnp.zeros((SPAN, 128), F32)
    old[NZ] = zero_tile
    old[2 * NZ + 1] = zero_tile
    e_old[NZ] = jnp.zeros((8, 128), F32)
    e_old[2 * NZ + 1] = jnp.zeros((8, 128), F32)
    t_send[1] = packed([edge_pair(old[z, :8, :], old[z, SPAN - 8 :, :], z % 4) for z in range(NZ)])

    def edge_copies(source, target, send, recv, start):
        for x, place in enumerate(places):
            for k in range(gy):
                if x == 1 and k == 0:
                    if start:
                        pltpu.make_async_copy(source, target.at[1, q], recv).start()
                    continue
                copy = remote(
                    source, target.at[2 - x, q], send.at[3 * k + x], recv, (place[0], place[1], lax.rem(q + k, gy))
                )
                if start:
                    copy.start()
                else:
                    copy.wait_send()

    edge_copies(t_send, t_recv, t_ssem, t_rsem, True)

    def unpacked(ref, at=None):
        tiles = []
        for k in range(gy):
            sides = [ref[x, k] if at is None else ref[x, k, at] for x in range(3)]
            tiles.append(jnp.where(
                xlane8 < HALO, roll(sides[0], -OWN), jnp.where(xlane8 >= HALO + OWN, roll(sides[2], OWN), sides[1])
            ))
        whole = []
        for k in range(4):
            tile = jnp.zeros((8, 128), F32)
            for b in range(gy):
                tile = jnp.where(group8 == b, roll(tiles[b], SPAN * (b - k)), tile)
            whole.append(jnp.where(inside8, tile, 0.0))
        return lambda i: roll(whole[i % 4], -2 * (i // 4), 0)

    def halo_copy(window, side, start):
        device = places[2 * side]
        device = (device[0], device[1], q)
        at = STEPS * window

        @pl.when(window < 4)
        def _():
            copy = remote(
                fresh.at[pl.ds(at, STEPS)], halo.at[window, 1 - side],
                u_ssem.at[window, side], u_rsem.at[window, 1 - side], device,
            )
            if start:
                copy.start()
            else:
                copy.wait_send()

        @pl.when(window >= 4)
        def _():
            copy = remote(
                fresh.at[at + STEPS - 1], halo.at[window, 1 - side, STEPS - 1],
                u_ssem.at[window, side], u_rsem.at[window, 1 - side], device,
            )
            if start:
                copy.start()
            else:
                copy.wait_send()

    def halo_wait(window):
        @pl.when(window < 4)
        def _():
            for side in range(2):
                ref = halo.at[window, side]
                pltpu.make_async_copy(ref, ref, u_rsem.at[window, side]).wait()

        @pl.when(window >= 4)
        def _():
            for side in range(2):
                ref = halo.at[window, side, STEPS - 1]
                pltpu.make_async_copy(ref, ref, u_rsem.at[window, side]).wait()

    def out_copy(z, start):
        owner = z // depth
        source = out_rows.at[z]
        target = out.at[lax.rem(z, depth), pl.ds(pl.multiple_of(OWN * p, OWN), OWN), :]

        @pl.when(owner != g)
        def _():
            copy = remote(source, target, o_ssem.at[z], o_rsem, (owner, a, q))
            if start:
                copy.start()
            else:
                copy.wait_send()

        if start:
            @pl.when(owner == g)
            def _():
                pltpu.make_async_copy(source, target, o_rsem).start()

    def window_step(window, carry):
        backward = window // 4
        m0 = STEPS * (window - 4 * backward)
        at = (NZ + 1) * backward + m0
        t0 = STEPS * window
        opening = m0 == 0

        def source_plane(m):
            return src[m + backward * (NZ - 1 - 2 * m)]

        guesses = []
        around = None
        for t in range(STEPS - 1):
            cell = old[at + t]
            near = cell + old[at + t + 1]
            residual = source_plane(m0 + t) - 27.0 * cell + box(near if t == 0 else near + old[at + t - 1])
            residual = residual + (jnp.where(opening, 0.0, last_box[...]) if t == 0 else boxed(around, t))
            around = product(residual, t)
            ends = (slice(0, 8), slice(SPAN - 8, SPAN))
            guesses.append(edge_pair(*(cell[end] + plain(around, end) for end in ends), t))
        done = []
        for k in range(STEPS):
            tile = fresh.at[jnp.maximum(t0 - STEPS + k, 0)]
            done.append(edge_pair(tile[:8, :], tile[SPAN - 8 :, :], k))
        first = packed(guesses + [jnp.where(window == 0, 0.0, done[3])])
        rest = packed([zero8] * 4 + [done[k] for k in range(3)])
        e_send[window] = first + jnp.where(window == 0, coef[0], rest)
        edge_copies(e_send.at[window], e_recv.at[window], e_ssem.at[window], e_rsem.at[window], True)

        @pl.when(window > 0)
        def _():
            halo_wait(window - 1)

        def merged(t):
            mid = fresh[jnp.maximum(t0 - STEPS + t, 0)]
            w = jnp.maximum(window - 1, 0)
            tile = jnp.where(
                xlane < HALO, roll(halo[w, 0, t], -OWN),
                jnp.where(xlane >= HALO + OWN, roll(halo[w, 1, t], OWN), mid),
            )
            return jnp.where(inside, tile, 0.0)

        @pl.when(jnp.logical_and(window > 0, window <= 4))
        def _():
            for t in range(STEPS):
                old[2 * NZ - jnp.maximum(t0 - STEPS + t, 0)] = merged(t)

        @pl.when(opening)
        def _():
            start[...] = zero_tile

        @pl.when(jnp.logical_not(opening))
        def _():
            start[...] = merged(STEPS - 1)

        for t in range(STEPS):
            cell = old[at + t]
            near = cell + old[at + t + 1]
            if t == 0:
                near = near + start[...]
            else:
                near = near + (free[0] if t == 1 else old[at + t - 1])
            value = source_plane(m0 + t) - 27.0 * cell + box(near)
            free[t] = cell + plain(product(value, 3)) if t == 0 else value

        @pl.when(window == 0)
        def _():
            pltpu.make_async_copy(t_recv, t_recv, t_rsem).wait()
            item = unpacked(t_recv, 0)
            for r in range(16):
                coef[2 + r] = item(r)
            item = unpacked(t_recv, 1)
            for r in range(NZ):
                e_old[r] = item(r)

        arrived = e_recv.at[window]
        pltpu.make_async_copy(arrived, arrived, e_rsem.at[window]).wait()
        item = unpacked(arrived)

        @pl.when(window == 0)
        def _():
            for r in range(2):
                coef[r] = item(4 + r)

        @pl.when(jnp.logical_and(window > 0, window <= 4))
        def _():
            for t in range(STEPS):
                e_old[2 * NZ - jnp.maximum(t0 - STEPS + t, 0)] = item(3 if t == 3 else 4 + t)

        before = jnp.where(opening, 0.0, item(3))
        gives = []
        around = None
        for t in range(STEPS):
            total = before + (e_old[at + t] + e_old[at + t + 1])
            reach = max(0, STEPS - 2 - t)
            low, high = jnp.broadcast_to(total[7:], (8, 128)), jnp.broadcast_to(total[:1], (8, 128))
            from_low = {c: roll(low, SPAN - c) for c in range(-reach - 1, reach + 2)}
            from_high = {c: roll(high, -SPAN - c) for c in range(-reach - 1, reach + 2)}
            give = {}
            for d in range(-reach, reach + 1):
                give[0, d] = jnp.where(group8 > 0, from_low[d - 1] + from_low[d] + from_low[d + 1], 0.0)
                give[1, d] = jnp.where(group8 < gy - 1, from_high[d - 1] + from_high[d] + from_high[d + 1], 0.0)
            gives.append(give)
            if t == 0:
                gain = {
                    key: spread(jnp.where(group8 == q, give[key], 0.0))[:1] for key in give if abs(key[1]) <= 1
                }
                now = free[0] + (resp[6] * gain[0, 0] + resp[7] * gain[1, 0])
            else:
                mine = (
                    jnp.where(top8, pltpu.roll(give[0, 0], lax.rem(128 - SPAN * q, 128), 1), 0.0),
                    jnp.where(bottom8, pltpu.roll(give[1, 0], SPAN * (3 - q), 1), 0.0),
                )
                if t == 1:
                    residual = free[1]
                    for f in range(2):
                        for d in range(-1, 2):
                            residual = residual + imp[3 * f + d + 1] * gain[f, d]
                else:
                    residual = free[t] + boxed(around, 1 + t)
                residual = jnp.concatenate(
                    [residual[:8] + mine[0], residual[8 : SPAN - 8], residual[SPAN - 8 :] + mine[1]], axis=0
                )
                around = product(residual, 3 + t)
                now = old[at + t] + plain(around)
            fresh[t0 + t] = now
            if t < STEPS - 1:
                value = item(t)
                for s in range(t + 1):
                    lag = t - s
                    for f in range(2):
                        for d in range(-lag, lag + 1):
                            r = (0, 2, 8)[lag] + f * (2 * lag + 1) + d + lag
                            value = value + coef[r] * gives[s][f, d]
                before = jnp.where(inside8, value, 0.0)

        last_box[...] = box(old[at + STEPS - 1]) + boxed(around, 4)

        @pl.when(backward == 0)
        def _():
            for t in range(STEPS):
                old[2 * NZ - jnp.minimum(t0 + t, NZ - 1)] = fresh[t0 + t]

        @pl.when(window < 7)
        def _():
            halo_copy(window, 0, True)
            halo_copy(window, 1, True)

        @pl.when(backward == 1)
        def _():
            tiles = [fresh[t0 + k] for k in range(4)]
            parts = []
            for i in range(4):
                part = tiles[0] if i == 0 else roll(tiles[0], -SPAN * i)
                for k in range(1, 4):
                    part = jnp.where(group == k, roll(tiles[k], SPAN * (k - i)), part)
                parts.append(part)
            lines = jnp.concatenate(parts, axis=0).T
            for k in range(4):
                z = jnp.maximum(2 * NZ - 1 - t0 - k, 0)
                out_rows[z] = lines[SPAN * k + HALO : SPAN * k + HALO + OWN]
                out_copy(z, True)

        return carry

    lax.fori_loop(0, 8, window_step, 0)

    field_copies(False)
    b_remote(False)
    edge_copies(t_send, t_recv, t_ssem, t_rsem, False)

    def drain(window, carry):
        edge_copies(e_send.at[window], e_recv.at[window], e_ssem.at[window], e_rsem.at[window], False)

        @pl.when(window < 7)
        def _():
            halo_copy(window, 0, False)
            halo_copy(window, 1, False)

        return carry

    lax.fori_loop(0, 8, drain, 0)

    def drain_out(z, carry):
        out_copy(z, False)
        return carry

    lax.fori_loop(0, NZ, drain_out, 0)
    pltpu.make_async_copy(out, out, o_rsem).wait()


def solution(mesh):
    n, gx, gy = mesh.shape["gz"], mesh.shape["gx"], mesh.shape["gy"]

    def body(initial_field, source_term, block_inverse):
        depth, local, width = initial_field.shape
        vmem = lambda *shape: pltpu.VMEM(shape, F32)
        dma = pltpu.SemaphoreType.DMA
        return pl.pallas_call(
            functools.partial(kernel, n, gx, gy, depth),
            out_shape=jax.ShapeDtypeStruct(initial_field.shape, F32),
            in_specs=[pl.BlockSpec(memory_space=pltpu.HBM)] * 3,
            out_specs=pl.BlockSpec(memory_space=pltpu.VMEM),
            scratch_shapes=[
                vmem(NZ, SPAN, 128), vmem(NZ, SPAN, 128), vmem(SPAN * 128, 128), vmem(SPAN, 128, 128),
                vmem(2 * NZ + 2, SPAN, 128), vmem(NZ, SPAN, 128), vmem(2 * NZ, SPAN, 128),
                vmem(8, 2, STEPS, SPAN, 128),
                vmem(STEPS, SPAN, 128), vmem(8, SPAN, 128), vmem(8, SPAN + 16, 128), vmem(SPAN, 128), vmem(SPAN, 128),
                vmem(8, 8, 128), vmem(8, 3, gy, 8, 128), vmem(2, 8, 128), vmem(3, gy, 2, 8, 128),
                vmem(2 * NZ + 2, 8, 128), vmem(18, 8, 128), vmem(2, SPAN, 128),
                vmem(6, SPAN, 128), vmem(8, SPAN, 128), vmem(NZ, OWN, 128),
                dma((2, n + 2)), dma((2,)), dma((3,)), dma((2,)),
                dma((8, 3 * gy)), dma((8,)), dma((3 * gy,)), dma,
                dma((8, 2)), dma((8, 2)), dma((NZ,)), dma,
            ],
            compiler_params=pltpu.CompilerParams(
                collective_id=0, has_side_effects=True, vmem_limit_bytes=60 * 1024 * 1024
            ),
        )(initial_field, source_term, block_inverse.reshape(local * width, width))

    return jax.shard_map(
        body, mesh=mesh,
        in_specs=(P("gz", "gx", "gy"), P("gz", "gx", "gy"), P("gx", "gy", None)),
        out_specs=P("gz", "gx", "gy"), check_vma=False,
    )
```

```python
import functools

import jax
import jax.numpy as jnp
from jax import lax
from jax.experimental import pallas as pl
from jax.experimental.pallas import tpu as pltpu
from jax.sharding import PartitionSpec as P

MESH = pl.DeviceIdType.MESH
F32 = jnp.float32
OWN = 16
HALO = 8
SPAN = 32
STEPS = 4
NZ = 16


def roll(value, shift, axis=1):
    size = value.shape[axis]
    shift = shift % size
    return value if shift == 0 else pltpu.roll(value, shift, axis)


def kernel(
    n, gx, gy, depth,
    v_in, s_in, b_in, out,
    v_rows, s_rows, b_rows, blocks, old, src, fresh, halo,
    free, res, pad, last_box, start, e_send, e_recv, t_send, t_recv, e_old, coef, rows2, imp, raw, wide, resp, out_rows,
    field_send, field_recv, b_recv, b_send, e_ssem, e_rsem, t_ssem, t_rsem, u_ssem, u_rsem, o_ssem, o_rsem,
):
    g, a, q = lax.axis_index("gz"), lax.axis_index("gx"), lax.axis_index("gy")
    par = lax.rem(a, 2)
    local = OWN * n

    def flip(p):
        return p + par * (n - 1 - 2 * p)

    p = flip(g)
    a_left, a_right = lax.rem(a + gx - 1, gx), lax.rem(a + 1, gx)
    step_up = 1 - 2 * par
    first, last = p == 0, p == n - 1
    left = (jnp.where(first, g, g - step_up), jnp.where(first, a_left, a))
    right = (jnp.where(last, g, g + step_up), jnp.where(last, a_right, a))
    places = (left, (g, a), right)

    def remote(source, target, send, recv, device):
        return pltpu.make_async_remote_copy(
            src_ref=source, dst_ref=target, send_sem=send, recv_sem=recv, device_id=device, device_id_type=MESH
        )

    def b_local(source_line, row, count, sem):
        return pltpu.make_async_copy(
            b_in.at[pl.ds(pl.multiple_of(source_line * 128, 128), count * 128)],
            b_rows.at[pl.ds(row * 128, count * 128)], sem,
        )

    b_local(OWN * p, HALO, OWN, b_recv.at[0]).start()

    @pl.when(p > 0)
    def _():
        b_local(OWN * p - HALO, 0, HALO, b_recv.at[1]).start()

    @pl.when(p < n - 1)
    def _():
        b_local(OWN * p + OWN, HALO + OWN, HALO, b_recv.at[2]).start()

    barrier = pltpu.get_barrier_semaphore()

    def greet(i, carry):
        g2, a2 = lax.rem(i, n), lax.rem(a + gx - 1 + i // n, gx)

        @pl.when(jnp.logical_or(g2 != g, a2 != a))
        def _():
            pl.semaphore_signal(barrier, inc=1, device_id=(g2, a2, q), device_id_type=MESH)

        return carry

    lax.fori_loop(0, 3 * n, greet, 0)
    for place in places:
        for k in range(1, gy):
            pl.semaphore_signal(
                barrier, inc=1, device_id=(place[0], place[1], lax.rem(q + k, gy)), device_id_type=MESH
            )
    pl.semaphore_wait(barrier, 3 * n - 1 + 3 * (gy - 1))

    fields = ((v_in, v_rows), (s_in, s_rows))
    planes = pl.ds(depth * g, depth)

    def field_copies(start):
        for other in range(n):
            lo, hi = max(0, OWN * other - HALO), min(local, OWN * other + OWN + HALO)
            row = lo - (OWN * other - HALO)
            target = flip(other)
            for f, (source, place) in enumerate(fields):
                args = (source.at[:, pl.ds(lo, hi - lo), :], place.at[planes, pl.ds(row, hi - lo), :])

                @pl.when(target != g)
                def _():
                    copy = remote(*args, field_send.at[f, other], field_recv.at[f], (target, a, q))
                    if start:
                        copy.start()
                    else:
                        copy.wait_send()

                if start:
                    @pl.when(target == g)
                    def _():
                        pltpu.make_async_copy(*args, field_recv.at[f]).start()

        for f, (source, place) in enumerate(fields):
            ends = (
                (local - HALO, 0, (flip(n - 1), a_right, q), n),
                (0, HALO + OWN, (flip(0), a_left, q), n + 1),
            )
            for line, row, device, sem in ends:
                copy = remote(
                    source.at[:, pl.ds(line, HALO), :], place.at[planes, pl.ds(row, HALO), :],
                    field_send.at[f, sem], field_recv.at[f], device,
                )
                if start:
                    copy.start()
                else:
                    copy.wait_send()

    share = HALO // n

    def b_remote(start):
        for side, line, row, device in (
            (0, local - HALO, 0, (flip(n - 1), a_right, q)), (1, 0, HALO + OWN, (flip(0), a_left, q)),
        ):
            rows = lambda at: pl.ds(pl.multiple_of((at + share * g) * 128, 128), share * 128)
            copy = remote(b_in.at[rows(line)], b_rows.at[rows(row)], b_send.at[side], b_recv.at[1 + side], device)
            if start:
                copy.start()
            else:
                copy.wait_send()

    b_remote(True)
    field_copies(True)

    lane = lax.broadcasted_iota(jnp.int32, (SPAN, 128), 1)
    row = lax.broadcasted_iota(jnp.int32, (SPAN, 128), 0)
    group, xlane = lane // SPAN, lane % SPAN
    line = local * a + OWN * p - HALO + xlane
    inside = jnp.logical_and(line >= 0, line < local * gx)
    low_half, even = group < 2, group % 2 == 0
    group1 = group[:1]
    group8, xlane8, inside8, sub8 = group[:8], xlane[:8], inside[:8], row[:8]
    ends8 = jnp.logical_and(jnp.logical_or(sub8 == 0, sub8 == 7), jnp.logical_and(xlane8 >= HALO, xlane8 < HALO + OWN))
    top8, bottom8 = jnp.logical_and(sub8 == 0, group8 == 0), jnp.logical_and(sub8 == 7, group8 == 3)

    zero8 = jnp.zeros((8, 128), F32)

    def y_sum(cells):
        up = jnp.where(group1 == 0, 0.0, roll(cells[SPAN - 1 :], SPAN))
        down = jnp.where(group1 == 3, 0.0, roll(cells[:1], -SPAN))
        return cells + jnp.where(row == 0, up, roll(cells, 1, 0)) + jnp.where(row == SPAN - 1, down, roll(cells, -1, 0))

    def box(cells):
        return y_sum(cells + roll(cells, 1) + roll(cells, -1))

    def product(residual, slot):
        res[slot] = residual
        acc = blocks[0] * res[slot, :1, :]
        for j in range(1, SPAN):
            acc = acc + blocks[j] * res[slot, j : j + 1, :]
        rows = [acc[SPAN * i : SPAN * (i + 1)] for i in range(4)]
        parts = []
        for k in range(4):
            part = rows[-k % 4]
            for i in range(1, 4):
                part = jnp.where(group == i, rows[(i - k) % 4], part)
            parts.append(part)
        return parts

    def summed(parts, shifts, at=slice(None)):
        total = None
        for k in range(4):
            for shift in shifts:
                term = roll(parts[k][at], shift - SPAN * k)
                total = term if total is None else total + term
        return total

    def plain(parts, at=slice(None)):
        return summed(parts, (0,), at)

    def apply(residual):
        return plain(product(residual, 7))

    def boxed(parts, slot):
        up = summed(parts, (SPAN - 1, SPAN, SPAN + 1), slice(SPAN - 8, SPAN))
        down = summed(parts, (-SPAN - 1, -SPAN, -SPAN + 1), slice(0, 8))
        pad[slot, :8, :] = jnp.where(group8 == 0, 0.0, up)
        pad[slot, 8 : SPAN + 8, :] = summed(parts, (-1, 0, 1))
        pad[slot, SPAN + 8 :, :] = jnp.where(group8 == 3, 0.0, down)
        return pad[slot, 7 : SPAN + 7, :] + pad[slot, 8 : SPAN + 8, :] + pad[slot, 9 : SPAN + 9, :]

    def turn(x, carry):
        rows = pl.ds(pl.multiple_of(x * 128, 128), 128)
        b_rows[rows, :] = b_rows[rows, :].T
        return carry

    b_local(0, HALO, OWN, b_recv.at[0]).wait()
    lax.fori_loop(HALO, HALO + OWN, turn, 0, unroll=4)
    b_local(0, 0, HALO, b_recv.at[1]).wait()
    lax.fori_loop(0, HALO, turn, 0, unroll=4)
    b_local(0, HALO + OWN, HALO, b_recv.at[2]).wait()
    lax.fori_loop(HALO + OWN, SPAN, turn, 0, unroll=4)

    def gather(j, carry):
        parts = [b_rows[pl.ds(SPAN * jg + j, SPAN, stride=128), :] for jg in range(4)]
        blocks[j] = jnp.where(inside[:1], jnp.concatenate(parts, axis=0).T, 0.0)
        return carry

    lax.fori_loop(0, SPAN, gather, 0, unroll=4)

    columns, cells = [], []
    for slot, at in ((0, 0), (SPAN - 1, 3)):
        column = jnp.zeros((SPAN, 128), F32)
        for i in range(4):
            column = jnp.where(group == i, roll(blocks[slot, SPAN * i : SPAN * (i + 1), :], SPAN * (i - at)), column)
        columns.append(jnp.where(inside, column, 0.0))
        cells.append(y_sum(columns[-1]))
    resp[6], resp[7] = columns
    for j in range(SPAN):
        rows2[0, j : j + 1, :] = blocks[j, :1, :]
        rows2[1, j : j + 1, :] = blocks[j, 127:, :]
    for e in range(2):
        for d in range(3):
            imp[3 * e + d] = roll(cells[e], -(d - 1))

    def respond(i, carry):
        raw[i] = apply(imp[i])
        resp[i] = y_sum(raw[i])
        return carry

    lax.fori_loop(0, 6, respond, 0)

    def spread(value):
        return (value + roll(value, 32)) + (roll(value, 64) + roll(value, 96))

    def pair(values):
        return jnp.where(sub8 == 0, spread(values[0]), spread(values[1]))

    def dots(value):
        return pair([jnp.sum(rows2[e] * value, axis=0, keepdims=True) for e in range(2)])

    def packed(pairs):
        tile = None
        for m in range(0, len(pairs), 4):
            part = jnp.zeros((8, 128), F32)
            for k, value in enumerate(pairs[m : m + 4]):
                part = jnp.where(group8 == k, value, part)
            part = roll(jnp.where(ends8, part, 0.0), m // 2, 0)
            tile = part if tile is None else tile + part
        return tile

    def edge_pair(top, bottom, k):
        return jnp.where(sub8 == 0, roll(top, SPAN * k), roll(bottom, SPAN * (k - 3)))

    first_pairs = [
        pair([jnp.where(group1 == 0, rows2[e, :1, :], 0.0) for e in range(2)]),
        pair([jnp.where(group1 == 3, rows2[e, SPAN - 1 :, :], 0.0) for e in range(2)]),
    ]
    coef[0] = packed([zero8] * 4 + first_pairs)
    later_pairs = [dots(roll(cells[f], -d)) for f in range(2) for d in range(-1, 2)]
    for f in range(2):
        for d in range(-2, 3):
            total = None
            for near in range(-1, 2):
                far = d - near
                if abs(far) <= 1:
                    term = roll(resp[3 * f + far + 1], -near)
                    total = term if total is None else total + term
            wide[5 * f + d + 2] = total
            later_pairs.append(dots(total))
    t_send[0] = packed(later_pairs)

    for f, (place, rows_ref) in enumerate(((old, v_rows), (src, s_rows))):
        pltpu.make_async_copy(rows_ref, rows_ref, field_recv.at[f]).wait()
        for w in range(NZ // 4):
            turned = rows_ref[4 * w : 4 * w + 4].reshape(128, 128).T
            for k in range(4):
                tile = jnp.zeros((SPAN, 128), F32)
                for i in range(4):
                    tile = jnp.where(group == i, roll(turned[SPAN * i : SPAN * (i + 1)], SPAN * (i - k)), tile)
                place[4 * w + k] = jnp.where(inside, tile, 0.0)
    zero_tile = jnp.zeros((SPAN, 128), F32)
    old[NZ] = zero_tile
    old[2 * NZ + 1] = zero_tile
    e_old[NZ] = jnp.zeros((8, 128), F32)
    e_old[2 * NZ + 1] = jnp.zeros((8, 128), F32)
    t_send[1] = packed([edge_pair(old[z, :8, :], old[z, SPAN - 8 :, :], z % 4) for z in range(NZ)])

    def edge_copies(source, target, send, recv, start):
        for k in sorted(range(gy), key=lambda k: -min(k, gy - k)):
            for x in (0, 2, 1):
                place = places[x]
                if x == 1 and k == 0:
                    if start:
                        pltpu.make_async_copy(source, target.at[1, q], recv).start()
                    continue
                copy = remote(
                    source, target.at[2 - x, q], send.at[3 * k + x], recv, (place[0], place[1], lax.rem(q + k, gy))
                )
                if start:
                    copy.start()
                else:
                    copy.wait_send()

    edge_copies(t_send, t_recv, t_ssem, t_rsem, True)

    def unpacked(ref, at=None):
        tiles = []
        for k in range(gy):
            sides = [ref[x, k] if at is None else ref[x, k, at] for x in range(3)]
            tiles.append(jnp.where(
                xlane8 < HALO, roll(sides[0], -OWN), jnp.where(xlane8 >= HALO + OWN, roll(sides[2], OWN), sides[1])
            ))
        whole = []
        for k in range(4):
            tile = jnp.zeros((8, 128), F32)
            for b in range(gy):
                tile = jnp.where(group8 == b, roll(tiles[b], SPAN * (b - k)), tile)
            whole.append(jnp.where(inside8, tile, 0.0))
        return lambda i: roll(whole[i % 4], -2 * (i // 4), 0)

    def halo_copy(window, side, start):
        device = places[2 * side]
        device = (device[0], device[1], q)
        at = STEPS * window

        @pl.when(window < 4)
        def _():
            copy = remote(
                fresh.at[pl.ds(at, STEPS)], halo.at[window, 1 - side],
                u_ssem.at[window, side], u_rsem.at[window, 1 - side], device,
            )
            if start:
                copy.start()
            else:
                copy.wait_send()

        @pl.when(window >= 4)
        def _():
            copy = remote(
                fresh.at[at + STEPS - 1], halo.at[window, 1 - side, STEPS - 1],
                u_ssem.at[window, side], u_rsem.at[window, 1 - side], device,
            )
            if start:
                copy.start()
            else:
                copy.wait_send()

    def halo_wait(window):
        @pl.when(window < 4)
        def _():
            for side in range(2):
                ref = halo.at[window, side]
                pltpu.make_async_copy(ref, ref, u_rsem.at[window, side]).wait()

        @pl.when(window >= 4)
        def _():
            for side in range(2):
                ref = halo.at[window, side, STEPS - 1]
                pltpu.make_async_copy(ref, ref, u_rsem.at[window, side]).wait()

    def out_copy(z, start):
        owner = z // depth
        source = out_rows.at[z]
        target = out.at[lax.rem(z, depth), pl.ds(pl.multiple_of(OWN * p, OWN), OWN), :]

        @pl.when(owner != g)
        def _():
            copy = remote(source, target, o_ssem.at[z], o_rsem, (owner, a, q))
            if start:
                copy.start()
            else:
                copy.wait_send()

        if start:
            @pl.when(owner == g)
            def _():
                pltpu.make_async_copy(source, target, o_rsem).start()

    def window_step(window, carry):
        backward = window // 4
        m0 = STEPS * (window - 4 * backward)
        at = (NZ + 1) * backward + m0
        t0 = STEPS * window
        opening = m0 == 0

        def source_plane(m):
            return src[m + backward * (NZ - 1 - 2 * m)]

        guesses = []
        around = None
        for t in range(STEPS - 1):
            cell = old[at + t]
            near = cell + old[at + t + 1]
            residual = source_plane(m0 + t) - 27.0 * cell + box(near if t == 0 else near + old[at + t - 1])
            residual = residual + (jnp.where(opening, 0.0, last_box[...]) if t == 0 else boxed(around, t))
            ends = (slice(0, 8), slice(SPAN - 8, SPAN))
            if t < STEPS - 2:
                around = product(residual, t)
                guesses.append(edge_pair(*(cell[end] + plain(around, end) for end in ends), t))
            else:
                guesses.append(edge_pair(*(cell[end] for end in ends), t) + dots(residual))
        done = []
        for k in range(STEPS):
            tile = fresh.at[jnp.maximum(t0 - STEPS + k, 0)]
            done.append(edge_pair(tile[:8, :], tile[SPAN - 8 :, :], k))
        first = packed(guesses + [jnp.where(window == 0, 0.0, done[3])])
        rest = packed([zero8] * 4 + [done[k] for k in range(3)])
        e_send[window] = first + jnp.where(window == 0, coef[0], rest)
        edge_copies(e_send.at[window], e_recv.at[window], e_ssem.at[window], e_rsem.at[window], True)

        @pl.when(window > 0)
        def _():
            halo_wait(window - 1)

        def merged(t):
            mid = fresh[jnp.maximum(t0 - STEPS + t, 0)]
            w = jnp.maximum(window - 1, 0)
            tile = jnp.where(
                xlane < HALO, roll(halo[w, 0, t], -OWN),
                jnp.where(xlane >= HALO + OWN, roll(halo[w, 1, t], OWN), mid),
            )
            return jnp.where(inside, tile, 0.0)

        @pl.when(jnp.logical_and(window > 0, window <= 4))
        def _():
            for t in range(STEPS):
                old[2 * NZ - jnp.maximum(t0 - STEPS + t, 0)] = merged(t)

        @pl.when(opening)
        def _():
            start[...] = zero_tile

        @pl.when(jnp.logical_not(opening))
        def _():
            start[...] = merged(STEPS - 1)

        for t in range(STEPS):
            cell = old[at + t]
            before = start[...] if t == 0 else free[t - 1] if t < 3 else old[at + t - 1]
            value = source_plane(m0 + t) - 27.0 * cell + box(cell + old[at + t + 1] + before)
            free[t] = cell + plain(product(value, 2 + t)) if t < 2 else value

        @pl.when(window == 0)
        def _():
            pltpu.make_async_copy(t_recv, t_recv, t_rsem).wait()
            item = unpacked(t_recv, 0)
            for r in range(16):
                coef[2 + r] = item(r)
            item = unpacked(t_recv, 1)
            for r in range(NZ):
                e_old[r] = item(r)

        arrived = e_recv.at[window]
        pltpu.make_async_copy(arrived, arrived, e_rsem.at[window]).wait()
        item = unpacked(arrived)

        @pl.when(window == 0)
        def _():
            for r in range(2):
                coef[r] = item(4 + r)

        @pl.when(jnp.logical_and(window > 0, window <= 4))
        def _():
            for t in range(STEPS):
                e_old[2 * NZ - jnp.maximum(t0 - STEPS + t, 0)] = item(3 if t == 3 else 4 + t)

        before = jnp.where(opening, 0.0, item(3))
        gives, gains = [], []
        around = None
        for t in range(STEPS):
            total = before + (e_old[at + t] + e_old[at + t + 1])
            reach = max(0, STEPS - 2 - t)
            low, high = jnp.broadcast_to(total[7:], (8, 128)), jnp.broadcast_to(total[:1], (8, 128))
            from_low = {c: roll(low, SPAN - c) for c in range(-reach - 1, reach + 2)}
            from_high = {c: roll(high, -SPAN - c) for c in range(-reach - 1, reach + 2)}
            give = {}
            for d in range(-reach, reach + 1):
                give[0, d] = jnp.where(group8 > 0, from_low[d - 1] + from_low[d] + from_low[d + 1], 0.0)
                give[1, d] = jnp.where(group8 < gy - 1, from_high[d - 1] + from_high[d] + from_high[d + 1], 0.0)
            gives.append(give)
            if t < 2:
                gains.append({
                    key: jnp.concatenate([spread(jnp.where(group8 == q, give[key], 0.0))] * 4, axis=0) for key in give
                })
                now = free[t] + (resp[6] * gains[t][0, 0] + resp[7] * gains[t][1, 0])
                if t == 1:
                    for f in range(2):
                        for d in range(-1, 2):
                            now = now + raw[3 * f + d + 1] * gains[0][f, d]
            else:
                mine = (
                    jnp.where(top8, pltpu.roll(give[0, 0], lax.rem(128 - SPAN * q, 128), 1), 0.0),
                    jnp.where(bottom8, pltpu.roll(give[1, 0], SPAN * (3 - q), 1), 0.0),
                )
                if t == 2:
                    residual = free[2]
                    for f in range(2):
                        for d in range(-1, 2):
                            residual = residual + imp[3 * f + d + 1] * gains[1][f, d]
                        for d in range(-2, 3):
                            residual = residual + wide[5 * f + d + 2] * gains[0][f, d]
                else:
                    residual = free[t] + boxed(around, 1 + t)
                residual = jnp.concatenate(
                    [residual[:8] + mine[0], residual[8 : SPAN - 8], residual[SPAN - 8 :] + mine[1]], axis=0
                )
                around = product(residual, 2 + t)
                now = old[at + t] + plain(around)
            fresh[t0 + t] = now
            if t < STEPS - 1:
                value = item(t)
                for s in range(t + 1):
                    lag = t - s
                    for f in range(2):
                        for d in range(-lag, lag + 1):
                            r = (0, 2, 8)[lag] + f * (2 * lag + 1) + d + lag
                            value = value + coef[r] * gives[s][f, d]
                before = jnp.where(inside8, value, 0.0)

        last_box[...] = box(old[at + STEPS - 1]) + boxed(around, 4)

        @pl.when(backward == 0)
        def _():
            for t in range(STEPS):
                old[2 * NZ - jnp.minimum(t0 + t, NZ - 1)] = fresh[t0 + t]

        @pl.when(window < 7)
        def _():
            halo_copy(window, 0, True)
            halo_copy(window, 1, True)

        @pl.when(backward == 1)
        def _():
            tiles = [fresh[t0 + k] for k in range(4)]
            parts = []
            for i in range(4):
                part = tiles[0] if i == 0 else roll(tiles[0], -SPAN * i)
                for k in range(1, 4):
                    part = jnp.where(group == k, roll(tiles[k], SPAN * (k - i)), part)
                parts.append(part)
            lines = jnp.concatenate(parts, axis=0).T
            for k in range(4):
                z = jnp.maximum(2 * NZ - 1 - t0 - k, 0)
                out_rows[z] = lines[SPAN * k + HALO : SPAN * k + HALO + OWN]
                out_copy(z, True)

        return carry

    lax.fori_loop(0, 8, window_step, 0)

    field_copies(False)
    b_remote(False)
    edge_copies(t_send, t_recv, t_ssem, t_rsem, False)

    def drain(window, carry):
        edge_copies(e_send.at[window], e_recv.at[window], e_ssem.at[window], e_rsem.at[window], False)

        @pl.when(window < 7)
        def _():
            halo_copy(window, 0, False)
            halo_copy(window, 1, False)

        return carry

    lax.fori_loop(0, 8, drain, 0)

    def drain_out(z, carry):
        out_copy(z, False)
        return carry

    lax.fori_loop(0, NZ, drain_out, 0)
    pltpu.make_async_copy(out, out, o_rsem).wait()


def solution(mesh):
    n, gx, gy = mesh.shape["gz"], mesh.shape["gx"], mesh.shape["gy"]

    def body(initial_field, source_term, block_inverse):
        depth, local, width = initial_field.shape
        vmem = lambda *shape: pltpu.VMEM(shape, F32)
        dma = pltpu.SemaphoreType.DMA
        return pl.pallas_call(
            functools.partial(kernel, n, gx, gy, depth),
            out_shape=jax.ShapeDtypeStruct(initial_field.shape, F32),
            in_specs=[pl.BlockSpec(memory_space=pltpu.HBM)] * 3,
            out_specs=pl.BlockSpec(memory_space=pltpu.VMEM),
            scratch_shapes=[
                vmem(NZ, SPAN, 128), vmem(NZ, SPAN, 128), vmem(SPAN * 128, 128), vmem(SPAN, 128, 128),
                vmem(2 * NZ + 2, SPAN, 128), vmem(NZ, SPAN, 128), vmem(2 * NZ, SPAN, 128),
                vmem(8, 2, STEPS, SPAN, 128),
                vmem(STEPS, SPAN, 128), vmem(8, SPAN, 128), vmem(8, SPAN + 16, 128), vmem(SPAN, 128), vmem(SPAN, 128),
                vmem(8, 8, 128), vmem(8, 3, gy, 8, 128), vmem(2, 8, 128), vmem(3, gy, 2, 8, 128),
                vmem(2 * NZ + 2, 8, 128), vmem(18, 8, 128), vmem(2, SPAN, 128),
                vmem(6, SPAN, 128), vmem(6, SPAN, 128), vmem(10, SPAN, 128), vmem(8, SPAN, 128), vmem(NZ, OWN, 128),
                dma((2, n + 2)), dma((2,)), dma((3,)), dma((2,)),
                dma((8, 3 * gy)), dma((8,)), dma((3 * gy,)), dma,
                dma((8, 2)), dma((8, 2)), dma((NZ,)), dma,
            ],
            compiler_params=pltpu.CompilerParams(
                collective_id=0, has_side_effects=True, vmem_limit_bytes=60 * 1024 * 1024
            ),
        )(initial_field, source_term, block_inverse.reshape(local * width, width))

    return jax.shard_map(
        body, mesh=mesh,
        in_specs=(P("gz", "gx", "gy"), P("gz", "gx", "gy"), P("gx", "gy", None)),
        out_specs=P("gz", "gx", "gy"), check_vma=False,
    )
```

```python
import functools

import jax
import jax.numpy as jnp
from jax import lax
from jax.experimental import pallas as pl
from jax.experimental.pallas import tpu as pltpu
from jax.sharding import PartitionSpec as P

MESH = pl.DeviceIdType.MESH
F32 = jnp.float32
OWN = 16
HALO = 8
SPAN = 32
STEPS = 4
NZ = 16


def roll(value, shift, axis=1):
    size = value.shape[axis]
    shift = shift % size
    return value if shift == 0 else pltpu.roll(value, shift, axis)


def kernel(
    n, gx, gy, depth,
    v_in, s_in, b_in, out,
    v_rows, s_rows, b_rows, blocks, old, src, fresh, halo,
    free, res, pad, last_box, start, e_send, e_recv, t_send, t_recv, e_old, coef, rows2, imp, raw, wide, resp, out_rows,
    field_send, field_recv, b_recv, b_send, e_ssem, e_rsem, t_ssem, t_rsem, u_ssem, u_rsem, o_ssem, o_rsem,
):
    g, a, q = lax.axis_index("gz"), lax.axis_index("gx"), lax.axis_index("gy")
    par = lax.rem(a, 2)
    local = OWN * n

    def flip(p):
        return p + par * (n - 1 - 2 * p)

    p = flip(g)
    a_left, a_right = lax.rem(a + gx - 1, gx), lax.rem(a + 1, gx)
    step_up = 1 - 2 * par
    first, last = p == 0, p == n - 1
    left = (jnp.where(first, g, g - step_up), jnp.where(first, a_left, a))
    right = (jnp.where(last, g, g + step_up), jnp.where(last, a_right, a))
    places = (left, (g, a), right)

    def remote(source, target, send, recv, device):
        return pltpu.make_async_remote_copy(
            src_ref=source, dst_ref=target, send_sem=send, recv_sem=recv, device_id=device, device_id_type=MESH
        )

    def b_local(source_line, row, count, sem):
        return pltpu.make_async_copy(
            b_in.at[pl.ds(pl.multiple_of(source_line * 128, 128), count * 128)],
            b_rows.at[pl.ds(row * 128, count * 128)], sem,
        )

    b_local(OWN * p, HALO, OWN, b_recv.at[0]).start()

    @pl.when(p > 0)
    def _():
        b_local(OWN * p - HALO, 0, HALO, b_recv.at[1]).start()

    @pl.when(p < n - 1)
    def _():
        b_local(OWN * p + OWN, HALO + OWN, HALO, b_recv.at[2]).start()

    barrier = pltpu.get_barrier_semaphore()

    def greet(i, carry):
        g2, a2 = lax.rem(i, n), lax.rem(a + gx - 1 + i // n, gx)

        @pl.when(jnp.logical_or(g2 != g, a2 != a))
        def _():
            pl.semaphore_signal(barrier, inc=1, device_id=(g2, a2, q), device_id_type=MESH)

        return carry

    lax.fori_loop(0, 3 * n, greet, 0)
    for place in places:
        for k in range(1, gy):
            pl.semaphore_signal(
                barrier, inc=1, device_id=(place[0], place[1], lax.rem(q + k, gy)), device_id_type=MESH
            )
    pl.semaphore_wait(barrier, 3 * n - 1 + 3 * (gy - 1))

    fields = ((v_in, v_rows), (s_in, s_rows))
    planes = pl.ds(depth * g, depth)

    def field_copies(start):
        for other in range(n):
            lo, hi = max(0, OWN * other - HALO), min(local, OWN * other + OWN + HALO)
            row = lo - (OWN * other - HALO)
            target = flip(other)
            for f, (source, place) in enumerate(fields):
                args = (source.at[:, pl.ds(lo, hi - lo), :], place.at[planes, pl.ds(row, hi - lo), :])

                @pl.when(target != g)
                def _():
                    copy = remote(*args, field_send.at[f, other], field_recv.at[f], (target, a, q))
                    if start:
                        copy.start()
                    else:
                        copy.wait_send()

                if start:
                    @pl.when(target == g)
                    def _():
                        pltpu.make_async_copy(*args, field_recv.at[f]).start()

        for f, (source, place) in enumerate(fields):
            ends = (
                (local - HALO, 0, (flip(n - 1), a_right, q), n),
                (0, HALO + OWN, (flip(0), a_left, q), n + 1),
            )
            for line, row, device, sem in ends:
                copy = remote(
                    source.at[:, pl.ds(line, HALO), :], place.at[planes, pl.ds(row, HALO), :],
                    field_send.at[f, sem], field_recv.at[f], device,
                )
                if start:
                    copy.start()
                else:
                    copy.wait_send()

    share = HALO // n

    def b_remote(start):
        for side, line, row, device in (
            (0, local - HALO, 0, (flip(n - 1), a_right, q)), (1, 0, HALO + OWN, (flip(0), a_left, q)),
        ):
            rows = lambda at: pl.ds(pl.multiple_of((at + share * g) * 128, 128), share * 128)
            copy = remote(b_in.at[rows(line)], b_rows.at[rows(row)], b_send.at[side], b_recv.at[1 + side], device)
            if start:
                copy.start()
            else:
                copy.wait_send()

    b_remote(True)
    field_copies(True)

    lane = lax.broadcasted_iota(jnp.int32, (SPAN, 128), 1)
    row = lax.broadcasted_iota(jnp.int32, (SPAN, 128), 0)
    group, xlane = lane // SPAN, lane % SPAN
    line = local * a + OWN * p - HALO + xlane
    inside = jnp.logical_and(line >= 0, line < local * gx)
    low_half, even = group < 2, group % 2 == 0
    group1 = group[:1]
    group8, xlane8, inside8, sub8 = group[:8], xlane[:8], inside[:8], row[:8]
    ends8 = jnp.logical_and(sub8 < 2, jnp.logical_and(xlane8 >= HALO, xlane8 < HALO + OWN))
    top8, bottom8 = jnp.logical_and(sub8 == 0, group8 == 0), jnp.logical_and(sub8 == 7, group8 == 3)

    zero8 = jnp.zeros((8, 128), F32)

    def y_sum(cells):
        up = jnp.where(group1 == 0, 0.0, roll(cells[SPAN - 1 :], SPAN))
        down = jnp.where(group1 == 3, 0.0, roll(cells[:1], -SPAN))
        return cells + jnp.where(row == 0, up, roll(cells, 1, 0)) + jnp.where(row == SPAN - 1, down, roll(cells, -1, 0))

    def box(cells):
        return y_sum(cells + roll(cells, 1) + roll(cells, -1))

    def product(residual, slot):
        res[slot] = residual
        acc = blocks[0] * res[slot, :1, :]
        for j in range(1, SPAN):
            acc = acc + blocks[j] * res[slot, j : j + 1, :]
        rows = [acc[SPAN * i : SPAN * (i + 1)] for i in range(4)]
        parts = []
        for k in range(4):
            part = rows[-k % 4]
            for i in range(1, 4):
                part = jnp.where(group == i, rows[(i - k) % 4], part)
            parts.append(part)
        return parts

    def summed(parts, shifts, at=slice(None)):
        total = None
        for k in range(4):
            for shift in shifts:
                term = roll(parts[k][at], shift - SPAN * k)
                total = term if total is None else total + term
        return total

    def plain(parts, at=slice(None)):
        return summed(parts, (0,), at)

    def apply(residual):
        return plain(product(residual, 7))

    def boxed(parts, slot):
        up = summed(parts, (SPAN - 1, SPAN, SPAN + 1), slice(SPAN - 8, SPAN))
        down = summed(parts, (-SPAN - 1, -SPAN, -SPAN + 1), slice(0, 8))
        pad[slot, :8, :] = jnp.where(group8 == 0, 0.0, up)
        pad[slot, 8 : SPAN + 8, :] = summed(parts, (-1, 0, 1))
        pad[slot, SPAN + 8 :, :] = jnp.where(group8 == 3, 0.0, down)
        return pad[slot, 7 : SPAN + 7, :] + pad[slot, 8 : SPAN + 8, :] + pad[slot, 9 : SPAN + 9, :]

    def turn(x, carry):
        rows = pl.ds(pl.multiple_of(x * 128, 128), 128)
        b_rows[rows, :] = b_rows[rows, :].T
        return carry

    b_local(0, HALO, OWN, b_recv.at[0]).wait()
    lax.fori_loop(HALO, HALO + OWN, turn, 0, unroll=4)
    b_local(0, 0, HALO, b_recv.at[1]).wait()
    lax.fori_loop(0, HALO, turn, 0, unroll=4)
    b_local(0, HALO + OWN, HALO, b_recv.at[2]).wait()
    lax.fori_loop(HALO + OWN, SPAN, turn, 0, unroll=4)

    def gather(j, carry):
        parts = [b_rows[pl.ds(SPAN * jg + j, SPAN, stride=128), :] for jg in range(4)]
        blocks[j] = jnp.where(inside[:1], jnp.concatenate(parts, axis=0).T, 0.0)
        return carry

    lax.fori_loop(0, SPAN, gather, 0, unroll=4)

    columns, cells = [], []
    for slot, at in ((0, 0), (SPAN - 1, 3)):
        column = jnp.zeros((SPAN, 128), F32)
        for i in range(4):
            column = jnp.where(group == i, roll(blocks[slot, SPAN * i : SPAN * (i + 1), :], SPAN * (i - at)), column)
        columns.append(jnp.where(inside, column, 0.0))
        cells.append(y_sum(columns[-1]))
    resp[6], resp[7] = columns
    for j in range(SPAN):
        rows2[0, j : j + 1, :] = blocks[j, :1, :]
        rows2[1, j : j + 1, :] = blocks[j, 127:, :]
    for e in range(2):
        for d in range(3):
            imp[3 * e + d] = roll(cells[e], -(d - 1))

    def respond(i, carry):
        raw[i] = apply(imp[i])
        resp[i] = y_sum(raw[i])
        return carry

    lax.fori_loop(0, 6, respond, 0)

    def spread(value):
        return (value + roll(value, 32)) + (roll(value, 64) + roll(value, 96))

    def pair(values):
        return jnp.where(sub8 == 0, spread(values[0]), spread(values[1]))

    def dots(value):
        return pair([jnp.sum(rows2[e] * value, axis=0, keepdims=True) for e in range(2)])

    def packed(pairs):
        tile = None
        for m in range(0, len(pairs), 4):
            part = jnp.zeros((8, 128), F32)
            for k, value in enumerate(pairs[m : m + 4]):
                part = jnp.where(group8 == k, value, part)
            part = roll(jnp.where(ends8, part, 0.0), m // 2, 0)
            tile = part if tile is None else tile + part
        return tile

    def edge_pair(top, bottom, k):
        return jnp.where(sub8 == 0, roll(top, SPAN * k), roll(roll(bottom, 2, 0), SPAN * (k - 3)))

    first_pairs = [
        pair([jnp.where(group1 == 0, rows2[e, :1, :], 0.0) for e in range(2)]),
        pair([jnp.where(group1 == 3, rows2[e, SPAN - 1 :, :], 0.0) for e in range(2)]),
    ]
    coef[0] = packed([zero8] * 4 + first_pairs)
    later_pairs = [dots(roll(cells[f], -d)) for f in range(2) for d in range(-1, 2)]
    for f in range(2):
        for d in range(-2, 3):
            total = None
            for near in range(-1, 2):
                far = d - near
                if abs(far) <= 1:
                    term = roll(resp[3 * f + far + 1], -near)
                    total = term if total is None else total + term
            wide[5 * f + d + 2] = total
            later_pairs.append(dots(total))
    t_send[0] = packed(later_pairs)

    for f, (place, rows_ref) in enumerate(((old, v_rows), (src, s_rows))):
        pltpu.make_async_copy(rows_ref, rows_ref, field_recv.at[f]).wait()
        for w in range(NZ // 4):
            turned = rows_ref[4 * w : 4 * w + 4].reshape(128, 128).T
            for k in range(4):
                tile = jnp.zeros((SPAN, 128), F32)
                for i in range(4):
                    tile = jnp.where(group == i, roll(turned[SPAN * i : SPAN * (i + 1)], SPAN * (i - k)), tile)
                place[4 * w + k] = jnp.where(inside, tile, 0.0)
    zero_tile = jnp.zeros((SPAN, 128), F32)
    old[NZ] = zero_tile
    old[2 * NZ + 1] = zero_tile
    e_old[NZ] = jnp.zeros((8, 128), F32)
    e_old[2 * NZ + 1] = jnp.zeros((8, 128), F32)
    t_send[1] = packed([edge_pair(old[z, :8, :], old[z, SPAN - 8 :, :], z % 4) for z in range(NZ)])

    def edge_copies(source, target, send, recv, start):
        for k in sorted(range(gy), key=lambda k: -min(k, gy - k)):
            for x in (0, 2, 1):
                place = places[x]
                if x == 1 and k == 0:
                    if start:
                        pltpu.make_async_copy(source, target.at[1, q], recv).start()
                    continue
                copy = remote(
                    source, target.at[2 - x, q], send.at[3 * k + x], recv, (place[0], place[1], lax.rem(q + k, gy))
                )
                if start:
                    copy.start()
                else:
                    copy.wait_send()

    edge_copies(t_send, t_recv, t_ssem, t_rsem, True)

    def unpacked(ref, at=None):
        tiles = []
        for k in range(gy):
            sides = [ref[x, k] if at is None else ref[x, k, at] for x in range(3)]
            tiles.append(jnp.where(
                xlane8 < HALO, roll(sides[0], -OWN), jnp.where(xlane8 >= HALO + OWN, roll(sides[2], OWN), sides[1])
            ))
        whole = []
        for k in range(4):
            tile = jnp.zeros((8, 128), F32)
            for b in range(gy):
                tile = jnp.where(group8 == b, roll(tiles[b], SPAN * (b - k)), tile)
            whole.append(jnp.where(inside8, tile, 0.0))
        return lambda i: roll(whole[i % 4], -2 * (i // 4), 0)

    def halo_copy(window, side, start):
        device = places[2 * side]
        device = (device[0], device[1], q)
        at = STEPS * window

        @pl.when(window < 4)
        def _():
            copy = remote(
                fresh.at[pl.ds(at, STEPS)], halo.at[window, 1 - side],
                u_ssem.at[window, side], u_rsem.at[window, 1 - side], device,
            )
            if start:
                copy.start()
            else:
                copy.wait_send()

        @pl.when(window >= 4)
        def _():
            copy = remote(
                fresh.at[at + STEPS - 1], halo.at[window, 1 - side, STEPS - 1],
                u_ssem.at[window, side], u_rsem.at[window, 1 - side], device,
            )
            if start:
                copy.start()
            else:
                copy.wait_send()

    def halo_wait(window):
        @pl.when(window < 4)
        def _():
            for side in range(2):
                ref = halo.at[window, side]
                pltpu.make_async_copy(ref, ref, u_rsem.at[window, side]).wait()

        @pl.when(window >= 4)
        def _():
            for side in range(2):
                ref = halo.at[window, side, STEPS - 1]
                pltpu.make_async_copy(ref, ref, u_rsem.at[window, side]).wait()

    def out_copy(z, start):
        owner = z // depth
        source = out_rows.at[z]
        target = out.at[lax.rem(z, depth), pl.ds(pl.multiple_of(OWN * p, OWN), OWN), :]

        @pl.when(owner != g)
        def _():
            copy = remote(source, target, o_ssem.at[z], o_rsem, (owner, a, q))
            if start:
                copy.start()
            else:
                copy.wait_send()

        if start:
            @pl.when(owner == g)
            def _():
                pltpu.make_async_copy(source, target, o_rsem).start()

    def deliver(window):
        at = STEPS * window
        tiles = [fresh[at + k] for k in range(4)]
        parts = []
        for i in range(4):
            part = roll(tiles[0], -SPAN * i)
            for k in range(1, 4):
                part = jnp.where(group == k, roll(tiles[k], SPAN * (k - i)), part)
            parts.append(part)
        lines = jnp.concatenate(parts, axis=0).T
        for k in range(4):
            z = 2 * NZ - 1 - at - k
            out_rows[z] = lines[SPAN * k + HALO : SPAN * k + HALO + OWN]
            out_copy(z, True)

    def window_step(window, carry):
        backward = window // 4
        m0 = STEPS * (window - 4 * backward)
        at = (NZ + 1) * backward + m0
        t0 = STEPS * window
        opening = m0 == 0

        def source_plane(m):
            return src[m + backward * (NZ - 1 - 2 * m)]

        guesses = []
        around = None
        for t in range(STEPS - 1):
            cell = old[at + t]
            near = cell + old[at + t + 1]
            residual = source_plane(m0 + t) - 27.0 * cell + box(near if t == 0 else near + old[at + t - 1])
            residual = residual + (jnp.where(opening, 0.0, last_box[...]) if t == 0 else boxed(around, t))
            ends = (slice(0, 8), slice(SPAN - 8, SPAN))
            if t < STEPS - 2:
                around = product(residual, t)
                change = jnp.where(
                    sub8 == 0, summed(around, (SPAN * t,), ends[0]),
                    roll(summed(around, (SPAN * (t - 3),), ends[1]), 2, 0),
                )
                guesses.append(edge_pair(*(cell[end] for end in ends), t) + change)
            else:
                guesses.append(edge_pair(*(cell[end] for end in ends), t) + dots(residual))
        done = []
        for k in range(STEPS):
            tile = fresh.at[jnp.maximum(t0 - STEPS + k, 0)]
            done.append(edge_pair(tile[:8, :], tile[SPAN - 8 :, :], k))
        first = packed(guesses + [jnp.where(window == 0, 0.0, done[3])])
        rest = packed([zero8] * 4 + [done[k] for k in range(3)])
        e_send[window] = first + jnp.where(window == 0, coef[0], rest)
        edge_copies(e_send.at[window, :4], e_recv.at[window, :, :, :4], e_ssem.at[window], e_rsem.at[window], True)

        @pl.when(window > 4)
        def _():
            deliver(window - 1)

        @pl.when(window > 0)
        def _():
            halo_wait(window - 1)

        def merged(t):
            mid = fresh[jnp.maximum(t0 - STEPS + t, 0)]
            w = jnp.maximum(window - 1, 0)
            tile = jnp.where(
                xlane < HALO, roll(halo[w, 0, t], -OWN),
                jnp.where(xlane >= HALO + OWN, roll(halo[w, 1, t], OWN), mid),
            )
            return jnp.where(inside, tile, 0.0)

        @pl.when(jnp.logical_and(window > 0, window <= 4))
        def _():
            for t in range(STEPS):
                old[2 * NZ - jnp.maximum(t0 - STEPS + t, 0)] = merged(t)

        @pl.when(opening)
        def _():
            start[...] = zero_tile

        @pl.when(jnp.logical_not(opening))
        def _():
            start[...] = merged(STEPS - 1)

        for t in range(STEPS):
            cell = old[at + t]
            before = start[...] if t == 0 else free[t - 1] if t < 3 else old[at + t - 1]
            value = source_plane(m0 + t) - 27.0 * cell + box(cell + old[at + t + 1] + before)
            free[t] = cell + plain(product(value, 2 + t)) if t < 2 else value

        @pl.when(window == 0)
        def _():
            pltpu.make_async_copy(t_recv, t_recv, t_rsem).wait()
            item = unpacked(t_recv, 0)
            for r in range(16):
                coef[2 + r] = item(r)
            item = unpacked(t_recv, 1)
            for r in range(NZ):
                e_old[r] = item(r)

        arrived, landed = e_recv.at[window], e_recv.at[window, :, :, :4]
        pltpu.make_async_copy(landed, landed, e_rsem.at[window]).wait()
        item = unpacked(arrived)

        for r in range(2):
            coef[r] = jnp.where(window == 0, item(4 + r), coef[r])
        kept = jnp.logical_and(window > 0, window <= 4)
        for t in range(STEPS):
            place = jnp.where(kept, 2 * NZ - (t0 - STEPS + t), 2 * NZ + 2)
            e_old[place] = item(3 if t == 3 else 4 + t)

        before = jnp.where(opening, 0.0, item(3))
        gives, gains, planes_now = [], [], []
        around = None
        for t in range(STEPS):
            total = before + (e_old[at + t] + e_old[at + t + 1])
            reach = max(0, STEPS - 2 - t)
            low, high = jnp.broadcast_to(total[1:2], (8, 128)), jnp.broadcast_to(total[:1], (8, 128))
            from_low = {c: roll(low, SPAN - c) for c in range(-reach - 1, reach + 2)}
            from_high = {c: roll(high, -SPAN - c) for c in range(-reach - 1, reach + 2)}
            give = {}
            for d in range(-reach, reach + 1):
                give[0, d] = jnp.where(group8 > 0, from_low[d - 1] + from_low[d] + from_low[d + 1], 0.0)
                give[1, d] = jnp.where(group8 < gy - 1, from_high[d - 1] + from_high[d] + from_high[d + 1], 0.0)
            gives.append(give)
            if t < 2:
                gains.append({
                    key: jnp.concatenate([spread(jnp.where(group8 == q, give[key], 0.0))] * 4, axis=0) for key in give
                })
                now = free[t] + (resp[6] * gains[t][0, 0] + resp[7] * gains[t][1, 0])
                if t == 1:
                    for f in range(2):
                        for d in range(-1, 2):
                            now = now + raw[3 * f + d + 1] * gains[0][f, d]
            else:
                mine = (
                    jnp.where(top8, pltpu.roll(give[0, 0], lax.rem(128 - SPAN * q, 128), 1), 0.0),
                    jnp.where(bottom8, pltpu.roll(give[1, 0], SPAN * (3 - q), 1), 0.0),
                )
                if t == 2:
                    residual = free[2]
                    for f in range(2):
                        for d in range(-1, 2):
                            residual = residual + imp[3 * f + d + 1] * gains[1][f, d]
                        for d in range(-2, 3):
                            residual = residual + wide[5 * f + d + 2] * gains[0][f, d]
                else:
                    residual = free[t] + boxed(around, 1 + t)
                residual = jnp.concatenate(
                    [residual[:8] + mine[0], residual[8 : SPAN - 8], residual[SPAN - 8 :] + mine[1]], axis=0
                )
                around = product(residual, 2 + t)
                now = old[at + t] + plain(around)
            fresh[t0 + t] = now
            planes_now.append(now)
            if t < STEPS - 1:
                value = item(t)
                for s in range(t + 1):
                    lag = t - s
                    for f in range(2):
                        for d in range(-lag, lag + 1):
                            r = (0, 2, 8)[lag] + f * (2 * lag + 1) + d + lag
                            value = value + coef[r] * gives[s][f, d]
                before = jnp.where(inside8, value, 0.0)

        last_box[...] = box(old[at + STEPS - 1]) + boxed(around, 4)

        for t in range(STEPS):
            old[jnp.where(backward == 0, 2 * NZ - (t0 + t), 2 * NZ + 2)] = planes_now[t]

        @pl.when(window < 7)
        def _():
            halo_copy(window, 0, True)
            halo_copy(window, 1, True)

        return carry

    lax.fori_loop(0, 8, window_step, 0)
    deliver(7)

    field_copies(False)
    b_remote(False)
    edge_copies(t_send, t_recv, t_ssem, t_rsem, False)

    def drain(window, carry):
        edge_copies(e_send.at[window, :4], e_recv.at[window, :, :, :4], e_ssem.at[window], e_rsem.at[window], False)

        @pl.when(window < 7)
        def _():
            halo_copy(window, 0, False)
            halo_copy(window, 1, False)

        return carry

    lax.fori_loop(0, 8, drain, 0)

    def drain_out(z, carry):
        out_copy(z, False)
        return carry

    lax.fori_loop(0, NZ, drain_out, 0)
    pltpu.make_async_copy(out, out, o_rsem).wait()


def solution(mesh):
    n, gx, gy = mesh.shape["gz"], mesh.shape["gx"], mesh.shape["gy"]

    def body(initial_field, source_term, block_inverse):
        depth, local, width = initial_field.shape
        vmem = lambda *shape: pltpu.VMEM(shape, F32)
        dma = pltpu.SemaphoreType.DMA
        return pl.pallas_call(
            functools.partial(kernel, n, gx, gy, depth),
            out_shape=jax.ShapeDtypeStruct(initial_field.shape, F32),
            in_specs=[pl.BlockSpec(memory_space=pltpu.HBM)] * 3,
            out_specs=pl.BlockSpec(memory_space=pltpu.VMEM),
            scratch_shapes=[
                vmem(NZ, SPAN, 128), vmem(NZ, SPAN, 128), vmem(SPAN * 128, 128), vmem(SPAN, 128, 128),
                vmem(2 * NZ + 3, SPAN, 128), vmem(NZ, SPAN, 128), vmem(2 * NZ, SPAN, 128),
                vmem(8, 2, STEPS, SPAN, 128),
                vmem(STEPS, SPAN, 128), vmem(8, SPAN, 128), vmem(8, SPAN + 16, 128), vmem(SPAN, 128), vmem(SPAN, 128),
                vmem(8, 8, 128), vmem(8, 3, gy, 8, 128), vmem(2, 8, 128), vmem(3, gy, 2, 8, 128),
                vmem(2 * NZ + 3, 8, 128), vmem(18, 8, 128), vmem(2, SPAN, 128),
                vmem(6, SPAN, 128), vmem(6, SPAN, 128), vmem(10, SPAN, 128), vmem(8, SPAN, 128), vmem(NZ, OWN, 128),
                dma((2, n + 2)), dma((2,)), dma((3,)), dma((2,)),
                dma((8, 3 * gy)), dma((8,)), dma((3 * gy,)), dma,
                dma((8, 2)), dma((8, 2)), dma((NZ,)), dma,
            ],
            compiler_params=pltpu.CompilerParams(
                collective_id=0, has_side_effects=True, vmem_limit_bytes=60 * 1024 * 1024
            ),
        )(initial_field, source_term, block_inverse.reshape(local * width, width))

    return jax.shard_map(
        body, mesh=mesh,
        in_specs=(P("gz", "gx", "gy"), P("gz", "gx", "gy"), P("gx", "gy", None)),
        out_specs=P("gz", "gx", "gy"), check_vma=False,
    )
```

```python
import functools

import jax
import jax.numpy as jnp
from jax import lax
from jax.experimental import pallas as pl
from jax.experimental.pallas import tpu as pltpu
from jax.sharding import PartitionSpec as P

MESH = pl.DeviceIdType.MESH
F32 = jnp.float32
OWN = 16
HALO = 8
SPAN = 32
STEPS = 4
NZ = 16


def roll(value, shift, axis=1):
    size = value.shape[axis]
    shift = shift % size
    return value if shift == 0 else pltpu.roll(value, shift, axis)


def kernel(
    n, gx, gy, depth,
    v_in, s_in, b_in, out,
    v_rows, s_rows, b_rows, blocks, old, src, fresh, halo,
    free, res, pad, last_box, start, e_send, e_recv, t_send, t_recv, e_old, coef, rows2, imp, raw, wide, resp, out_rows,
    field_send, field_recv, b_recv, b_send, e_ssem, e_rsem, t_ssem, t_rsem, u_ssem, u_rsem, o_ssem, o_rsem, met,
):
    g, a, q = lax.axis_index("gz"), lax.axis_index("gx"), lax.axis_index("gy")
    par = lax.rem(a, 2)
    local = OWN * n

    def flip(p):
        return p + par * (n - 1 - 2 * p)

    p = flip(g)
    a_left, a_right = lax.rem(a + gx - 1, gx), lax.rem(a + 1, gx)
    step_up = 1 - 2 * par
    first, last = p == 0, p == n - 1
    left = (jnp.where(first, g, g - step_up), jnp.where(first, a_left, a))
    right = (jnp.where(last, g, g + step_up), jnp.where(last, a_right, a))
    places = (left, (g, a), right)

    def remote(source, target, send, recv, device):
        return pltpu.make_async_remote_copy(
            src_ref=source, dst_ref=target, send_sem=send, recv_sem=recv, device_id=device, device_id_type=MESH
        )

    def b_local(source_line, row, count, sem):
        return pltpu.make_async_copy(
            b_in.at[pl.ds(pl.multiple_of(source_line * 128, 128), count * 128)],
            b_rows.at[pl.ds(row * 128, count * 128)], sem,
        )

    b_local(OWN * p, HALO, OWN, b_recv.at[0]).start()

    @pl.when(p > 0)
    def _():
        b_local(OWN * p - HALO, 0, HALO, b_recv.at[1]).start()

    @pl.when(p < n - 1)
    def _():
        b_local(OWN * p + OWN, HALO + OWN, HALO, b_recv.at[2]).start()

    barrier = pltpu.get_barrier_semaphore()

    def greet(i, carry):
        g2, a2 = lax.rem(i, n), lax.rem(a + gx - 1 + i // n, gx)

        @pl.when(jnp.logical_or(g2 != g, a2 != a))
        def _():
            pl.semaphore_signal(barrier, inc=1, device_id=(g2, a2, q), device_id_type=MESH)

        return carry

    lax.fori_loop(0, 3 * n, greet, 0)
    beside = [(place[0], place[1], lax.rem(q + k, gy)) for place in places for k in (1, gy - 1)]
    for device in beside:
        pl.semaphore_signal(barrier, inc=1, device_id=device, device_id_type=MESH)
    pl.semaphore_wait(barrier, 3 * n - 1 + 6)
    for device in beside:
        pl.semaphore_signal(met, inc=1, device_id=device, device_id_type=MESH)

    fields = ((v_in, v_rows), (s_in, s_rows))
    planes = pl.ds(depth * g, depth)

    early = depth * g < STEPS

    def field_copies(start, f):
        source, place = fields[f]
        arrival = field_recv.at[jnp.where(early, f, 2 * f)]
        for other in range(n):
            lo, hi = max(0, OWN * other - HALO), min(local, OWN * other + OWN + HALO)
            row = lo - (OWN * other - HALO)
            target = flip(other)
            args = (source.at[:, pl.ds(lo, hi - lo), :], place.at[planes, pl.ds(row, hi - lo), :])

            @pl.when(target != g)
            def _():
                copy = remote(*args, field_send.at[f, other], arrival, (target, a, q))
                if start:
                    copy.start()
                else:
                    copy.wait_send()

            if start:
                @pl.when(target == g)
                def _():
                    pltpu.make_async_copy(*args, arrival).start()

        ends = (
            (local - HALO, 0, (flip(n - 1), a_right, q), n),
            (0, HALO + OWN, (flip(0), a_left, q), n + 1),
        )
        for line, row, device, sem in ends:
            copy = remote(
                source.at[:, pl.ds(line, HALO), :], place.at[planes, pl.ds(row, HALO), :],
                field_send.at[f, sem], arrival, device,
            )
            if start:
                copy.start()
            else:
                copy.wait_send()

    share = HALO // n

    def b_remote(start):
        for side, line, row, device in (
            (0, local - HALO, 0, (flip(n - 1), a_right, q)), (1, 0, HALO + OWN, (flip(0), a_left, q)),
        ):
            rows = lambda at: pl.ds(pl.multiple_of((at + share * g) * 128, 128), share * 128)
            copy = remote(b_in.at[rows(line)], b_rows.at[rows(row)], b_send.at[side], b_recv.at[1 + side], device)
            if start:
                copy.start()
            else:
                copy.wait_send()

    b_remote(True)
    field_copies(True, 0)

    @pl.when(early)
    def _():
        field_copies(True, 1)


    lane = lax.broadcasted_iota(jnp.int32, (SPAN, 128), 1)
    row = lax.broadcasted_iota(jnp.int32, (SPAN, 128), 0)
    group, xlane = lane // SPAN, lane % SPAN
    line = local * a + OWN * p - HALO + xlane
    inside = jnp.logical_and(line >= 0, line < local * gx)
    low_half, even = group < 2, group % 2 == 0
    group1 = group[:1]
    group8, xlane8, inside8, sub8 = group[:8], xlane[:8], inside[:8], row[:8]
    ends8 = jnp.logical_and(sub8 < 2, jnp.logical_and(xlane8 >= HALO, xlane8 < HALO + OWN))
    top8, bottom8 = jnp.logical_and(sub8 == 0, group8 == 0), jnp.logical_and(sub8 == 7, group8 == 3)

    zero8 = jnp.zeros((8, 128), F32)

    def y_sum(cells):
        up = jnp.where(group1 == 0, 0.0, roll(cells[SPAN - 1 :], SPAN))
        down = jnp.where(group1 == 3, 0.0, roll(cells[:1], -SPAN))
        return cells + jnp.where(row == 0, up, roll(cells, 1, 0)) + jnp.where(row == SPAN - 1, down, roll(cells, -1, 0))

    def box(cells):
        return y_sum(cells + roll(cells, 1) + roll(cells, -1))

    def product(residual, slot):
        res[slot] = residual
        acc = blocks[0] * res[slot, :1, :]
        for j in range(1, SPAN):
            acc = acc + blocks[j] * res[slot, j : j + 1, :]
        rows = [acc[SPAN * i : SPAN * (i + 1)] for i in range(4)]
        parts = []
        for k in range(4):
            part = rows[-k % 4]
            for i in range(1, 4):
                part = jnp.where(group == i, rows[(i - k) % 4], part)
            parts.append(part)
        return parts

    def summed(parts, shifts, at=slice(None)):
        total = None
        for k in range(4):
            for shift in shifts:
                term = roll(parts[k][at], shift - SPAN * k)
                total = term if total is None else total + term
        return total

    def plain(parts, at=slice(None)):
        return summed(parts, (0,), at)

    def apply(residual):
        return plain(product(residual, 7))

    def boxed(parts, slot):
        up = summed(parts, (SPAN - 1, SPAN, SPAN + 1), slice(SPAN - 8, SPAN))
        down = summed(parts, (-SPAN - 1, -SPAN, -SPAN + 1), slice(0, 8))
        pad[slot, :8, :] = jnp.where(group8 == 0, 0.0, up)
        pad[slot, 8 : SPAN + 8, :] = summed(parts, (-1, 0, 1))
        pad[slot, SPAN + 8 :, :] = jnp.where(group8 == 3, 0.0, down)
        return pad[slot, 7 : SPAN + 7, :] + pad[slot, 8 : SPAN + 8, :] + pad[slot, 9 : SPAN + 9, :]

    def turn(x, carry):
        rows = pl.ds(pl.multiple_of(x * 128, 128), 128)
        b_rows[rows, :] = b_rows[rows, :].T
        return carry

    b_local(0, HALO, OWN, b_recv.at[0]).wait()
    lax.fori_loop(HALO, HALO + OWN, turn, 0, unroll=4)
    b_local(0, 0, HALO, b_recv.at[1]).wait()
    lax.fori_loop(0, HALO, turn, 0, unroll=4)
    b_local(0, HALO + OWN, HALO, b_recv.at[2]).wait()
    lax.fori_loop(HALO + OWN, SPAN, turn, 0, unroll=4)

    def gather(j, carry):
        parts = [b_rows[pl.ds(SPAN * jg + j, SPAN, stride=128), :] for jg in range(4)]
        blocks[j] = jnp.where(inside[:1], jnp.concatenate(parts, axis=0).T, 0.0)
        return carry

    lax.fori_loop(0, SPAN, gather, 0, unroll=4)

    columns, cells = [], []
    for slot, at in ((0, 0), (SPAN - 1, 3)):
        column = jnp.zeros((SPAN, 128), F32)
        for i in range(4):
            column = jnp.where(group == i, roll(blocks[slot, SPAN * i : SPAN * (i + 1), :], SPAN * (i - at)), column)
        columns.append(jnp.where(inside, column, 0.0))
        cells.append(y_sum(columns[-1]))
    resp[6], resp[7] = columns
    for j in range(SPAN):
        rows2[0, j : j + 1, :] = blocks[j, :1, :]
        rows2[1, j : j + 1, :] = blocks[j, 127:, :]
    for e in range(2):
        for d in range(3):
            imp[3 * e + d] = roll(cells[e], -(d - 1))

    def respond(i, carry):
        raw[i] = apply(imp[i])
        resp[i] = y_sum(raw[i])
        return carry

    lax.fori_loop(0, 6, respond, 0)

    def spread(value):
        return (value + roll(value, 32)) + (roll(value, 64) + roll(value, 96))

    def pair(values):
        return jnp.where(sub8 == 0, spread(values[0]), spread(values[1]))

    def dots(value):
        return pair([jnp.sum(rows2[e] * value, axis=0, keepdims=True) for e in range(2)])

    def packed(pairs):
        tile = None
        for m in range(0, len(pairs), 4):
            part = jnp.zeros((8, 128), F32)
            for k, value in enumerate(pairs[m : m + 4]):
                part = jnp.where(group8 == k, value, part)
            part = roll(jnp.where(ends8, part, 0.0), m // 2, 0)
            tile = part if tile is None else tile + part
        return tile

    def edge_pair(top, bottom, k):
        return jnp.where(sub8 == 0, roll(top, SPAN * k), roll(roll(bottom, 2, 0), SPAN * (k - 3)))

    first_pairs = [
        pair([jnp.where(group1 == 0, rows2[e, :1, :], 0.0) for e in range(2)]),
        pair([jnp.where(group1 == 3, rows2[e, SPAN - 1 :, :], 0.0) for e in range(2)]),
    ]
    coef[0] = packed([zero8] * 4 + first_pairs)
    later_pairs = [dots(roll(cells[f], -d)) for f in range(2) for d in range(-1, 2)]
    for f in range(2):
        for d in range(-2, 3):
            total = None
            for near in range(-1, 2):
                far = d - near
                if abs(far) <= 1:
                    term = roll(resp[3 * f + far + 1], -near)
                    total = term if total is None else total + term
            wide[5 * f + d + 2] = total
            later_pairs.append(dots(total))
    t_send[0] = packed(later_pairs)

    @pl.when(jnp.logical_not(early))
    def _():
        field_copies(True, 1)

    def settle(place, rows_ref, parts, sem):
        ref = rows_ref.at[4 * parts.start : 4 * parts.stop]
        pltpu.make_async_copy(ref, ref, sem).wait()
        for w in parts:
            turned = rows_ref[4 * w : 4 * w + 4].reshape(128, 128).T
            for k in range(4):
                tile = jnp.zeros((SPAN, 128), F32)
                for i in range(4):
                    tile = jnp.where(group == i, roll(turned[SPAN * i : SPAN * (i + 1)], SPAN * (i - k)), tile)
                place[4 * w + k] = jnp.where(inside, tile, 0.0)

    settle(old, v_rows, range(NZ // 4), field_recv.at[0])
    settle(src, s_rows, range(1), field_recv.at[1])
    zero_tile = jnp.zeros((SPAN, 128), F32)
    old[NZ] = zero_tile
    old[2 * NZ + 1] = zero_tile
    e_old[NZ] = jnp.zeros((8, 128), F32)
    e_old[2 * NZ + 1] = jnp.zeros((8, 128), F32)
    t_send[1] = packed([edge_pair(old[z, :8, :], old[z, SPAN - 8 :, :], z % 4) for z in range(NZ)])

    def edge_copies(source, target, send, recv, start):
        for k in sorted(range(gy), key=lambda k: -min(k, gy - k)):
            for x in (0, 2, 1):
                place = places[x]
                if x == 1 and k == 0:
                    if start:
                        pltpu.make_async_copy(source, target.at[1, q], recv).start()
                    continue
                copy = remote(
                    source, target.at[2 - x, q], send.at[3 * k + x], recv, (place[0], place[1], lax.rem(q + k, gy))
                )
                if start:
                    copy.start()
                else:
                    copy.wait_send()

    pl.semaphore_wait(met, 6)
    edge_copies(t_send, t_recv, t_ssem, t_rsem, True)

    def unpacked(ref, at=None):
        low_side, high_side = xlane8 < HALO, xlane8 >= HALO + OWN
        whole = []
        for k in range(4):
            tile = jnp.zeros((8, 128), F32)
            for b in range(gy):
                sides = [ref[x, b] if at is None else ref[x, b, at] for x in range(3)]
                sides = [roll(sides[x], SPAN * (b - k) + OWN * (x - 1)) for x in range(3)]
                side = jnp.where(low_side, sides[0], jnp.where(high_side, sides[2], sides[1]))
                tile = jnp.where(group8 == b, side, tile)
            whole.append(jnp.where(inside8, tile, 0.0))
        return lambda i: roll(whole[i % 4], -2 * (i // 4), 0)

    def halo_copy(window, side, start):
        device = places[2 * side]
        device = (device[0], device[1], q)
        at = STEPS * window

        @pl.when(window < 4)
        def _():
            copy = remote(
                fresh.at[pl.ds(at, STEPS)], halo.at[window, 1 - side],
                u_ssem.at[window, side], u_rsem.at[window, 1 - side], device,
            )
            if start:
                copy.start()
            else:
                copy.wait_send()

        @pl.when(window >= 4)
        def _():
            copy = remote(
                fresh.at[at + STEPS - 1], halo.at[window, 1 - side, STEPS - 1],
                u_ssem.at[window, side], u_rsem.at[window, 1 - side], device,
            )
            if start:
                copy.start()
            else:
                copy.wait_send()

    def halo_wait(window):
        @pl.when(window < 4)
        def _():
            for side in range(2):
                ref = halo.at[window, side]
                pltpu.make_async_copy(ref, ref, u_rsem.at[window, side]).wait()

        @pl.when(window >= 4)
        def _():
            for side in range(2):
                ref = halo.at[window, side, STEPS - 1]
                pltpu.make_async_copy(ref, ref, u_rsem.at[window, side]).wait()

    def out_copy(z, start):
        owner = z // depth
        source = out_rows.at[z]
        target = out.at[lax.rem(z, depth), pl.ds(pl.multiple_of(OWN * p, OWN), OWN), :]

        @pl.when(owner != g)
        def _():
            copy = remote(source, target, o_ssem.at[z], o_rsem, (owner, a, q))
            if start:
                copy.start()
            else:
                copy.wait_send()

        if start:
            @pl.when(owner == g)
            def _():
                pltpu.make_async_copy(source, target, o_rsem).start()

    def deliver(window):
        at = STEPS * window
        tiles = [fresh[at + k] for k in range(4)]
        parts = []
        for i in range(4):
            part = roll(tiles[0], -SPAN * i)
            for k in range(1, 4):
                part = jnp.where(group == k, roll(tiles[k], SPAN * (k - i)), part)
            parts.append(part)
        lines = jnp.concatenate(parts, axis=0).T
        for k in range(4):
            z = 2 * NZ - 1 - at - k
            out_rows[z] = lines[SPAN * k + HALO : SPAN * k + HALO + OWN]
            out_copy(z, True)

    def window_step(window, carry):
        backward = window // 4
        m0 = STEPS * (window - 4 * backward)
        at = (NZ + 1) * backward + m0
        t0 = STEPS * window
        opening = m0 == 0

        def source_plane(m):
            return src[m + backward * (NZ - 1 - 2 * m)]

        guesses = []
        around = None
        for t in range(STEPS - 1):
            cell = old[at + t]
            near = cell + old[at + t + 1]
            residual = source_plane(m0 + t) - 27.0 * cell + box(near if t == 0 else near + old[at + t - 1])
            residual = residual + (jnp.where(opening, 0.0, last_box[...]) if t == 0 else boxed(around, t))
            ends = (slice(0, 8), slice(SPAN - 8, SPAN))
            if t < STEPS - 2:
                around = product(residual, t)
                change = jnp.where(
                    sub8 == 0, summed(around, (SPAN * t,), ends[0]),
                    roll(summed(around, (SPAN * (t - 3),), ends[1]), 2, 0),
                )
                guesses.append(edge_pair(*(cell[end] for end in ends), t) + change)
            else:
                guesses.append(edge_pair(*(cell[end] for end in ends), t) + dots(residual))
        done = []
        for k in range(STEPS):
            tile = fresh.at[jnp.maximum(t0 - STEPS + k, 0)]
            done.append(edge_pair(tile[:8, :], tile[SPAN - 8 :, :], k))
        first = packed(guesses + [jnp.where(window == 0, 0.0, done[3])])
        rest = packed([zero8] * 4 + [done[k] for k in range(3)])
        e_send[window] = first + jnp.where(window == 0, coef[0], rest)
        edge_copies(e_send.at[window, :4], e_recv.at[window, :, :, :4], e_ssem.at[window], e_rsem.at[window], True)

        @pl.when(window == 0)
        def _():
            settle(src, s_rows, range(1, NZ // 4), field_recv.at[2])

        @pl.when(window > 4)
        def _():
            deliver(window - 1)

        @pl.when(window > 0)
        def _():
            halo_wait(window - 1)

        def merged(t):
            mid = fresh[jnp.maximum(t0 - STEPS + t, 0)]
            w = jnp.maximum(window - 1, 0)
            tile = jnp.where(
                xlane < HALO, roll(halo[w, 0, t], -OWN),
                jnp.where(xlane >= HALO + OWN, roll(halo[w, 1, t], OWN), mid),
            )
            return jnp.where(inside, tile, 0.0)

        @pl.when(jnp.logical_and(window > 0, window <= 4))
        def _():
            for t in range(STEPS):
                old[2 * NZ - jnp.maximum(t0 - STEPS + t, 0)] = merged(t)

        @pl.when(opening)
        def _():
            start[...] = zero_tile

        @pl.when(jnp.logical_not(opening))
        def _():
            start[...] = merged(STEPS - 1)

        for t in range(STEPS):
            cell = old[at + t]
            before = start[...] if t == 0 else free[t - 1] if t < 3 else old[at + t - 1]
            value = source_plane(m0 + t) - 27.0 * cell + box(cell + old[at + t + 1] + before)
            free[t] = cell + plain(product(value, 2 + t)) if t < 2 else value

        @pl.when(window == 0)
        def _():
            pltpu.make_async_copy(t_recv, t_recv, t_rsem).wait()
            item = unpacked(t_recv, 0)
            for r in range(16):
                coef[2 + r] = item(r)
            item = unpacked(t_recv, 1)
            for r in range(NZ):
                e_old[r] = item(r)

        arrived, landed = e_recv.at[window], e_recv.at[window, :, :, :4]
        pltpu.make_async_copy(landed, landed, e_rsem.at[window]).wait()
        item = unpacked(arrived)

        for r in range(2):
            coef[r] = jnp.where(window == 0, item(4 + r), coef[r])
        kept = jnp.logical_and(window > 0, window <= 4)
        for t in range(STEPS):
            place = jnp.where(kept, 2 * NZ - (t0 - STEPS + t), 2 * NZ + 2)
            e_old[place] = item(3 if t == 3 else 4 + t)

        before = jnp.where(opening, 0.0, item(3))
        gives, gains, planes_now = [], [], []
        around = None
        for t in range(STEPS):
            total = before + (e_old[at + t] + e_old[at + t + 1])
            reach = max(0, STEPS - 2 - t)
            low, high = jnp.broadcast_to(total[1:2], (8, 128)), jnp.broadcast_to(total[:1], (8, 128))
            from_low = {c: roll(low, SPAN - c) for c in range(-reach - 1, reach + 2)}
            from_high = {c: roll(high, -SPAN - c) for c in range(-reach - 1, reach + 2)}
            give = {}
            for d in range(-reach, reach + 1):
                give[0, d] = jnp.where(group8 > 0, from_low[d - 1] + from_low[d] + from_low[d + 1], 0.0)
                give[1, d] = jnp.where(group8 < gy - 1, from_high[d - 1] + from_high[d] + from_high[d + 1], 0.0)
            gives.append(give)
            if t < 2:
                gains.append({
                    key: jnp.concatenate([spread(jnp.where(group8 == q, give[key], 0.0))] * 4, axis=0) for key in give
                })
                now = free[t] + (resp[6] * gains[t][0, 0] + resp[7] * gains[t][1, 0])
                if t == 1:
                    for f in range(2):
                        for d in range(-1, 2):
                            now = now + raw[3 * f + d + 1] * gains[0][f, d]
            else:
                mine = (
                    jnp.where(top8, pltpu.roll(give[0, 0], lax.rem(128 - SPAN * q, 128), 1), 0.0),
                    jnp.where(bottom8, pltpu.roll(give[1, 0], SPAN * (3 - q), 1), 0.0),
                )
                if t == 2:
                    residual = free[2]
                    for f in range(2):
                        for d in range(-1, 2):
                            residual = residual + imp[3 * f + d + 1] * gains[1][f, d]
                        for d in range(-2, 3):
                            residual = residual + wide[5 * f + d + 2] * gains[0][f, d]
                else:
                    residual = free[t] + boxed(around, 1 + t)
                residual = jnp.concatenate(
                    [residual[:8] + mine[0], residual[8 : SPAN - 8], residual[SPAN - 8 :] + mine[1]], axis=0
                )
                around = product(residual, 2 + t)
                now = old[at + t] + plain(around)
            fresh[t0 + t] = now
            planes_now.append(now)
            if t < STEPS - 1:
                value = item(t)
                for s in range(t + 1):
                    lag = t - s
                    for f in range(2):
                        for d in range(-lag, lag + 1):
                            r = (0, 2, 8)[lag] + f * (2 * lag + 1) + d + lag
                            value = value + coef[r] * gives[s][f, d]
                before = jnp.where(inside8, value, 0.0)

        last_box[...] = box(old[at + STEPS - 1]) + boxed(around, 4)

        for t in range(STEPS):
            old[jnp.where(backward == 0, 2 * NZ - (t0 + t), 2 * NZ + 2)] = planes_now[t]

        @pl.when(window < 7)
        def _():
            halo_copy(window, 0, True)
            halo_copy(window, 1, True)

        return carry

    lax.fori_loop(0, 8, window_step, 0)
    deliver(7)

    field_copies(False, 0)
    field_copies(False, 1)
    b_remote(False)
    edge_copies(t_send, t_recv, t_ssem, t_rsem, False)

    def drain(window, carry):
        edge_copies(e_send.at[window, :4], e_recv.at[window, :, :, :4], e_ssem.at[window], e_rsem.at[window], False)

        @pl.when(window < 7)
        def _():
            halo_copy(window, 0, False)
            halo_copy(window, 1, False)

        return carry

    lax.fori_loop(0, 8, drain, 0)

    def drain_out(z, carry):
        out_copy(z, False)
        return carry

    lax.fori_loop(0, NZ, drain_out, 0)
    pltpu.make_async_copy(out, out, o_rsem).wait()


def solution(mesh):
    n, gx, gy = mesh.shape["gz"], mesh.shape["gx"], mesh.shape["gy"]

    def body(initial_field, source_term, block_inverse):
        depth, local, width = initial_field.shape
        vmem = lambda *shape: pltpu.VMEM(shape, F32)
        dma = pltpu.SemaphoreType.DMA
        return pl.pallas_call(
            functools.partial(kernel, n, gx, gy, depth),
            out_shape=jax.ShapeDtypeStruct(initial_field.shape, F32),
            in_specs=[pl.BlockSpec(memory_space=pltpu.HBM)] * 3,
            out_specs=pl.BlockSpec(memory_space=pltpu.VMEM),
            scratch_shapes=[
                vmem(NZ, SPAN, 128), vmem(NZ, SPAN, 128), vmem(SPAN * 128, 128), vmem(SPAN, 128, 128),
                vmem(2 * NZ + 3, SPAN, 128), vmem(NZ, SPAN, 128), vmem(2 * NZ, SPAN, 128),
                vmem(8, 2, STEPS, SPAN, 128),
                vmem(STEPS, SPAN, 128), vmem(8, SPAN, 128), vmem(8, SPAN + 16, 128), vmem(SPAN, 128), vmem(SPAN, 128),
                vmem(8, 8, 128), vmem(8, 3, gy, 8, 128), vmem(2, 8, 128), vmem(3, gy, 2, 8, 128),
                vmem(2 * NZ + 3, 8, 128), vmem(18, 8, 128), vmem(2, SPAN, 128),
                vmem(6, SPAN, 128), vmem(6, SPAN, 128), vmem(10, SPAN, 128), vmem(8, SPAN, 128), vmem(NZ, OWN, 128),
                dma((2, n + 2)), dma((3,)), dma((3,)), dma((2,)),
                dma((8, 3 * gy)), dma((8,)), dma((3 * gy,)), dma,
                dma((8, 2)), dma((8, 2)), dma((NZ,)), dma, pltpu.SemaphoreType.REGULAR,
            ],
            compiler_params=pltpu.CompilerParams(
                collective_id=0, has_side_effects=True, vmem_limit_bytes=60 * 1024 * 1024
            ),
        )(initial_field, source_term, block_inverse.reshape(local * width, width))

    return jax.shard_map(
        body, mesh=mesh,
        in_specs=(P("gz", "gx", "gy"), P("gz", "gx", "gy"), P("gx", "gy", None)),
        out_specs=P("gz", "gx", "gy"), check_vma=False,
    )
```

```python
import functools

import jax
import jax.numpy as jnp
from jax import lax
from jax.experimental import pallas as pl
from jax.experimental.pallas import tpu as pltpu
from jax.sharding import PartitionSpec as P

MESH = pl.DeviceIdType.MESH
F32 = jnp.float32
OWN = 16
HALO = 8
SPAN = 32
STEPS = 4
NZ = 16


def roll(value, shift, axis=1):
    size = value.shape[axis]
    shift = shift % size
    return value if shift == 0 else pltpu.roll(value, shift, axis)


def kernel(
    n, gx, gy, depth,
    v_in, s_in, b_in, out,
    v_rows, s_rows, b_rows, blocks, old, src, fresh, halo,
    free, res, pad, last_box, start, e_send, e_recv, t_send, t_recv, e_old, coef, rows2, imp, raw, raw2, resp2, wide, wide2, resp, out_rows,
    field_send, field_recv, b_recv, b_send, e_ssem, e_rsem, t_ssem, t_rsem, u_ssem, u_rsem, o_ssem, o_rsem, met,
):
    g, a, q = lax.axis_index("gz"), lax.axis_index("gx"), lax.axis_index("gy")
    par = lax.rem(a, 2)
    local = OWN * n

    def flip(p):
        return p + par * (n - 1 - 2 * p)

    p = flip(g)
    a_left, a_right = lax.rem(a + gx - 1, gx), lax.rem(a + 1, gx)
    step_up = 1 - 2 * par
    first, last = p == 0, p == n - 1
    left = (jnp.where(first, g, g - step_up), jnp.where(first, a_left, a))
    right = (jnp.where(last, g, g + step_up), jnp.where(last, a_right, a))
    places = (left, (g, a), right)

    def remote(source, target, send, recv, device):
        return pltpu.make_async_remote_copy(
            src_ref=source, dst_ref=target, send_sem=send, recv_sem=recv, device_id=device, device_id_type=MESH
        )

    def b_local(source_line, row, count, sem):
        return pltpu.make_async_copy(
            b_in.at[pl.ds(pl.multiple_of(source_line * 128, 128), count * 128)],
            b_rows.at[pl.ds(row * 128, count * 128)], sem,
        )

    b_local(OWN * p, HALO, OWN, b_recv.at[0]).start()

    @pl.when(p > 0)
    def _():
        b_local(OWN * p - HALO, 0, HALO, b_recv.at[1]).start()

    @pl.when(p < n - 1)
    def _():
        b_local(OWN * p + OWN, HALO + OWN, HALO, b_recv.at[2]).start()

    barrier = pltpu.get_barrier_semaphore()

    def greet(i, carry):
        g2, a2 = lax.rem(i, n), lax.rem(a + gx - 1 + i // n, gx)

        @pl.when(jnp.logical_or(g2 != g, a2 != a))
        def _():
            pl.semaphore_signal(barrier, inc=1, device_id=(g2, a2, q), device_id_type=MESH)

        return carry

    lax.fori_loop(0, 3 * n, greet, 0)
    beside = [(place[0], place[1], lax.rem(q + k, gy)) for place in places for k in (1, gy - 1)]
    for device in beside:
        pl.semaphore_signal(barrier, inc=1, device_id=device, device_id_type=MESH)
    pl.semaphore_wait(barrier, 3 * n - 1 + 6)
    for device in beside:
        pl.semaphore_signal(met, inc=1, device_id=device, device_id_type=MESH)

    fields = ((v_in, v_rows), (s_in, s_rows))
    planes = pl.ds(depth * g, depth)

    early = depth * g < STEPS

    def field_copies(start, f):
        source, place = fields[f]
        arrival = field_recv.at[jnp.where(early, f, 2 * f)]
        for other in range(n):
            lo, hi = max(0, OWN * other - HALO), min(local, OWN * other + OWN + HALO)
            row = lo - (OWN * other - HALO)
            target = flip(other)
            args = (source.at[:, pl.ds(lo, hi - lo), :], place.at[planes, pl.ds(row, hi - lo), :])

            @pl.when(target != g)
            def _():
                copy = remote(*args, field_send.at[f, other], arrival, (target, a, q))
                if start:
                    copy.start()
                else:
                    copy.wait_send()

            if start:
                @pl.when(target == g)
                def _():
                    pltpu.make_async_copy(*args, arrival).start()

        ends = (
            (local - HALO, 0, (flip(n - 1), a_right, q), n),
            (0, HALO + OWN, (flip(0), a_left, q), n + 1),
        )
        for line, row, device, sem in ends:
            copy = remote(
                source.at[:, pl.ds(line, HALO), :], place.at[planes, pl.ds(row, HALO), :],
                field_send.at[f, sem], arrival, device,
            )
            if start:
                copy.start()
            else:
                copy.wait_send()

    share = HALO // n

    def b_remote(start):
        for side, line, row, device in (
            (0, local - HALO, 0, (flip(n - 1), a_right, q)), (1, 0, HALO + OWN, (flip(0), a_left, q)),
        ):
            rows = lambda at: pl.ds(pl.multiple_of((at + share * g) * 128, 128), share * 128)
            copy = remote(b_in.at[rows(line)], b_rows.at[rows(row)], b_send.at[side], b_recv.at[1 + side], device)
            if start:
                copy.start()
            else:
                copy.wait_send()

    b_remote(True)
    field_copies(True, 0)

    @pl.when(early)
    def _():
        field_copies(True, 1)


    lane = lax.broadcasted_iota(jnp.int32, (SPAN, 128), 1)
    row = lax.broadcasted_iota(jnp.int32, (SPAN, 128), 0)
    group, xlane = lane // SPAN, lane % SPAN
    line = local * a + OWN * p - HALO + xlane
    inside = jnp.logical_and(line >= 0, line < local * gx)
    low_half, even = group < 2, group % 2 == 0
    group1 = group[:1]
    group8, xlane8, inside8, sub8 = group[:8], xlane[:8], inside[:8], row[:8]
    ends8 = jnp.logical_and(sub8 < 2, jnp.logical_and(xlane8 >= HALO, xlane8 < HALO + OWN))
    top8, bottom8 = jnp.logical_and(sub8 == 0, group8 == 0), jnp.logical_and(sub8 == 7, group8 == 3)

    zero8 = jnp.zeros((8, 128), F32)

    def y_sum(cells):
        up = jnp.where(group1 == 0, 0.0, roll(cells[SPAN - 1 :], SPAN))
        down = jnp.where(group1 == 3, 0.0, roll(cells[:1], -SPAN))
        return cells + jnp.where(row == 0, up, roll(cells, 1, 0)) + jnp.where(row == SPAN - 1, down, roll(cells, -1, 0))

    def box(cells):
        return y_sum(cells + roll(cells, 1) + roll(cells, -1))

    def product(residual, slot):
        res[slot] = residual
        acc = blocks[0] * res[slot, :1, :]
        for j in range(1, SPAN):
            acc = acc + blocks[j] * res[slot, j : j + 1, :]
        rows = [acc[SPAN * i : SPAN * (i + 1)] for i in range(4)]
        parts = []
        for k in range(4):
            part = rows[-k % 4]
            for i in range(1, 4):
                part = jnp.where(group == i, rows[(i - k) % 4], part)
            parts.append(part)
        return parts

    def summed(parts, shifts, at=slice(None)):
        total = None
        for k in range(4):
            for shift in shifts:
                term = roll(parts[k][at], shift - SPAN * k)
                total = term if total is None else total + term
        return total

    def plain(parts, at=slice(None)):
        return summed(parts, (0,), at)

    def apply(residual):
        return plain(product(residual, 7))

    def boxed(parts, slot):
        up = summed(parts, (SPAN - 1, SPAN, SPAN + 1), slice(SPAN - 8, SPAN))
        down = summed(parts, (-SPAN - 1, -SPAN, -SPAN + 1), slice(0, 8))
        pad[slot, :8, :] = jnp.where(group8 == 0, 0.0, up)
        pad[slot, 8 : SPAN + 8, :] = summed(parts, (-1, 0, 1))
        pad[slot, SPAN + 8 :, :] = jnp.where(group8 == 3, 0.0, down)
        return pad[slot, 7 : SPAN + 7, :] + pad[slot, 8 : SPAN + 8, :] + pad[slot, 9 : SPAN + 9, :]

    def turn(x, carry):
        rows = pl.ds(pl.multiple_of(x * 128, 128), 128)
        b_rows[rows, :] = b_rows[rows, :].T
        return carry

    b_local(0, HALO, OWN, b_recv.at[0]).wait()
    lax.fori_loop(HALO, HALO + OWN, turn, 0, unroll=4)
    b_local(0, 0, HALO, b_recv.at[1]).wait()
    lax.fori_loop(0, HALO, turn, 0, unroll=4)
    b_local(0, HALO + OWN, HALO, b_recv.at[2]).wait()
    lax.fori_loop(HALO + OWN, SPAN, turn, 0, unroll=4)

    def gather(j, carry):
        parts = [b_rows[pl.ds(SPAN * jg + j, SPAN, stride=128), :] for jg in range(4)]
        blocks[j] = jnp.where(inside[:1], jnp.concatenate(parts, axis=0).T, 0.0)
        return carry

    lax.fori_loop(0, SPAN, gather, 0, unroll=4)

    columns, cells = [], []
    for slot, at in ((0, 0), (SPAN - 1, 3)):
        column = jnp.zeros((SPAN, 128), F32)
        for i in range(4):
            column = jnp.where(group == i, roll(blocks[slot, SPAN * i : SPAN * (i + 1), :], SPAN * (i - at)), column)
        columns.append(jnp.where(inside, column, 0.0))
        cells.append(y_sum(columns[-1]))
    resp[6], resp[7] = columns
    for j in range(SPAN):
        rows2[0, j : j + 1, :] = blocks[j, :1, :]
        rows2[1, j : j + 1, :] = blocks[j, 127:, :]
    for e in range(2):
        for d in range(3):
            imp[3 * e + d] = roll(cells[e], -(d - 1))

    def respond(i, carry):
        raw[i] = apply(imp[i])
        resp[i] = y_sum(raw[i])
        return carry

    lax.fori_loop(0, 6, respond, 0)

    def spread(value):
        return (value + roll(value, 32)) + (roll(value, 64) + roll(value, 96))

    def pair(values):
        return jnp.where(sub8 == 0, spread(values[0]), spread(values[1]))

    def dots(value):
        return pair([jnp.sum(rows2[e] * value, axis=0, keepdims=True) for e in range(2)])

    def packed(pairs):
        tile = None
        for m in range(0, len(pairs), 4):
            part = jnp.zeros((8, 128), F32)
            for k, value in enumerate(pairs[m : m + 4]):
                part = jnp.where(group8 == k, value, part)
            part = roll(jnp.where(ends8, part, 0.0), m // 2, 0)
            tile = part if tile is None else tile + part
        return tile

    def edge_pair(top, bottom, k):
        return jnp.where(sub8 == 0, roll(top, SPAN * k), roll(roll(bottom, 2, 0), SPAN * (k - 3)))

    first_pairs = [
        pair([jnp.where(group1 == 0, rows2[e, :1, :], 0.0) for e in range(2)]),
        pair([jnp.where(group1 == 3, rows2[e, SPAN - 1 :, :], 0.0) for e in range(2)]),
    ]
    coef[0] = packed([zero8] * 4 + first_pairs)
    later_pairs = [dots(roll(cells[f], -d)) for f in range(2) for d in range(-1, 2)]
    for f in range(2):
        for d in range(-2, 3):
            total = None
            for near in range(-1, 2):
                far = d - near
                if abs(far) <= 1:
                    term = roll(resp[3 * f + far + 1], -near)
                    total = term if total is None else total + term
            wide[5 * f + d + 2] = total
            later_pairs.append(dots(total))
    t_send[0] = packed(later_pairs)

    @pl.when(jnp.logical_not(early))
    def _():
        field_copies(True, 1)

    def settle(place, rows_ref, parts, sem):
        ref = rows_ref.at[4 * parts.start : 4 * parts.stop]
        pltpu.make_async_copy(ref, ref, sem).wait()
        for w in parts:
            turned = rows_ref[4 * w : 4 * w + 4].reshape(128, 128).T
            for k in range(4):
                tile = jnp.zeros((SPAN, 128), F32)
                for i in range(4):
                    tile = jnp.where(group == i, roll(turned[SPAN * i : SPAN * (i + 1)], SPAN * (i - k)), tile)
                place[4 * w + k] = jnp.where(inside, tile, 0.0)

    settle(old, v_rows, range(NZ // 4), field_recv.at[0])
    settle(src, s_rows, range(1), field_recv.at[1])
    zero_tile = jnp.zeros((SPAN, 128), F32)
    old[NZ] = zero_tile
    old[2 * NZ + 1] = zero_tile
    e_old[NZ] = jnp.zeros((8, 128), F32)
    e_old[2 * NZ + 1] = jnp.zeros((8, 128), F32)
    t_send[1] = packed([edge_pair(old[z, :8, :], old[z, SPAN - 8 :, :], z % 4) for z in range(NZ)])

    def edge_copies(source, target, send, recv, start):
        for k in sorted(range(gy), key=lambda k: -min(k, gy - k)):
            for x in (0, 2, 1):
                place = places[x]
                if x == 1 and k == 0:
                    if start:
                        pltpu.make_async_copy(source, target.at[1, q], recv).start()
                    continue
                copy = remote(
                    source, target.at[2 - x, q], send.at[3 * k + x], recv, (place[0], place[1], lax.rem(q + k, gy))
                )
                if start:
                    copy.start()
                else:
                    copy.wait_send()

    pl.semaphore_wait(met, 6)
    edge_copies(t_send, t_recv, t_ssem, t_rsem, True)

    def unpacked(ref, at=None):
        low_side, high_side = xlane8 < HALO, xlane8 >= HALO + OWN
        whole = []
        for k in range(4):
            tile = jnp.zeros((8, 128), F32)
            for b in range(gy):
                sides = [ref[x, b] if at is None else ref[x, b, at] for x in range(3)]
                sides = [roll(sides[x], SPAN * (b - k) + OWN * (x - 1)) for x in range(3)]
                side = jnp.where(low_side, sides[0], jnp.where(high_side, sides[2], sides[1]))
                tile = jnp.where(group8 == b, side, tile)
            whole.append(jnp.where(inside8, tile, 0.0))
        return lambda i: roll(whole[i % 4], -2 * (i // 4), 0)

    def halo_copy(window, side, start):
        device = places[2 * side]
        device = (device[0], device[1], q)
        at = STEPS * window

        @pl.when(window < 4)
        def _():
            copy = remote(
                fresh.at[pl.ds(at, STEPS)], halo.at[window, 1 - side],
                u_ssem.at[window, side], u_rsem.at[window, 1 - side], device,
            )
            if start:
                copy.start()
            else:
                copy.wait_send()

        @pl.when(window >= 4)
        def _():
            copy = remote(
                fresh.at[at + STEPS - 1], halo.at[window, 1 - side, STEPS - 1],
                u_ssem.at[window, side], u_rsem.at[window, 1 - side], device,
            )
            if start:
                copy.start()
            else:
                copy.wait_send()

    def halo_wait(window):
        @pl.when(window < 4)
        def _():
            for side in range(2):
                ref = halo.at[window, side]
                pltpu.make_async_copy(ref, ref, u_rsem.at[window, side]).wait()

        @pl.when(window >= 4)
        def _():
            for side in range(2):
                ref = halo.at[window, side, STEPS - 1]
                pltpu.make_async_copy(ref, ref, u_rsem.at[window, side]).wait()

    def out_copy(z, start):
        owner = z // depth
        source = out_rows.at[z]
        target = out.at[lax.rem(z, depth), pl.ds(pl.multiple_of(OWN * p, OWN), OWN), :]

        @pl.when(owner != g)
        def _():
            copy = remote(source, target, o_ssem.at[z], o_rsem, (owner, a, q))
            if start:
                copy.start()
            else:
                copy.wait_send()

        if start:
            @pl.when(owner == g)
            def _():
                pltpu.make_async_copy(source, target, o_rsem).start()

    def deliver(window):
        at = STEPS * window
        tiles = [fresh[at + k] for k in range(4)]
        parts = []
        for i in range(4):
            part = roll(tiles[0], -SPAN * i)
            for k in range(1, 4):
                part = jnp.where(group == k, roll(tiles[k], SPAN * (k - i)), part)
            parts.append(part)
        lines = jnp.concatenate(parts, axis=0).T
        for k in range(4):
            z = 2 * NZ - 1 - at - k
            out_rows[z] = lines[SPAN * k + HALO : SPAN * k + HALO + OWN]
            out_copy(z, True)

    def window_step(window, carry):
        backward = window // 4
        m0 = STEPS * (window - 4 * backward)
        at = (NZ + 1) * backward + m0
        t0 = STEPS * window
        opening = m0 == 0

        def source_plane(m):
            return src[m + backward * (NZ - 1 - 2 * m)]

        guesses = []
        around = None
        for t in range(STEPS - 1):
            cell = old[at + t]
            near = cell + old[at + t + 1]
            residual = source_plane(m0 + t) - 27.0 * cell + box(near if t == 0 else near + old[at + t - 1])
            residual = residual + (jnp.where(opening, 0.0, last_box[...]) if t == 0 else boxed(around, t))
            ends = (slice(0, 8), slice(SPAN - 8, SPAN))
            if t < STEPS - 2:
                around = product(residual, t)
                change = jnp.where(
                    sub8 == 0, summed(around, (SPAN * t,), ends[0]),
                    roll(summed(around, (SPAN * (t - 3),), ends[1]), 2, 0),
                )
                guesses.append(edge_pair(*(cell[end] for end in ends), t) + change)
            else:
                guesses.append(edge_pair(*(cell[end] for end in ends), t) + dots(residual))
        done = []
        for k in range(STEPS):
            tile = fresh.at[jnp.maximum(t0 - STEPS + k, 0)]
            done.append(edge_pair(tile[:8, :], tile[SPAN - 8 :, :], k))
        first = packed(guesses + [jnp.where(window == 0, 0.0, done[3])])
        rest = packed([zero8] * 4 + [done[k] for k in range(3)])
        e_send[window] = first + jnp.where(window == 0, coef[0], rest)
        edge_copies(e_send.at[window, :4], e_recv.at[window, :, :, :4], e_ssem.at[window], e_rsem.at[window], True)

        @pl.when(window == 0)
        def _():
            settle(src, s_rows, range(1, NZ // 4), field_recv.at[2])

            for i in range(10):
                value = plain(product(wide[i], i % 8))
                raw2[i] = value
                resp2[i] = y_sum(value)

            for f in range(2):
                for d in range(-3, 4):
                    total = None
                    for near in range(-1, 2):
                        far = d - near
                        if abs(far) <= 2:
                            term = roll(resp2[5 * f + far + 2], -near)
                            total = term if total is None else total + term
                    wide2[7 * f + d + 3] = total

        @pl.when(window > 4)
        def _():
            deliver(window - 1)

        @pl.when(window > 0)
        def _():
            halo_wait(window - 1)

        def merged(t):
            mid = fresh[jnp.maximum(t0 - STEPS + t, 0)]
            w = jnp.maximum(window - 1, 0)
            tile = jnp.where(
                xlane < HALO, roll(halo[w, 0, t], -OWN),
                jnp.where(xlane >= HALO + OWN, roll(halo[w, 1, t], OWN), mid),
            )
            return jnp.where(inside, tile, 0.0)

        @pl.when(jnp.logical_and(window > 0, window <= 4))
        def _():
            for t in range(STEPS):
                old[2 * NZ - jnp.maximum(t0 - STEPS + t, 0)] = merged(t)

        @pl.when(opening)
        def _():
            start[...] = zero_tile

        @pl.when(jnp.logical_not(opening))
        def _():
            start[...] = merged(STEPS - 1)

        for t in range(STEPS):
            cell = old[at + t]
            before = start[...] if t == 0 else free[t - 1]
            value = source_plane(m0 + t) - 27.0 * cell + box(cell + old[at + t + 1] + before)
            free[t] = cell + plain(product(value, 2 + t)) if t < STEPS - 1 else value

        @pl.when(window == 0)
        def _():
            pltpu.make_async_copy(t_recv, t_recv, t_rsem).wait()
            item = unpacked(t_recv, 0)
            for r in range(16):
                coef[2 + r] = item(r)
            item = unpacked(t_recv, 1)
            for r in range(NZ):
                e_old[r] = item(r)

        arrived, landed = e_recv.at[window], e_recv.at[window, :, :, :4]
        pltpu.make_async_copy(landed, landed, e_rsem.at[window]).wait()
        item = unpacked(arrived)

        for r in range(2):
            coef[r] = jnp.where(window == 0, item(4 + r), coef[r])
        kept = jnp.logical_and(window > 0, window <= 4)
        for t in range(STEPS):
            place = jnp.where(kept, 2 * NZ - (t0 - STEPS + t), 2 * NZ + 2)
            e_old[place] = item(3 if t == 3 else 4 + t)

        before = jnp.where(opening, 0.0, item(3))
        gives, gains, planes_now = [], [], []
        around = None
        for t in range(STEPS):
            total = before + (e_old[at + t] + e_old[at + t + 1])
            reach = max(0, STEPS - 2 - t)
            low, high = jnp.broadcast_to(total[1:2], (8, 128)), jnp.broadcast_to(total[:1], (8, 128))
            from_low = {c: roll(low, SPAN - c) for c in range(-reach - 1, reach + 2)}
            from_high = {c: roll(high, -SPAN - c) for c in range(-reach - 1, reach + 2)}
            give = {}
            for d in range(-reach, reach + 1):
                give[0, d] = jnp.where(group8 > 0, from_low[d - 1] + from_low[d] + from_low[d + 1], 0.0)
                give[1, d] = jnp.where(group8 < gy - 1, from_high[d - 1] + from_high[d] + from_high[d + 1], 0.0)
            gives.append(give)
            if t < STEPS - 1:
                wing = STEPS - 1 - t
                gain = {}
                for f, (edge, there) in enumerate(((low, q - 1), (high, q + 1))):
                    mine = spread(jnp.where(group8 == there, edge, 0.0))
                    moved = {c: roll(mine, -c) for c in range(-wing - 1, wing + 2)}
                    for d in range(-wing, wing + 1):
                        gain[f, d] = jnp.concatenate([moved[d - 1] + moved[d] + moved[d + 1]] * 4, axis=0)
                gains.append(gain)
                now = free[t]
                for s in range(t + 1):
                    lag = t - s
                    for f in range(2):
                        for d in range(-lag, lag + 1):
                            if lag == 0:
                                tile = resp[6 + f]
                            else:
                                tile = raw[3 * f + d + 1] if lag == 1 else raw2[5 * f + d + 2]
                            now = now + tile * gains[s][f, d]
            else:
                mine = (
                    jnp.where(top8, pltpu.roll(give[0, 0], lax.rem(128 - SPAN * q, 128), 1), 0.0),
                    jnp.where(bottom8, pltpu.roll(give[1, 0], SPAN * (3 - q), 1), 0.0),
                )
                residual = free[t]
                for s, (tiles, width) in enumerate(((wide2, 3), (wide, 2), (imp, 1))):
                    for f in range(2):
                        for d in range(-width, width + 1):
                            residual = residual + tiles[(2 * width + 1) * f + d + width] * gains[s][f, d]
                residual = jnp.concatenate(
                    [residual[:8] + mine[0], residual[8 : SPAN - 8], residual[SPAN - 8 :] + mine[1]], axis=0
                )
                around = product(residual, 5)
                now = old[at + t] + plain(around)
            fresh[t0 + t] = now
            planes_now.append(now)
            if t < STEPS - 1:
                value = item(t)
                for s in range(t + 1):
                    lag = t - s
                    for f in range(2):
                        for d in range(-lag, lag + 1):
                            r = (0, 2, 8)[lag] + f * (2 * lag + 1) + d + lag
                            value = value + coef[r] * gives[s][f, d]
                before = jnp.where(inside8, value, 0.0)

        last_box[...] = box(old[at + STEPS - 1]) + boxed(around, 4)

        for t in range(STEPS):
            old[jnp.where(backward == 0, 2 * NZ - (t0 + t), 2 * NZ + 2)] = planes_now[t]

        @pl.when(window < 7)
        def _():
            halo_copy(window, 0, True)
            halo_copy(window, 1, True)

        return carry

    lax.fori_loop(0, 8, window_step, 0)
    deliver(7)

    field_copies(False, 0)
    field_copies(False, 1)
    b_remote(False)
    edge_copies(t_send, t_recv, t_ssem, t_rsem, False)

    def drain(window, carry):
        edge_copies(e_send.at[window, :4], e_recv.at[window, :, :, :4], e_ssem.at[window], e_rsem.at[window], False)

        @pl.when(window < 7)
        def _():
            halo_copy(window, 0, False)
            halo_copy(window, 1, False)

        return carry

    lax.fori_loop(0, 8, drain, 0)

    def drain_out(z, carry):
        out_copy(z, False)
        return carry

    lax.fori_loop(0, NZ, drain_out, 0)
    pltpu.make_async_copy(out, out, o_rsem).wait()


def solution(mesh):
    n, gx, gy = mesh.shape["gz"], mesh.shape["gx"], mesh.shape["gy"]

    def body(initial_field, source_term, block_inverse):
        depth, local, width = initial_field.shape
        vmem = lambda *shape: pltpu.VMEM(shape, F32)
        dma = pltpu.SemaphoreType.DMA
        return pl.pallas_call(
            functools.partial(kernel, n, gx, gy, depth),
            out_shape=jax.ShapeDtypeStruct(initial_field.shape, F32),
            in_specs=[pl.BlockSpec(memory_space=pltpu.HBM)] * 3,
            out_specs=pl.BlockSpec(memory_space=pltpu.VMEM),
            scratch_shapes=[
                vmem(NZ, SPAN, 128), vmem(NZ, SPAN, 128), vmem(SPAN * 128, 128), vmem(SPAN, 128, 128),
                vmem(2 * NZ + 3, SPAN, 128), vmem(NZ, SPAN, 128), vmem(2 * NZ, SPAN, 128),
                vmem(8, 2, STEPS, SPAN, 128),
                vmem(STEPS, SPAN, 128), vmem(8, SPAN, 128), vmem(8, SPAN + 16, 128), vmem(SPAN, 128), vmem(SPAN, 128),
                vmem(8, 8, 128), vmem(8, 3, gy, 8, 128), vmem(2, 8, 128), vmem(3, gy, 2, 8, 128),
                vmem(2 * NZ + 3, 8, 128), vmem(18, 8, 128), vmem(2, SPAN, 128),
                vmem(6, SPAN, 128), vmem(6, SPAN, 128), vmem(10, SPAN, 128), vmem(10, SPAN, 128), vmem(10, SPAN, 128),
                vmem(14, SPAN, 128), vmem(8, SPAN, 128), vmem(NZ, OWN, 128),
                dma((2, n + 2)), dma((3,)), dma((3,)), dma((2,)),
                dma((8, 3 * gy)), dma((8,)), dma((3 * gy,)), dma,
                dma((8, 2)), dma((8, 2)), dma((NZ,)), dma, pltpu.SemaphoreType.REGULAR,
            ],
            compiler_params=pltpu.CompilerParams(
                collective_id=0, has_side_effects=True, vmem_limit_bytes=60 * 1024 * 1024
            ),
        )(initial_field, source_term, block_inverse.reshape(local * width, width))

    return jax.shard_map(
        body, mesh=mesh,
        in_specs=(P("gz", "gx", "gy"), P("gz", "gx", "gy"), P("gx", "gy", None)),
        out_specs=P("gz", "gx", "gy"), check_vma=False,
    )
```

```python
import functools

import jax
import jax.numpy as jnp
from jax import lax
from jax.experimental import pallas as pl
from jax.experimental.pallas import tpu as pltpu
from jax.sharding import PartitionSpec as P

MESH = pl.DeviceIdType.MESH
F32 = jnp.float32
OWN = 16
HALO = 8
SPAN = 32
STEPS = 4
NZ = 16


def roll(value, shift, axis=1):
    size = value.shape[axis]
    shift = shift % size
    return value if shift == 0 else pltpu.roll(value, shift, axis)


def kernel(
    n, gx, gy, depth,
    v_in, s_in, b_in, out,
    v_rows, s_rows, b_rows, blocks, old, src, fresh, halo,
    free, res, pad, last_box, start, e_send, e_recv, t_send, t_recv, e_old, coef, rows2, imp, raw, raw2, resp2, wide, wide2, resp, out_rows,
    field_send, field_recv, b_recv, b_send, e_ssem, e_rsem, t_ssem, t_rsem, u_ssem, u_rsem, o_ssem, o_rsem, met,
):
    g, a, q = lax.axis_index("gz"), lax.axis_index("gx"), lax.axis_index("gy")
    par = lax.rem(a, 2)
    local = OWN * n

    def flip(p):
        return p + par * (n - 1 - 2 * p)

    p = flip(g)
    a_left, a_right = lax.rem(a + gx - 1, gx), lax.rem(a + 1, gx)
    step_up = 1 - 2 * par
    first, last = p == 0, p == n - 1
    left = (jnp.where(first, g, g - step_up), jnp.where(first, a_left, a))
    right = (jnp.where(last, g, g + step_up), jnp.where(last, a_right, a))
    places = (left, (g, a), right)

    def remote(source, target, send, recv, device):
        return pltpu.make_async_remote_copy(
            src_ref=source, dst_ref=target, send_sem=send, recv_sem=recv, device_id=device, device_id_type=MESH
        )

    def b_local(source_line, row, count, sem):
        return pltpu.make_async_copy(
            b_in.at[pl.ds(pl.multiple_of(source_line * 128, 128), count * 128)],
            b_rows.at[pl.ds(row * 128, count * 128)], sem,
        )

    b_local(OWN * p, HALO, OWN, b_recv.at[0]).start()

    @pl.when(p > 0)
    def _():
        b_local(OWN * p - HALO, 0, HALO, b_recv.at[1]).start()

    @pl.when(p < n - 1)
    def _():
        b_local(OWN * p + OWN, HALO + OWN, HALO, b_recv.at[2]).start()

    barrier = pltpu.get_barrier_semaphore()

    def greet(i, carry):
        g2, a2 = lax.rem(i, n), lax.rem(a + gx - 1 + i // n, gx)

        @pl.when(jnp.logical_or(g2 != g, a2 != a))
        def _():
            pl.semaphore_signal(barrier, inc=1, device_id=(g2, a2, q), device_id_type=MESH)

        return carry

    lax.fori_loop(0, 3 * n, greet, 0)
    beside = [(place[0], place[1], lax.rem(q + k, gy)) for place in places for k in (1, gy - 1)]
    for device in beside:
        pl.semaphore_signal(barrier, inc=1, device_id=device, device_id_type=MESH)
    pl.semaphore_wait(barrier, 3 * n - 1 + 6)
    for device in beside:
        pl.semaphore_signal(met, inc=1, device_id=device, device_id_type=MESH)

    fields = ((v_in, v_rows), (s_in, s_rows))
    planes = pl.ds(depth * g, depth)

    early = depth * g < STEPS

    def field_copies(start, f):
        source, place = fields[f]
        arrival = field_recv.at[jnp.where(early, f, 2 * f)]
        for other in range(n):
            lo, hi = max(0, OWN * other - HALO), min(local, OWN * other + OWN + HALO)
            row = lo - (OWN * other - HALO)
            target = flip(other)
            args = (source.at[:, pl.ds(lo, hi - lo), :], place.at[planes, pl.ds(row, hi - lo), :])

            @pl.when(target != g)
            def _():
                copy = remote(*args, field_send.at[f, other], arrival, (target, a, q))
                if start:
                    copy.start()
                else:
                    copy.wait_send()

            if start:
                @pl.when(target == g)
                def _():
                    pltpu.make_async_copy(*args, arrival).start()

        ends = (
            (local - HALO, 0, (flip(n - 1), a_right, q), n),
            (0, HALO + OWN, (flip(0), a_left, q), n + 1),
        )
        for line, row, device, sem in ends:
            copy = remote(
                source.at[:, pl.ds(line, HALO), :], place.at[planes, pl.ds(row, HALO), :],
                field_send.at[f, sem], arrival, device,
            )
            if start:
                copy.start()
            else:
                copy.wait_send()

    share = HALO // n

    def b_remote(start):
        for side, line, row, device in (
            (0, local - HALO, 0, (flip(n - 1), a_right, q)), (1, 0, HALO + OWN, (flip(0), a_left, q)),
        ):
            rows = lambda at: pl.ds(pl.multiple_of((at + share * g) * 128, 128), share * 128)
            copy = remote(b_in.at[rows(line)], b_rows.at[rows(row)], b_send.at[side], b_recv.at[1 + side], device)
            if start:
                copy.start()
            else:
                copy.wait_send()

    b_remote(True)
    field_copies(True, 0)

    @pl.when(early)
    def _():
        field_copies(True, 1)


    lane = lax.broadcasted_iota(jnp.int32, (SPAN, 128), 1)
    row = lax.broadcasted_iota(jnp.int32, (SPAN, 128), 0)
    group, xlane = lane // SPAN, lane % SPAN
    line = local * a + OWN * p - HALO + xlane
    inside = jnp.logical_and(line >= 0, line < local * gx)
    low_half, even = group < 2, group % 2 == 0
    group1 = group[:1]
    group8, xlane8, inside8, sub8 = group[:8], xlane[:8], inside[:8], row[:8]
    ends8 = jnp.logical_and(sub8 < 2, jnp.logical_and(xlane8 >= HALO, xlane8 < HALO + OWN))
    top8, bottom8 = jnp.logical_and(sub8 == 0, group8 == 0), jnp.logical_and(sub8 == 7, group8 == 3)

    zero8 = jnp.zeros((8, 128), F32)

    def y_sum(cells):
        up = jnp.where(group1 == 0, 0.0, roll(cells[SPAN - 1 :], SPAN))
        down = jnp.where(group1 == 3, 0.0, roll(cells[:1], -SPAN))
        return cells + jnp.where(row == 0, up, roll(cells, 1, 0)) + jnp.where(row == SPAN - 1, down, roll(cells, -1, 0))

    def box(cells):
        return y_sum(cells + roll(cells, 1) + roll(cells, -1))

    def product(residual, slot):
        res[slot] = residual
        acc = blocks[0] * res[slot, :1, :]
        for j in range(1, SPAN):
            acc = acc + blocks[j] * res[slot, j : j + 1, :]
        rows = [acc[SPAN * i : SPAN * (i + 1)] for i in range(4)]
        parts = []
        for k in range(4):
            part = rows[-k % 4]
            for i in range(1, 4):
                part = jnp.where(group == i, rows[(i - k) % 4], part)
            parts.append(part)
        return parts

    def summed(parts, shifts, at=slice(None)):
        total = None
        for k in range(4):
            for shift in shifts:
                term = roll(parts[k][at], shift - SPAN * k)
                total = term if total is None else total + term
        return total

    def plain(parts, at=slice(None)):
        return summed(parts, (0,), at)

    def apply(residual):
        return plain(product(residual, 7))

    def boxed(parts, slot):
        up = summed(parts, (SPAN - 1, SPAN, SPAN + 1), slice(SPAN - 8, SPAN))
        down = summed(parts, (-SPAN - 1, -SPAN, -SPAN + 1), slice(0, 8))
        pad[slot, :8, :] = jnp.where(group8 == 0, 0.0, up)
        pad[slot, 8 : SPAN + 8, :] = summed(parts, (-1, 0, 1))
        pad[slot, SPAN + 8 :, :] = jnp.where(group8 == 3, 0.0, down)
        return pad[slot, 7 : SPAN + 7, :] + pad[slot, 8 : SPAN + 8, :] + pad[slot, 9 : SPAN + 9, :]

    def turn(x, carry):
        rows = pl.ds(pl.multiple_of(x * 128, 128), 128)
        b_rows[rows, :] = b_rows[rows, :].T
        return carry

    b_local(0, HALO, OWN, b_recv.at[0]).wait()
    lax.fori_loop(HALO, HALO + OWN, turn, 0, unroll=4)
    b_local(0, 0, HALO, b_recv.at[1]).wait()
    lax.fori_loop(0, HALO, turn, 0, unroll=4)
    b_local(0, HALO + OWN, HALO, b_recv.at[2]).wait()
    lax.fori_loop(HALO + OWN, SPAN, turn, 0, unroll=4)

    def gather(j, carry):
        parts = [b_rows[pl.ds(SPAN * jg + j, SPAN, stride=128), :] for jg in range(4)]
        blocks[j] = jnp.where(inside[:1], jnp.concatenate(parts, axis=0).T, 0.0)
        return carry

    lax.fori_loop(0, SPAN, gather, 0, unroll=4)

    columns, cells = [], []
    for slot, at in ((0, 0), (SPAN - 1, 3)):
        column = jnp.zeros((SPAN, 128), F32)
        for i in range(4):
            column = jnp.where(group == i, roll(blocks[slot, SPAN * i : SPAN * (i + 1), :], SPAN * (i - at)), column)
        columns.append(jnp.where(inside, column, 0.0))
        cells.append(y_sum(columns[-1]))
    resp[6], resp[7] = columns
    for j in range(SPAN):
        rows2[0, j : j + 1, :] = blocks[j, :1, :]
        rows2[1, j : j + 1, :] = blocks[j, 127:, :]
    for e in range(2):
        for d in range(3):
            imp[3 * e + d] = roll(cells[e], -(d - 1))

    for i in range(6):
        value = plain(product(imp[i], i))
        raw[i] = value
        resp[i] = y_sum(value)

    def spread(value):
        return (value + roll(value, 32)) + (roll(value, 64) + roll(value, 96))

    def pair(values):
        return jnp.where(sub8 == 0, spread(values[0]), spread(values[1]))

    def dots(value):
        return pair([jnp.sum(rows2[e] * value, axis=0, keepdims=True) for e in range(2)])

    def packed(pairs):
        tile = None
        for m in range(0, len(pairs), 4):
            part = jnp.zeros((8, 128), F32)
            for k, value in enumerate(pairs[m : m + 4]):
                part = jnp.where(group8 == k, value, part)
            part = roll(jnp.where(ends8, part, 0.0), m // 2, 0)
            tile = part if tile is None else tile + part
        return tile

    def edge_pair(top, bottom, k):
        return jnp.where(sub8 == 0, roll(top, SPAN * k), roll(roll(bottom, 2, 0), SPAN * (k - 3)))

    first_pairs = [
        pair([jnp.where(group1 == 0, rows2[e, :1, :], 0.0) for e in range(2)]),
        pair([jnp.where(group1 == 3, rows2[e, SPAN - 1 :, :], 0.0) for e in range(2)]),
    ]
    coef[0] = packed([zero8] * 4 + first_pairs)
    later_pairs = [dots(roll(cells[f], -d)) for f in range(2) for d in range(-1, 2)]
    for f in range(2):
        for d in range(-2, 3):
            total = None
            for near in range(-1, 2):
                far = d - near
                if abs(far) <= 1:
                    term = roll(resp[3 * f + far + 1], -near)
                    total = term if total is None else total + term
            wide[5 * f + d + 2] = total
            later_pairs.append(dots(total))
    t_send[0] = packed(later_pairs)

    @pl.when(jnp.logical_not(early))
    def _():
        field_copies(True, 1)

    def settle(place, rows_ref, parts, sem):
        ref = rows_ref.at[4 * parts.start : 4 * parts.stop]
        pltpu.make_async_copy(ref, ref, sem).wait()
        for w in parts:
            turned = rows_ref[4 * w : 4 * w + 4].reshape(128, 128).T
            for k in range(4):
                tile = jnp.zeros((SPAN, 128), F32)
                for i in range(4):
                    tile = jnp.where(group == i, roll(turned[SPAN * i : SPAN * (i + 1)], SPAN * (i - k)), tile)
                place[4 * w + k] = jnp.where(inside, tile, 0.0)

    settle(old, v_rows, range(NZ // 4), field_recv.at[0])
    settle(src, s_rows, range(1), field_recv.at[1])
    zero_tile = jnp.zeros((SPAN, 128), F32)
    old[NZ] = zero_tile
    old[2 * NZ + 1] = zero_tile
    e_old[NZ] = jnp.zeros((8, 128), F32)
    e_old[2 * NZ + 1] = jnp.zeros((8, 128), F32)
    t_send[1] = packed([edge_pair(old[z, :8, :], old[z, SPAN - 8 :, :], z % 4) for z in range(NZ)])

    def edge_copies(source, target, send, recv, start):
        for k in sorted(range(gy), key=lambda k: -min(k, gy - k)):
            for x in (0, 2, 1):
                place = places[x]
                if x == 1 and k == 0:
                    if start:
                        pltpu.make_async_copy(source, target.at[1, q], recv).start()
                    continue
                copy = remote(
                    source, target.at[2 - x, q], send.at[3 * k + x], recv, (place[0], place[1], lax.rem(q + k, gy))
                )
                if start:
                    copy.start()
                else:
                    copy.wait_send()

    pl.semaphore_wait(met, 6)
    edge_copies(t_send, t_recv, t_ssem, t_rsem, True)

    def unpacked(ref, at=None):
        low_side, high_side = xlane8 < HALO, xlane8 >= HALO + OWN
        whole = []
        for k in range(4):
            tile = jnp.zeros((8, 128), F32)
            for b in range(gy):
                sides = [ref[x, b] if at is None else ref[x, b, at] for x in range(3)]
                sides = [roll(sides[x], SPAN * (b - k) + OWN * (x - 1)) for x in range(3)]
                side = jnp.where(low_side, sides[0], jnp.where(high_side, sides[2], sides[1]))
                tile = jnp.where(group8 == b, side, tile)
            whole.append(jnp.where(inside8, tile, 0.0))
        return lambda i: roll(whole[i % 4], -2 * (i // 4), 0)

    def halo_copy(window, side, start):
        device = places[2 * side]
        device = (device[0], device[1], q)
        at = STEPS * window

        @pl.when(window < 4)
        def _():
            copy = remote(
                fresh.at[pl.ds(at, STEPS)], halo.at[window, 1 - side],
                u_ssem.at[window, side], u_rsem.at[window, 1 - side], device,
            )
            if start:
                copy.start()
            else:
                copy.wait_send()

        @pl.when(window >= 4)
        def _():
            copy = remote(
                fresh.at[at + STEPS - 1], halo.at[window, 1 - side, STEPS - 1],
                u_ssem.at[window, side], u_rsem.at[window, 1 - side], device,
            )
            if start:
                copy.start()
            else:
                copy.wait_send()

    def halo_wait(window):
        @pl.when(window < 4)
        def _():
            for side in range(2):
                ref = halo.at[window, side]
                pltpu.make_async_copy(ref, ref, u_rsem.at[window, side]).wait()

        @pl.when(window >= 4)
        def _():
            for side in range(2):
                ref = halo.at[window, side, STEPS - 1]
                pltpu.make_async_copy(ref, ref, u_rsem.at[window, side]).wait()

    def out_copy(z, start):
        owner = z // depth
        source = out_rows.at[z]
        target = out.at[lax.rem(z, depth), pl.ds(pl.multiple_of(OWN * p, OWN), OWN), :]

        @pl.when(owner != g)
        def _():
            copy = remote(source, target, o_ssem.at[z], o_rsem, (owner, a, q))
            if start:
                copy.start()
            else:
                copy.wait_send()

        if start:
            @pl.when(owner == g)
            def _():
                pltpu.make_async_copy(source, target, o_rsem).start()

    def deliver(window):
        at = STEPS * window
        tiles = [fresh[at + k] for k in range(4)]
        parts = []
        for i in range(4):
            part = roll(tiles[0], -SPAN * i)
            for k in range(1, 4):
                part = jnp.where(group == k, roll(tiles[k], SPAN * (k - i)), part)
            parts.append(part)
        lines = jnp.concatenate(parts, axis=0).T
        for k in range(4):
            z = 2 * NZ - 1 - at - k
            out_rows[z] = lines[SPAN * k + HALO : SPAN * k + HALO + OWN]
            out_copy(z, True)

    def window_step(window, carry):
        backward = window // 4
        m0 = STEPS * (window - 4 * backward)
        at = (NZ + 1) * backward + m0
        t0 = STEPS * window
        opening = m0 == 0

        def source_plane(m):
            return src[m + backward * (NZ - 1 - 2 * m)]

        guesses = []
        around = None
        for t in range(STEPS - 1):
            cell = old[at + t]
            near = cell + old[at + t + 1]
            residual = source_plane(m0 + t) - 27.0 * cell + box(near if t == 0 else near + old[at + t - 1])
            residual = residual + (jnp.where(opening, 0.0, last_box[...]) if t == 0 else boxed(around, t))
            ends = (slice(0, 8), slice(SPAN - 8, SPAN))
            if t < STEPS - 2:
                around = product(residual, t)
                change = jnp.where(
                    sub8 == 0, summed(around, (SPAN * t,), ends[0]),
                    roll(summed(around, (SPAN * (t - 3),), ends[1]), 2, 0),
                )
                guesses.append(edge_pair(*(cell[end] for end in ends), t) + change)
            else:
                guesses.append(edge_pair(*(cell[end] for end in ends), t) + dots(residual))
        done = []
        for k in range(STEPS):
            tile = fresh.at[jnp.maximum(t0 - STEPS + k, 0)]
            done.append(edge_pair(tile[:8, :], tile[SPAN - 8 :, :], k))
        first = packed(guesses + [jnp.where(window == 0, 0.0, done[3])])
        rest = packed([zero8] * 4 + [done[k] for k in range(3)])
        e_send[window] = first + jnp.where(window == 0, coef[0], rest)
        edge_copies(e_send.at[window, :4], e_recv.at[window, :, :, :4], e_ssem.at[window], e_rsem.at[window], True)

        @pl.when(window == 0)
        def _():
            settle(src, s_rows, range(1, NZ // 4), field_recv.at[2])

            for i in range(10):
                value = plain(product(wide[i], i % 8))
                raw2[i] = value
                resp2[i] = y_sum(value)

            for f in range(2):
                for d in range(-3, 4):
                    total = None
                    for near in range(-1, 2):
                        far = d - near
                        if abs(far) <= 2:
                            term = roll(resp2[5 * f + far + 2], -near)
                            total = term if total is None else total + term
                    wide2[7 * f + d + 3] = total

        @pl.when(window > 4)
        def _():
            deliver(window - 1)

        @pl.when(window > 0)
        def _():
            halo_wait(window - 1)

        def merged(t):
            mid = fresh[jnp.maximum(t0 - STEPS + t, 0)]
            w = jnp.maximum(window - 1, 0)
            tile = jnp.where(
                xlane < HALO, roll(halo[w, 0, t], -OWN),
                jnp.where(xlane >= HALO + OWN, roll(halo[w, 1, t], OWN), mid),
            )
            return jnp.where(inside, tile, 0.0)

        @pl.when(jnp.logical_and(window > 0, window <= 4))
        def _():
            for t in range(STEPS):
                old[2 * NZ - jnp.maximum(t0 - STEPS + t, 0)] = merged(t)

        @pl.when(opening)
        def _():
            start[...] = zero_tile

        @pl.when(jnp.logical_not(opening))
        def _():
            start[...] = merged(STEPS - 1)

        for t in range(STEPS):
            cell = old[at + t]
            before = start[...] if t == 0 else free[t - 1]
            value = source_plane(m0 + t) - 27.0 * cell + box(cell + old[at + t + 1] + before)
            free[t] = cell + plain(product(value, 2 + t)) if t < STEPS - 1 else value

        @pl.when(window == 0)
        def _():
            pltpu.make_async_copy(t_recv, t_recv, t_rsem).wait()
            item = unpacked(t_recv, 0)
            for r in range(16):
                coef[2 + r] = item(r)
            item = unpacked(t_recv, 1)
            for r in range(NZ):
                e_old[r] = item(r)

        arrived, landed = e_recv.at[window], e_recv.at[window, :, :, :4]
        pltpu.make_async_copy(landed, landed, e_rsem.at[window]).wait()
        item = unpacked(arrived)

        for r in range(2):
            coef[r] = jnp.where(window == 0, item(4 + r), coef[r])
        kept = jnp.logical_and(window > 0, window <= 4)
        for t in range(STEPS):
            place = jnp.where(kept, 2 * NZ - (t0 - STEPS + t), 2 * NZ + 2)
            e_old[place] = item(3 if t == 3 else 4 + t)

        before = jnp.where(opening, 0.0, item(3))
        gives, gains, planes_now = [], [], []
        around = None
        for t in range(STEPS):
            total = before + (e_old[at + t] + e_old[at + t + 1])
            reach = max(0, STEPS - 2 - t)
            low, high = jnp.broadcast_to(total[1:2], (8, 128)), jnp.broadcast_to(total[:1], (8, 128))
            from_low = {c: roll(low, SPAN - c) for c in range(-reach - 1, reach + 2)}
            from_high = {c: roll(high, -SPAN - c) for c in range(-reach - 1, reach + 2)}
            give = {}
            for d in range(-reach, reach + 1):
                give[0, d] = jnp.where(group8 > 0, from_low[d - 1] + from_low[d] + from_low[d + 1], 0.0)
                give[1, d] = jnp.where(group8 < gy - 1, from_high[d - 1] + from_high[d] + from_high[d + 1], 0.0)
            gives.append(give)
            if t < STEPS - 1:
                wing = STEPS - 1 - t
                gain = {}
                for f, (edge, there) in enumerate(((low, q - 1), (high, q + 1))):
                    mine = spread(jnp.where(group8 == there, edge, 0.0))
                    moved = {c: roll(mine, -c) for c in range(-wing - 1, wing + 2)}
                    for d in range(-wing, wing + 1):
                        gain[f, d] = jnp.concatenate([moved[d - 1] + moved[d] + moved[d + 1]] * 4, axis=0)
                gains.append(gain)
                now = free[t]
                for s in range(t + 1):
                    lag = t - s
                    for f in range(2):
                        for d in range(-lag, lag + 1):
                            if lag == 0:
                                tile = resp[6 + f]
                            else:
                                tile = raw[3 * f + d + 1] if lag == 1 else raw2[5 * f + d + 2]
                            now = now + tile * gains[s][f, d]
            else:
                mine = (
                    jnp.where(top8, pltpu.roll(give[0, 0], lax.rem(128 - SPAN * q, 128), 1), 0.0),
                    jnp.where(bottom8, pltpu.roll(give[1, 0], SPAN * (3 - q), 1), 0.0),
                )
                residual = free[t]
                for s, (tiles, width) in enumerate(((wide2, 3), (wide, 2), (imp, 1))):
                    for f in range(2):
                        for d in range(-width, width + 1):
                            residual = residual + tiles[(2 * width + 1) * f + d + width] * gains[s][f, d]
                residual = jnp.concatenate(
                    [residual[:8] + mine[0], residual[8 : SPAN - 8], residual[SPAN - 8 :] + mine[1]], axis=0
                )
                around = product(residual, 5)
                now = old[at + t] + plain(around)
            fresh[t0 + t] = now
            planes_now.append(now)
            if t < STEPS - 1:
                value = item(t)
                for s in range(t + 1):
                    lag = t - s
                    for f in range(2):
                        for d in range(-lag, lag + 1):
                            r = (0, 2, 8)[lag] + f * (2 * lag + 1) + d + lag
                            value = value + coef[r] * gives[s][f, d]
                before = jnp.where(inside8, value, 0.0)

        last_box[...] = box(old[at + STEPS - 1]) + boxed(around, 4)

        for t in range(STEPS):
            old[jnp.where(backward == 0, 2 * NZ - (t0 + t), 2 * NZ + 2)] = planes_now[t]

        @pl.when(window < 7)
        def _():
            halo_copy(window, 0, True)
            halo_copy(window, 1, True)

        return carry

    lax.fori_loop(0, 8, window_step, 0)
    deliver(7)

    field_copies(False, 0)
    field_copies(False, 1)
    b_remote(False)
    edge_copies(t_send, t_recv, t_ssem, t_rsem, False)

    def drain(window, carry):
        edge_copies(e_send.at[window, :4], e_recv.at[window, :, :, :4], e_ssem.at[window], e_rsem.at[window], False)

        @pl.when(window < 7)
        def _():
            halo_copy(window, 0, False)
            halo_copy(window, 1, False)

        return carry

    lax.fori_loop(0, 8, drain, 0)

    def drain_out(z, carry):
        out_copy(z, False)
        return carry

    lax.fori_loop(0, NZ, drain_out, 0)
    pltpu.make_async_copy(out, out, o_rsem).wait()


def solution(mesh):
    n, gx, gy = mesh.shape["gz"], mesh.shape["gx"], mesh.shape["gy"]

    def body(initial_field, source_term, block_inverse):
        depth, local, width = initial_field.shape
        vmem = lambda *shape: pltpu.VMEM(shape, F32)
        dma = pltpu.SemaphoreType.DMA
        return pl.pallas_call(
            functools.partial(kernel, n, gx, gy, depth),
            out_shape=jax.ShapeDtypeStruct(initial_field.shape, F32),
            in_specs=[pl.BlockSpec(memory_space=pltpu.HBM)] * 3,
            out_specs=pl.BlockSpec(memory_space=pltpu.VMEM),
            scratch_shapes=[
                vmem(NZ, SPAN, 128), vmem(NZ, SPAN, 128), vmem(SPAN * 128, 128), vmem(SPAN, 128, 128),
                vmem(2 * NZ + 3, SPAN, 128), vmem(NZ, SPAN, 128), vmem(2 * NZ, SPAN, 128),
                vmem(8, 2, STEPS, SPAN, 128),
                vmem(STEPS, SPAN, 128), vmem(8, SPAN, 128), vmem(8, SPAN + 16, 128), vmem(SPAN, 128), vmem(SPAN, 128),
                vmem(8, 8, 128), vmem(8, 3, gy, 8, 128), vmem(2, 8, 128), vmem(3, gy, 2, 8, 128),
                vmem(2 * NZ + 3, 8, 128), vmem(18, 8, 128), vmem(2, SPAN, 128),
                vmem(6, SPAN, 128), vmem(6, SPAN, 128), vmem(10, SPAN, 128), vmem(10, SPAN, 128), vmem(10, SPAN, 128),
                vmem(14, SPAN, 128), vmem(8, SPAN, 128), vmem(NZ, OWN, 128),
                dma((2, n + 2)), dma((3,)), dma((3,)), dma((2,)),
                dma((8, 3 * gy)), dma((8,)), dma((3 * gy,)), dma,
                dma((8, 2)), dma((8, 2)), dma((NZ,)), dma, pltpu.SemaphoreType.REGULAR,
            ],
            compiler_params=pltpu.CompilerParams(
                collective_id=0, has_side_effects=True, vmem_limit_bytes=60 * 1024 * 1024
            ),
        )(initial_field, source_term, block_inverse.reshape(local * width, width))

    return jax.shard_map(
        body, mesh=mesh,
        in_specs=(P("gz", "gx", "gy"), P("gz", "gx", "gy"), P("gx", "gy", None)),
        out_specs=P("gz", "gx", "gy"), check_vma=False,
    )
```
